32 devices in a mesh: dp: 16 (over z, y, x), tensor: 2 (over core).
Axes of the slice: x: 2, y: 2, z: 4, core: 2. Of those that a mesh axis runs over, the one named last changes fastest.
Arguments:
- inputs: float32 [32, 197, 768], P('dp'), may hold values from -6 to 6
- image_count: int32 [16], P('dp'), may hold values from 1 to 2, as said below
- routes: int32 [2, 32, 197, 2], P(None, 'dp'), may hold values from 0 to 3, all different within a row; in each aligned block of 394 rows (0 to 393, 394 to 787, ..., all dimensions but the last counted through in order) at most 246 rows name the same one
- gates: float32 [2, 32, 197, 2], P(None, 'dp'), may hold values from 0.3 to 1
- norm_gain: bfloat16 [2, 2, 768], P(None, None, 'dp'), may hold values from 0.5 to 1.5
- norm_shift: bfloat16 [2, 2, 768], P(None, None, 'dp'), may hold values from -0.59765625 to 0.59765625
- attend_weight: bfloat16 [2, 3, 768, 768], P(None, None, 'dp', 'tensor'), may hold values from -0.21875 to 0.21875
- attend_bias: bfloat16 [2, 2, 768], P(None, None, ('tensor', 'dp')), may hold values from -1.1953125 to 1.1953125
- merge_weight: bfloat16 [2, 768, 768], P(None, ('tensor', 'dp')), may hold values from -0.875 to 0.875
- merge_bias: bfloat16 [2, 768], P(None, 'dp'), may hold values from -0.59765625 to 0.59765625
- up_weight: bfloat16 [2, 4, 768, 3072], P(None, None, 'dp', 'tensor'), may hold values from -0.21875 to 0.21875
- up_bias: bfloat16 [2, 4, 3072], P(None, None, ('tensor', 'dp')), may hold values from -1.1953125 to 1.1953125
- down_weight: bfloat16 [2, 4, 3072, 768], P(None, None, ('tensor', 'dp')), may hold values from -0.109375 to 0.109375
- down_bias: bfloat16 [2, 4, 768], P(None, None, 'dp'), may hold values from -0.59765625 to 0.59765625
- cotangent: float32 [32, 197, 768], P('dp'), may hold values from -6 to 6
Outputs:
- output: float32 [32, 197, 768], P('dp')
- input_grad: float32 [32, 197, 768], P('dp')
- gain_grad: float32 [2, 2, 768], P(None, None, 'dp')
- shift_grad: float32 [2, 2, 768], P(None, None, 'dp')
- attend_grad: float32 [2, 3, 768, 768], P(None, None, 'dp', 'tensor')
- attend_bias_grad: float32 [2, 2, 768], P(None, None, ('tensor', 'dp'))
- merge_grad: float32 [2, 768, 768], P(None, ('tensor', 'dp'))
- merge_bias_grad: float32 [2, 768], P(None, 'dp')
- up_grad: float32 [2, 4, 768, 3072], P(None, None, 'dp', 'tensor')
- up_bias_grad: float32 [2, 4, 3072], P(None, None, ('tensor', 'dp'))
- down_grad: float32 [2, 4, 3072, 768], P(None, None, ('tensor', 'dp'))
- down_bias_grad: float32 [2, 4, 768], P(None, None, 'dp')
The draws below stay inside these ranges and needn't reach their ends.
Inputs may be any that keep to these rules, and one draw needn't show every extreme that they name: `routes`: in each layer, no expert is named by more than 246 of the rows of one index of dp, and in some such block one expert is named by exactly 246; a row names two different experts. `image_count`: some index of dp holds 2 images in every draw; the images in use are the first of each block.
All inputs are finite; a program needn't handle non-finite values.
Results may differ from the reference program's by a relative error of at most 0.017.
Values may be sent and summed in bfloat16 or wider, within the bound.
No kernel may reach another device: no remote copies, remote signals or barrier semaphores. Data moves between devices by JAX's collectives and lax.ppermute only.
A program may use at most 320 MiB of HBM per device.

```python
import math
import jax
import jax.numpy as jnp
import numpy as np
from jax import lax

D = 768
H = 12
HD = 64
FF = 3072
E = 4
L = 2
S = 197
IMG_DEV = 2
IMAGES = 32
CAP = 246
N_DP = 16


def draw_image_count(key, part):
    key = jax.random.fold_in(key, 11)
    devices = IMAGES // IMG_DEV
    lowest = max(1, IMG_DEV // 2)
    counts = jax.random.randint(jax.random.fold_in(key, 1), (devices,), lowest, IMG_DEV + 1, dtype=jnp.int32)
    fullest = jax.random.randint(jax.random.fold_in(key, 2), (), 0, devices, dtype=jnp.int32)
    return jnp.where(jnp.arange(devices, dtype=jnp.int32) == fullest, IMG_DEV, counts).astype(jnp.int32)


def block_scale(own_key, extent, cuts, low, high):
    def one(axis_at, parts):
        heights = jax.random.uniform(jax.random.fold_in(jax.random.fold_in(own_key, 6), axis_at), (parts,), jnp.float32, low / len(cuts), high / len(cuts))
        return jnp.repeat(jnp.exp(heights), extent[axis_at] // parts).reshape((-1,) + (1,) * (len(extent) - axis_at - 1))

    level = one(*cuts[0])
    for cut in cuts[1:]:
        level = level * one(*cut)
    return level


def deal_out(stream_key, own, number, rows, amount, top, most, slope):
    ranking = jax.random.permutation(stream_key, amount)
    heavy_load, ordinary = portions_of(amount, rows * top, most, slope, True), portions_of(amount, rows * top, most, slope, False)
    places = jnp.arange(amount)

    def named(sizes, offset_by):
        used = int((sizes > 0).sum())
        fixed = max(1, used // 4)
        moved = fixed + (places - fixed + offset_by * (used - fixed)) % max(1, amount - fixed)
        return jnp.zeros((amount,), jnp.int32).at[ranking[jnp.where(places < fixed, places, moved)]].set(jnp.asarray(sizes, jnp.int32))

    sizes = jnp.where(number % 4 == 0, named(heavy_load, number // 4), named(ordinary, number - number // 4 - 1))
    mixed = jax.random.permutation(jax.random.fold_in(own, 3), amount)
    giver, receiver = mixed[0:amount // 2 * 2:2], mixed[1:amount // 2 * 2:2]
    slack = jnp.minimum(sizes[giver] - 1, most - sizes[receiver]) // 2
    slack = jnp.where((giver == ranking[0]) | (receiver == ranking[0]) | (sizes[receiver] == 0), 0, jnp.maximum(slack, 0))
    moved = jax.random.randint(jax.random.fold_in(own, 4), (amount // 2,), 0, 1 << 20) % (slack + 1)
    sizes = sizes.at[giver].add(-moved).at[receiver].add(moved)
    members = jnp.searchsorted(jnp.cumsum(sizes), jnp.arange(rows * top), side="right").astype(jnp.int32)
    table = members.reshape(top, rows).T
    table = table[jax.random.permutation(jax.random.fold_in(own, 1), rows)]
    offset_by = jax.random.randint(jax.random.fold_in(own, 2), (rows, 1), 0, top)
    return jnp.take_along_axis(table, (jnp.arange(top)[None, :] + offset_by) % top, axis=1)


def portions_of(count, total, most, skew, full):
    portions = [(1 << 20) // math.isqrt(grade ** skew) + 1 for grade in range(1, count + 1)]
    largest = most if full else min(most, max(-(-total // count), total * portions[0] // sum(portions)))
    least = 1 if total - largest >= count - 1 else 0
    given, spare = [largest] + [least] * (count - 1), total - largest - least * (count - 1)
    while spare > 0:
        movable = [i for i in range(1, count) if given[i] < largest] or [i for i in range(1, count) if given[i] < most]
        mass, remaining = sum([portions[i] for i in movable]), spare
        for i in movable:
            addition = min(most - given[i], max(1, remaining * portions[i] // mass), spare)
            given[i] = given[i] + addition
            spare = spare - addition
    return np.array(given)


def bell_draw(stream_key, shape, deviation, bound, cuts=(), kind=jnp.bfloat16):
    drawn = deviation * jax.random.normal(stream_key, shape, jnp.float32)
    if cuts:
        drawn = drawn * block_scale(stream_key, shape, cuts, -0.22, 0.18)
    return jnp.clip(drawn, -bound, bound).astype(kind)


def setup_inputs(seed: int = 0) -> dict:
    seeds = jax.random.split(jax.random.key(seed), 16)
    inputs = bell_draw(seeds[0], (IMAGES, S, D), 1.0, 6.0, ((0, 16),), jnp.float32)
    image_count = draw_image_count(jax.random.fold_in(seeds[15], 71), 0)
    routes_keys = jax.random.split(jax.random.fold_in(seeds[2], 1), L * IMAGES * S // (IMG_DEV * S))
    routes_turns = jax.random.permutation(jax.random.fold_in(seeds[2], 3), L * IMAGES * S // (IMG_DEV * S))
    routes = jax.vmap(lambda own, number: deal_out(jax.random.fold_in(seeds[2], 2), own, number, IMG_DEV * S, E, 2, CAP, 1))(routes_keys, routes_turns).reshape((L, IMAGES, S, 2))
    gates = jnp.clip(jnp.exp(math.log(1.0) - 1.2039728 * jax.random.uniform(seeds[3], (L, IMAGES, S, 2), jnp.float32) ** block_scale(seeds[3], (L, IMAGES, S, 2), ((1, 16),), -0.2, 0.2)), 0.3, 1.0)
    norm_gain = jnp.clip(1.0 + 0.1 * jax.random.normal(seeds[4], (L, 2, D), jnp.float32), 0.5, 1.5).astype(jnp.bfloat16)
    norm_shift = bell_draw(seeds[5], (L, 2, D), 0.1, 0.59765625, ((2, 16),))
    attend_weight = bell_draw(seeds[6], (L, 3, D, D), D ** -0.5, 0.21875, ((2, 16), (3, 2)))
    attend_bias = bell_draw(seeds[7], (L, 2, D), 0.2, 1.1953125, ((2, 32),))
    merge_weight = bell_draw(seeds[8], (L, D, D), (D // 16) ** -0.5, 0.875, ((1, 32),))
    merge_bias = bell_draw(seeds[9], (L, D), 0.1, 0.59765625, ((1, 16),))
    up_weight = bell_draw(seeds[10], (L, E, D, FF), D ** -0.5, 0.21875, ((2, 16), (3, 2)))
    up_bias = bell_draw(seeds[11], (L, E, FF), 0.2, 1.1953125, ((2, 32),))
    down_weight = bell_draw(seeds[12], (L, E, FF, D), FF ** -0.5, 0.109375, ((2, 32),))
    down_bias = bell_draw(seeds[13], (L, E, D), 0.1, 0.59765625, ((2, 16),))
    cotangent = bell_draw(seeds[14], (IMAGES, S, D), 1.0, 6.0, ((0, 16),), jnp.float32)
    return {"inputs": inputs, "image_count": image_count, "routes": routes, "gates": gates, "norm_gain": norm_gain, "norm_shift": norm_shift, "attend_weight": attend_weight, "attend_bias": attend_bias, "merge_weight": merge_weight, "merge_bias": merge_bias, "up_weight": up_weight, "up_bias": up_bias, "down_weight": down_weight, "down_bias": down_bias, "cotangent": cotangent}


@jax.custom_vjp
def low(v):
    return lax.optimization_barrier(v.astype(jnp.bfloat16)).astype(jnp.float32)

@jax.custom_vjp
def low_back(v):
    return v

def low_keep(v):
    return (low(v), None)

def low_pass(kept, grad):
    return (grad,)

def back_keep(v):
    return (v, None)

def back_low(kept, grad):
    return (low(grad),)
low.defvjp(low_keep, low_pass)
low_back.defvjp(back_keep, back_low)

def product(left, right):
    return jnp.dot(left, right, precision=lax.Precision.HIGHEST, preferred_element_type=jnp.float32)

def layer_norm(stream, gain, shift):
    center = stream - lax.optimization_barrier(jnp.mean(stream, axis=-1, keepdims=True))
    inverse = lax.rsqrt(lax.optimization_barrier(jnp.mean(center * center, axis=-1, keepdims=True)) + 1e-06)
    return center * inverse * gain + shift

def slot_targets(route, valid, experts, capacity):
    chosen = (route[:, :, None] == jnp.arange(experts, dtype=jnp.int32)).astype(jnp.int32)
    chosen = chosen * valid.astype(jnp.int32)[:, None, None]
    flat = chosen.reshape(-1, experts)
    ranks = (jnp.cumsum(flat, axis=0) - 1).astype(jnp.int32)
    slot = lax.optimization_barrier(jnp.sum(ranks * flat, axis=1)).astype(jnp.int32).reshape(route.shape)
    target = (route * capacity + slot).astype(jnp.int32)
    return jnp.where(valid[:, None], target, experts * capacity).astype(jnp.int32)

def one_layer(stream, weights, route, gate, valid):
    norm_gain, norm_shift, attend_weight, attend_bias, merge_weight, merge_bias, up_weight, up_bias, down_weight, down_bias = weights
    shape_heads = (IMG_DEV, S, H, HD)
    highest = lax.Precision.HIGHEST
    normed = low(layer_norm(stream, norm_gain[0], norm_shift[0]))
    query = low_back(low(product(normed, attend_weight[0]) + attend_bias[0]))
    keys = low_back(low(product(normed, attend_weight[1])))
    values = low_back(low(product(normed, attend_weight[2]) + attend_bias[1]))
    scores = jnp.einsum('ishd,ithd->ihst', query.reshape(shape_heads), keys.reshape(shape_heads), precision=highest)
    scores = low_back(scores * HD ** (-0.5))
    probs = low(jax.nn.softmax(scores, axis=-1))
    attended = jnp.einsum('ihst,ithd->ishd', probs, values.reshape(shape_heads), precision=highest)
    attended = low_back(low(attended.reshape(IMG_DEV * S, D)))
    middle = stream + low_back(product(attended, merge_weight) + merge_bias)
    normed_two = low(layer_norm(middle, norm_gain[1], norm_shift[1]))
    target = slot_targets(route, valid, E, CAP)
    buffer = jnp.zeros((E * CAP, D), jnp.float32).at[target.reshape(-1)].add(jnp.repeat(normed_two, 2, axis=0), mode='drop')
    hidden = jnp.einsum('ecd,edf->ecf', buffer.reshape(E, CAP, D), up_weight, precision=highest)
    hidden = low_back(hidden + up_bias[:, None, :])
    active = low(jax.nn.gelu(hidden))
    result = jnp.einsum('ecf,efd->ecd', active, down_weight, precision=highest)
    result = low_back(result + down_bias[:, None, :]).reshape(E * CAP, D)
    picked = result.at[target].get(mode='fill', fill_value=0.0)
    return middle + lax.optimization_barrier(jnp.sum(gate[:, :, None] * picked, axis=1))

def device_block(weights, block, route_block, gate_block, count):
    valid = jnp.repeat(jnp.arange(IMG_DEV, dtype=jnp.int32) < count, S)
    stream = block.reshape(IMG_DEV * S, D)
    for layer in range(L):
        layer_weights = tuple((piece[layer] for piece in weights))
        stream = one_layer(stream, layer_weights, route_block[layer], gate_block[layer], valid)
    return (stream * valid.astype(jnp.float32)[:, None]).reshape(IMG_DEV, S, D)

def forward(inputs, weights, routes, gates, image_count):
    blocks = inputs.reshape(N_DP, IMG_DEV, S, D)
    route_blocks = jnp.swapaxes(routes.reshape(L, N_DP, IMG_DEV * S, 2), 0, 1)
    gate_blocks = jnp.swapaxes(gates.reshape(L, N_DP, IMG_DEV * S, 2), 0, 1)
    stepper = jax.checkpoint(device_block)

    def run_block(item):
        return stepper(weights, item[0], item[1], item[2], item[3])
    outputs = lax.map(run_block, (blocks, route_blocks, gate_blocks, image_count))
    return outputs.reshape(inputs.shape)

def reference(inputs, image_count, routes, gates, norm_gain, norm_shift, attend_weight, attend_bias, merge_weight, merge_bias, up_weight, up_bias, down_weight, down_bias, cotangent):
    weights = tuple((piece.astype(jnp.float32) for piece in (norm_gain, norm_shift, attend_weight, attend_bias, merge_weight, merge_bias, up_weight, up_bias, down_weight, down_bias)))

    def whole(stream, params):
        return forward(stream, params, routes, gates, image_count)
    output, pullback = jax.vjp(whole, inputs, weights)
    input_grad, grads = pullback(cotangent)
    return (output, input_grad, grads[0], grads[1], grads[2], grads[3], grads[4], grads[5], grads[6], grads[7], grads[8], grads[9])
```

```python
import functools

import jax
import jax.numpy as jnp
from jax import lax
from jax.sharding import PartitionSpec as P

HD = 64
E = 4
SLOTS = 256
FAR = (0, 1, 4, 5)
LOW = jnp.bfloat16
F32 = jnp.float32


def dot(left, right):
    return jnp.dot(left, right, preferred_element_type=F32)


def dot_nt(left, right):
    return lax.dot_general(left, right, (((1,), (1,)), ((), ())), preferred_element_type=F32)


def dot_tn(left, right):
    return lax.dot_general(left, right, (((0,), (0,)), ((), ())), preferred_element_type=F32)


def swap(value, bit, count):
    return lax.ppermute(value, "dp", [(i, i ^ bit) for i in range(count)])


def cross(value):
    return lax.ppermute(value, "tensor", [(0, 1), (1, 0)])


def doubled(offsets, bits):
    for bit in bits:
        offsets = offsets + [o ^ bit for o in offsets]
    return offsets


def spread(value, bits, count):
    for bit in bits:
        value = jnp.concatenate([value, swap(value, bit, count)], axis=0)
    return value


def ordered(value, offsets, me):
    where = jnp.asarray([offsets.index(i) for i in range(len(offsets))], jnp.int32)
    index = where[jnp.arange(len(offsets), dtype=jnp.int32) ^ me]
    return jnp.take(value, index, axis=0, mode="clip")


def relative(value, offsets, me):
    return jnp.take(value, jnp.asarray(offsets, jnp.int32) ^ me, axis=0, mode="clip")


def halved(value, bits, count):
    for bit in reversed(bits):
        half = value.shape[0] // 2
        got = swap(value[half:].astype(LOW), bit, count)
        value = value[:half].astype(F32) + got.astype(F32)
    return value


def norm_forward(stream, gain, shift):
    center = stream - jnp.mean(stream, axis=-1, keepdims=True)
    inverse = lax.rsqrt(jnp.mean(center * center, axis=-1, keepdims=True) + 1e-06)
    unit = center * inverse
    return (unit * gain + shift, unit, inverse)


def norm_backward(grad, unit, inverse, gain):
    scaled = grad * gain
    inner = (
        scaled
        - jnp.mean(scaled, axis=-1, keepdims=True)
        - unit * jnp.mean(scaled * unit, axis=-1, keepdims=True)
    )
    return (inverse * inner, jnp.sum(grad * unit, axis=0), jnp.sum(grad, axis=0))


def slot_targets(route, valid):
    chosen = (route[:, :, None] == jnp.arange(E, dtype=jnp.int32)).astype(jnp.int32)
    chosen = chosen * valid.astype(jnp.int32)[:, None, None]
    flat = chosen.reshape(-1, E)
    ranks = jnp.cumsum(flat, axis=0) - 1
    slot = jnp.sum(ranks * flat, axis=1).reshape(route.shape)
    target = route * SLOTS + slot
    return jnp.where(valid[:, None], target, -1)


class Place:
    def __init__(self, count):
        self.count = count
        self.me = lax.axis_index("dp").astype(jnp.int32)
        self.core = lax.axis_index("tensor").astype(jnp.int32)
        self.expert = ((self.me >> 2) & 1) * 2 + (self.me & 1)
        powers = [1 << k for k in range(count.bit_length() - 1)]
        self.group_bits = [b for b in reversed(powers) if b not in (1, 4)]
        self.offsets = doubled(list(FAR), self.group_bits)
        high = [b for b in reversed(powers) if b not in (1, 2)]
        self.bits_p = high + [1, 2]
        self.bits_q = high + [2, 1]

    def deal(self, value):
        sent = [value[0]] + [swap(value[r], FAR[r], self.count) for r in range(1, E)]
        return jnp.stack(sent)

    def own_first(self, value):
        own = lax.dynamic_index_in_dim(value, self.core, 0, False)
        other = lax.dynamic_index_in_dim(value, 1 - self.core, 0, False)
        return own, other


def fetch_small(place, pieces):
    depth = pieces[0].shape[0]
    flat = jnp.concatenate([p.reshape(-1) for p in pieces])
    used = flat.shape[0]
    room = -(-used // 2048) * 2048
    flat = jnp.pad(flat, (0, room - used)).reshape(1, room // 128, 128)
    flat = jnp.concatenate([flat, cross(flat)], axis=0)
    bits = [1 << k for k in range(place.count.bit_length() - 1)]
    flat = spread(flat, bits, place.count)
    offsets = doubled([0, 1], [2 * b for b in bits])
    full = ordered(flat, offsets, place.me * 2 + place.core)
    full = full.reshape(place.count, 2, room)
    out, at = [], 0
    for piece in pieces:
        size = piece.size
        part = full[:, :, at : at + size].reshape((place.count, 2) + piece.shape)
        at += size
        out.append(part)
    gain, shift, merge_bias, attend_bias, up_bias, down_bias = out

    def over_dp(part):
        part = part[:, 0]
        return jnp.moveaxis(part, 0, -2).reshape(part.shape[1:-1] + (-1,))

    def over_both(part):
        part = jnp.moveaxis(part, 0, -2)
        return part.reshape(part.shape[:-2] + (-1,))

    attend_bias = over_both(attend_bias)
    up_bias = over_both(up_bias)
    return (
        over_dp(gain).astype(F32),
        over_dp(shift).astype(F32),
        over_dp(merge_bias).astype(F32),
        attend_bias.astype(F32),
        up_bias.astype(F32),
        over_dp(down_bias).astype(F32),
    )


def pack_attend(attend, merge):
    count, kinds, depth, wide = attend.shape
    first = attend[:, :2].reshape(count, 2 * depth, wide)
    sides = jnp.concatenate([merge[:, :, :wide], merge[:, :, wide:]], axis=1)
    second = jnp.concatenate([attend[:, 2], sides], axis=1)
    return first, second


def unpack_attend(first, second):
    count, double, wide = first.shape
    depth = double // 2
    some = first.reshape(count, 2, depth, wide)
    attend = jnp.concatenate([some, second[:, None, :depth]], axis=1)
    sides = second[:, depth:]
    merge = jnp.concatenate([sides[:, : depth // 2], sides[:, depth // 2 :]], axis=2)
    return attend, merge


def fetch_attend(place, attend, merge):
    first, second = pack_attend(attend[None], merge[None])
    first = ordered(
        spread(first, place.bits_p, place.count), doubled([0], place.bits_p), place.me
    )
    second = ordered(
        spread(second, place.bits_q, place.count), doubled([0], place.bits_q), place.me
    )
    first_other, second_other = cross(first), cross(second)
    sides = []
    for one, two in ((first, second), (first_other, second_other)):
        wide, rows = unpack_attend(one, two)
        wide = jnp.swapaxes(wide, 0, 1)
        wide = wide.reshape(3, -1, wide.shape[-1])
        sides.append((wide, rows.reshape(-1, rows.shape[-1])))
    (own, own_rows), (other, other_rows) = sides
    project = jnp.concatenate([own[0], other[0], own[1], other[1], own[2], other[2]], axis=1)
    return project, jnp.concatenate([own_rows, other_rows], axis=0)


def fetch_expert(place, up, down):
    def pick(stored):
        order = place.expert ^ jnp.arange(E, dtype=jnp.int32)
        return jnp.take(stored, order, axis=0, mode="clip")

    up, down = pick(up), pick(down)
    out = []
    for value in (up, down):
        value = place.deal(value)
        value = spread(value, place.group_bits, place.count)
        value = ordered(value, place.offsets, place.me)
        out.append(value.reshape(-1, value.shape[-1]))
    return out


def return_expert(place, grad, rows):
    grad = grad.astype(LOW).reshape(place.count, rows, grad.shape[-1])
    grad = relative(grad, place.offsets, place.me)
    grad = halved(grad, place.group_bits, place.count)
    grad = place.deal(grad.astype(LOW))
    order = place.expert ^ jnp.arange(E, dtype=jnp.int32)
    return jnp.take(grad, order, axis=0, mode="clip").astype(F32)


def return_attend(place, project_grad, merge_grad):
    wide = project_grad.shape[1] // 6
    project = project_grad.astype(LOW).reshape(place.count, -1, 3, 2, wide)
    merge = merge_grad.astype(LOW).reshape(2, place.count, -1, merge_grad.shape[-1])
    packs = []
    for side in range(2):
        attend = jnp.swapaxes(project[:, :, :, side], 1, 2)
        packs.append(pack_attend(attend, merge[side]))
    done = []
    for index, bits in ((0, place.bits_p), (1, place.bits_q)):
        total = packs[0][index].astype(F32) + cross(packs[1][index]).astype(F32)
        total = relative(total.astype(LOW), doubled([0], bits), place.me)
        done.append(halved(total, bits, place.count))
    attend, merge = unpack_attend(done[0], done[1])
    return attend[0], merge[0]


def heads_of(values):
    return values.reshape(values.shape[0], -1, HD)


def head_scores(query, keys):
    scores = jnp.einsum("shd,thd->hst", heads_of(query), heads_of(keys), preferred_element_type=F32)
    return scores * HD ** (-0.5)


def attention_forward(stream, gain, shift, project, bias, merge, merge_bias):
    normed, unit, inverse = norm_forward(stream, gain, shift)
    normed_low = normed.astype(LOW)
    width = stream.shape[1]
    projected = dot(normed_low, project)
    query = (projected[:, :width] + bias[0]).astype(LOW)
    keys = projected[:, width : 2 * width].astype(LOW)
    values = (projected[:, 2 * width :] + bias[1]).astype(LOW)
    scores = head_scores(query, keys)
    log_total = jax.nn.logsumexp(scores, axis=-1, keepdims=True)
    probs_low = jnp.exp(scores - log_total).astype(LOW)
    heads_out = jnp.einsum("hst,thd->shd", probs_low, heads_of(values), preferred_element_type=F32)
    attended = heads_out.reshape(stream.shape).astype(LOW)
    middle = stream + dot(attended, merge) + merge_bias
    return middle, (normed_low, unit, inverse, query, keys, values, log_total, attended)


def attention_backward(middle_grad, saved, gain, project, merge):
    normed_low, unit, inverse, query, keys, values, log_total, attended = saved
    merged_low = middle_grad.astype(LOW)
    merge_bias_grad = jnp.sum(merged_low, axis=0, dtype=F32)
    merge_grad = dot_tn(attended, merged_low)
    grad_heads = heads_of(dot_nt(merged_low, merge).astype(LOW))
    probs = jnp.exp(head_scores(query, keys) - log_total)
    probs_low = probs.astype(LOW)
    prob_grad = jnp.einsum("shd,thd->hst", grad_heads, heads_of(values), preferred_element_type=F32)
    value_grad = jnp.einsum("hst,shd->thd", probs_low, grad_heads, preferred_element_type=F32)
    score_grad = probs * (prob_grad - jnp.sum(prob_grad * probs, axis=-1, keepdims=True))
    score_grad = score_grad.astype(LOW)
    scale = HD ** (-0.5)
    query_grad = (
        jnp.einsum("hst,thd->shd", score_grad, heads_of(keys), preferred_element_type=F32) * scale
    )
    key_grad = (
        jnp.einsum("hst,shd->thd", score_grad, heads_of(query), preferred_element_type=F32) * scale
    )
    rows = middle_grad.shape[0]
    parts = [p.astype(LOW).reshape(rows, -1) for p in (query_grad, key_grad, value_grad)]
    bias_grad = jnp.stack(
        [jnp.sum(parts[0], axis=0, dtype=F32), jnp.sum(parts[2], axis=0, dtype=F32)]
    )
    stacked = jnp.concatenate(parts, axis=1)
    project_grad = dot_tn(normed_low, stacked)
    first_grad = dot_nt(stacked, project)
    norm_part, gain_grad, shift_grad = norm_backward(first_grad, unit, inverse, gain)
    return (
        middle_grad + norm_part,
        (project_grad, merge_grad),
        (gain_grad, shift_grad, bias_grad, merge_bias_grad),
    )


def routing(place, route, gate, valid):
    target = slot_targets(route, valid)
    images = target.shape[0] // 2
    target = target.reshape(2, images, 2)
    gate = gate.reshape(2, images, 2)
    target_own, target_other = place.own_first(target)
    gate_own, gate_other = place.own_first(gate)
    target = jnp.concatenate([target_own, target_other])
    gate = jnp.concatenate([gate_own, gate_other])
    expert = place.expert ^ jnp.arange(E, dtype=jnp.int32)
    half = SLOTS // 2
    lane = jnp.arange(half, dtype=jnp.int32)
    first = (expert[:, None] * SLOTS + place.core * half + lane).reshape(-1)
    second = (expert[:, None] * SLOTS + (1 - place.core) * half + lane).reshape(-1)

    def marks(slots, rows, weights):
        hit = slots[:, None, None] == rows[None]
        if weights is None:
            return jnp.sum(hit.astype(F32), axis=2).astype(LOW)
        return jnp.sum(jnp.where(hit, weights[None], 0.0), axis=2).astype(LOW)

    both = jnp.concatenate([first, second])
    return (
        marks(first, target, None),
        marks(first, target, gate),
        marks(both, target_own, None),
        marks(both, target_own, gate_own),
    )


def send_rows(place, marks, rows_low):
    rows = jnp.concatenate([rows_low, cross(rows_low)], axis=0)
    sent = dot(marks, rows).astype(LOW).reshape(E, -1, rows.shape[1])
    got = place.deal(sent).reshape(-1, rows.shape[1])
    return jnp.concatenate([got, cross(got)], axis=0)


def take_rows(place, marks, partial, bias):
    half = partial.shape[0] // 2
    total = partial[:half] + cross(partial[half:].astype(LOW)).astype(F32)
    if bias is not None:
        total = total + bias
    total = total.astype(LOW).reshape(E, -1, partial.shape[1])
    got = place.deal(total).reshape(-1, partial.shape[1])
    return dot_tn(marks, jnp.concatenate([got, cross(got)], axis=0))


def expert_forward(place, middle, marks, gain, shift, up, up_bias, down, down_bias):
    normed, unit, inverse = norm_forward(middle, gain, shift)
    buffer = send_rows(place, marks[0], normed.astype(LOW))
    hidden = dot(buffer, up) + up_bias
    active_low = jax.nn.gelu(hidden).astype(LOW)
    partial = dot(active_low, down)
    added = take_rows(place, marks[3], partial, down_bias)
    return middle + added, (unit, inverse, buffer, hidden, active_low)


def expert_backward(place, grad, saved, marks, gain, up, down):
    unit, inverse, buffer, hidden, active_low = saved
    slot_grad = send_rows(place, marks[1], grad.astype(LOW))
    down_bias_grad = jnp.sum(slot_grad, axis=0, dtype=F32)
    down_grad = dot_tn(active_low, slot_grad)
    active_grad = dot_nt(slot_grad, down)
    unused, gelu_pull = jax.vjp(jax.nn.gelu, hidden)
    hidden_grad = gelu_pull(active_grad)[0].astype(LOW)
    up_bias_grad = jnp.sum(hidden_grad, axis=0, dtype=F32)
    up_grad = dot_tn(buffer, hidden_grad)
    partial = dot_nt(hidden_grad, up)
    normed_grad = take_rows(place, marks[2], partial, None)
    norm_part, gain_grad, shift_grad = norm_backward(normed_grad, unit, inverse, gain)
    return (
        grad + norm_part,
        (up_grad, down_grad),
        (gain_grad, shift_grad, up_bias_grad, down_bias_grad),
    )


def sum_small(place, shared, split):
    sizes = [p.size for p in shared] + [p.size for p in split]
    one = jnp.concatenate([p.reshape(-1) for p in shared])
    two = jnp.concatenate([p.reshape(-1) for p in split])
    one = one + cross(one)
    flat = jnp.concatenate([one, two]).reshape(-1, 128)
    for bit in [1 << k for k in range(place.count.bit_length() - 1)]:
        flat = flat + swap(flat, bit, place.count)
    flat = flat.reshape(-1)
    out, at = [], 0
    for piece, size in zip(list(shared) + list(split), sizes):
        out.append(flat[at : at + size].reshape(piece.shape))
        at += size
    return out


def on_device(
    count,
    inputs,
    image_count,
    routes,
    gates,
    norm_gain,
    norm_shift,
    attend_weight,
    attend_bias,
    merge_weight,
    merge_bias,
    up_weight,
    up_bias,
    down_weight,
    down_bias,
    cotangent,
):
    place = Place(count)
    images, length, width = inputs.shape
    depth = routes.shape[0]
    here = jnp.arange(images, dtype=jnp.int32) < image_count[0]
    valid = jnp.repeat(here, length)
    kept = lax.dynamic_index_in_dim(here, place.core, 0, False).astype(F32)

    gain, shift, merge_shift, attend_shift, up_shift, down_shift = fetch_small(
        place, (norm_gain, norm_shift, merge_bias, attend_bias, up_bias, down_bias)
    )
    half = attend_shift.shape[-1]
    attend_shift = jnp.concatenate(place.own_first(attend_shift), axis=-1)
    up_shift = lax.dynamic_index_in_dim(up_shift, place.core, 0, False)
    up_shift = lax.dynamic_index_in_dim(up_shift, place.expert, 1, False)
    down_shift = lax.dynamic_index_in_dim(down_shift, place.expert, 1, False)

    attends = [fetch_attend(place, attend_weight[l], merge_weight[l]) for l in range(depth)]
    experts = [fetch_expert(place, up_weight[l], down_weight[l]) for l in range(depth)]
    marks = [
        routing(place, routes[l].reshape(-1, 2), gates[l].reshape(-1, 2), valid)
        for l in range(depth)
    ]

    stream = lax.dynamic_index_in_dim(inputs, place.core, 0, False)
    states = []
    for l in range(depth):
        project, merge = attends[l]
        up, down = experts[l]
        middle, attention_state = attention_forward(
            stream, gain[l, 0], shift[l, 0], project, attend_shift[l], merge, merge_shift[l]
        )
        stream, expert_state = expert_forward(
            place, middle, marks[l], gain[l, 1], shift[l, 1], up, up_shift[l], down, down_shift[l]
        )
        states.append((attention_state, expert_state))

    def whole(part):
        other = cross(part)
        pair = jnp.stack([part, other])
        return jnp.take(pair, jnp.arange(2, dtype=jnp.int32) ^ place.core, axis=0, mode="clip")

    output = whole(stream * kept)
    grad = lax.dynamic_index_in_dim(cotangent, place.core, 0, False) * kept
    up_grads, down_grads, attend_grads, merge_grads = ([None] * depth for _ in range(4))
    smalls = [None] * depth
    row_of_expert = (jnp.arange(E, dtype=jnp.int32) == place.expert).astype(F32)[:, None]
    for l in reversed(range(depth)):
        project, merge = attends[l]
        up, down = experts[l]
        attention_state, expert_state = states[l]
        grad, (up_grad, down_grad), (gain_two, shift_two, up_b, down_b) = expert_backward(
            place, grad, expert_state, marks[l], gain[l, 1], up, down
        )
        down_grads[l] = return_expert(place, down_grad, down_weight.shape[2])
        up_grads[l] = return_expert(place, up_grad, up_weight.shape[2])
        grad, (project_grad, merge_grad), (gain_one, shift_one, attend_b, merge_b) = (
            attention_backward(grad, attention_state, gain[l, 0], project, merge)
        )
        attend_grads[l], merge_grads[l] = return_attend(place, project_grad, merge_grad)
        attend_b = attend_b.reshape(2, 2, half)
        attend_b = jnp.take(
            attend_b, jnp.arange(2, dtype=jnp.int32) ^ place.core, axis=1, mode="clip"
        )
        smalls[l] = sum_small(
            place,
            (
                jnp.stack([gain_one, gain_two]),
                jnp.stack([shift_one, shift_two]),
                merge_b,
                attend_b,
            ),
            (row_of_expert * up_b, row_of_expert * down_b),
        )
    gain_grad, shift_grad, merge_b, attend_b, up_b, down_b = (
        jnp.stack([smalls[l][k] for l in range(depth)]) for k in range(6)
    )

    def mine(value, size):
        return lax.dynamic_slice_in_dim(value, place.me * size, size, value.ndim - 1)

    attend_b = lax.dynamic_index_in_dim(attend_b, place.core, 2, False)
    return (
        output,
        whole(grad),
        mine(gain_grad, norm_gain.shape[-1]),
        mine(shift_grad, norm_gain.shape[-1]),
        jnp.stack(attend_grads),
        mine(attend_b, attend_bias.shape[-1]),
        jnp.stack(merge_grads),
        mine(merge_b, merge_bias.shape[-1]),
        jnp.stack(up_grads),
        mine(up_b, up_bias.shape[-1]),
        jnp.stack(down_grads),
        mine(down_b, down_bias.shape[-1]),
    )


def solution(mesh):
    placed = (
        P("dp", None, None),
        P("dp"),
        P(None, "dp", None, None),
        P(None, "dp", None, None),
        P(None, None, "dp"),
        P(None, None, "dp"),
        P(None, None, "dp", "tensor"),
        P(None, None, ("tensor", "dp")),
        P(None, ("tensor", "dp"), None),
        P(None, "dp"),
        P(None, None, "dp", "tensor"),
        P(None, None, ("tensor", "dp")),
        P(None, None, ("tensor", "dp"), None),
        P(None, None, "dp"),
        P("dp", None, None),
    )
    return jax.shard_map(
        functools.partial(on_device, mesh.shape["dp"]),
        mesh=mesh,
        in_specs=placed,
        out_specs=(
            P("dp", None, None),
            P("dp", None, None),
            P(None, None, "dp"),
            P(None, None, "dp"),
            P(None, None, "dp", "tensor"),
            P(None, None, ("tensor", "dp")),
            P(None, ("tensor", "dp"), None),
            P(None, "dp"),
            P(None, None, "dp", "tensor"),
            P(None, None, ("tensor", "dp")),
            P(None, None, ("tensor", "dp"), None),
            P(None, None, "dp"),
        ),
        check_vma=False,
    )
```

```python
import functools

import jax
import jax.numpy as jnp
from jax import lax
from jax.experimental import pallas as pl
from jax.experimental.pallas import tpu as pltpu
from jax.sharding import PartitionSpec as P

HD = 64
E = 4
SLOTS = 256
HALF = SLOTS // 2
FAR = (0, 1, 4, 5)
PLANE = (0, 1, 2, 3)
ROWS = 256
LOW = jnp.bfloat16
F32 = jnp.float32
SCALE = HD ** (-0.5)


def dot(left, right):
    return jnp.dot(left, right, preferred_element_type=F32)


def dot_nt(left, right):
    return lax.dot_general(left, right, (((1,), (1,)), ((), ())), preferred_element_type=F32)


def dot_tn(left, right):
    return lax.dot_general(left, right, (((0,), (0,)), ((), ())), preferred_element_type=F32)


def swap(value, bit, count):
    return lax.ppermute(value, "dp", [(i, i ^ bit) for i in range(count)])


def cross(value):
    return lax.ppermute(value, "tensor", [(0, 1), (1, 0)])


def doubled(offsets, bits):
    for bit in bits:
        offsets = offsets + [o ^ bit for o in offsets]
    return offsets


def ordered(value, offsets, me):
    where = jnp.asarray([offsets.index(i) for i in range(len(offsets))], jnp.int32)
    index = where[jnp.arange(len(offsets), dtype=jnp.int32) ^ me]
    return jnp.take(value, index, axis=0, mode="clip")


def relative(value, offsets, me):
    return jnp.take(value, jnp.asarray(offsets, jnp.int32) ^ me, axis=0, mode="clip")


def call(kernel, outs, scalars, *args, scratch=()):
    memory = pl.BlockSpec(memory_space=pltpu.VMEM)
    return pl.pallas_call(
        kernel,
        out_shape=[jax.ShapeDtypeStruct(shape, kind) for shape, kind in outs],
        in_specs=[pl.BlockSpec(memory_space=pltpu.SMEM)] + [memory] * len(args),
        out_specs=[memory] * len(outs),
        scratch_shapes=[pltpu.VMEM(shape, kind) for shape, kind in scratch],
        compiler_params=pltpu.CompilerParams(vmem_limit_bytes=44 * 2**20),
    )(scalars, *args)


def unit_of(stream):
    center = stream - jnp.mean(stream, axis=-1, keepdims=True)
    inverse = lax.rsqrt(jnp.mean(center * center, axis=-1, keepdims=True) + 1e-06)
    return center * inverse, inverse


def norm_pull(grad, unit, inverse, gain):
    scaled = grad * gain
    return inverse * (
        scaled
        - jnp.mean(scaled, axis=-1, keepdims=True)
        - unit * jnp.mean(scaled * unit, axis=-1, keepdims=True)
    )


def column_sum(value):
    return jnp.sum(value, axis=0, keepdims=True)


def place_attend(where, pieces, offsets, project, merge):
    for ref, offs in zip(pieces, offsets):
        size, wide = ref.shape[1] // 4, ref.shape[2]
        part = size // 2
        for r, off in enumerate(offs):
            i = where ^ off
            at = pl.ds(pl.multiple_of(i * size, min(size, 16)), size)
            for s in range(3):
                project[at, s * wide : (s + 1) * wide] = ref[r, s * size : (s + 1) * size, :]
            sides = ref[r, 3 * size :, :].astype(F32)
            at = pl.ds(pl.multiple_of(i * part, min(part, 8)), part)
            merge[at, :wide] = sides[:part]
            merge[at, wide:] = sides[part:]


def place_expert(where, pieces, offsets, up, down):
    for ref, offs in zip(pieces, offsets):
        size, wide = ref.shape[1] // 2, ref.shape[2] // 2
        for r, off in enumerate(offs):
            i = where ^ off
            up[pl.ds(pl.multiple_of(i * size, min(size, 16)), size), :] = ref[r, :size, :]
            at = pl.multiple_of(i * 2 * size, min(size, 16))
            down[pl.ds(at, size), :] = ref[r, size:, :wide]
            down[pl.ds(at + size, size), :] = ref[r, size:, wide:]


def slot_marks(scalars, r, target, gate):
    base = (scalars[1] ^ r) * SLOTS + scalars[2] * HALF
    slots = lax.broadcasted_iota(jnp.int32, (HALF, target.shape[1]), 0) + base
    first, second = slots == target[0:1], slots == target[1:2]
    if gate is None:
        return jnp.where(first | second, 1.0, 0.0).astype(LOW)
    weight = jnp.where(first, gate[0:1], 0.0) + jnp.where(second, gate[1:2], 0.0)
    return weight.astype(LOW)


def row_marks(slots, target, gate):
    first, second = target[:, 0:1] == slots, target[:, 1:2] == slots
    if gate is None:
        return jnp.where(first | second, 1.0, 0.0).astype(LOW)
    weight = jnp.where(first, gate[:, 0:1], 0.0) + jnp.where(second, gate[:, 1:2], 0.0)
    return weight.astype(LOW)


def combined(slots, target, gate, own, other):
    split = own.shape[0]
    return dot(row_marks(slots[:, :split], target, gate), own) + dot(
        row_marks(slots[:, split:], target, gate), other
    )


def attend_body(length, images, offsets, count, from_slots, *refs):
    scalars, refs = refs[0], refs[1:]
    if from_slots:
        middle, own, other, target, gate, slots = refs[:6]
        refs = refs[6:]
    else:
        stream_in, refs = refs[0], refs[1:]
    gain, shift, bias = refs[:3]
    pieces, refs = refs[3 : 3 + count], refs[3 + count :]
    if from_slots:
        stream_out, refs = refs[0], refs[1:]
    partial, normed, projected, probs, attended, project, merge = refs
    place_attend(scalars[0], pieces, offsets, project, merge)
    if from_slots:
        stream = middle[...] + combined(slots[...], target[...], gate[...], own[...], other[...])
        stream_out[...] = stream
    else:
        stream = stream_in[...]
    unit, inverse = unit_of(stream)
    normed[...] = (unit * gain[...] + shift[...]).astype(LOW)
    projected[...] = (dot(normed[...], project[...]) + bias[...]).astype(LOW)
    rows = stream.shape[0] // images
    wide = merge.shape[0]
    heads = wide // HD
    keep = lax.broadcasted_iota(jnp.int32, (rows, rows), 1) < length
    for i in range(images):
        span = slice(i * rows, (i + 1) * rows)
        for h in range(heads):
            query = projected[span, h * HD : (h + 1) * HD]
            keys = projected[span, wide + h * HD : wide + (h + 1) * HD]
            values = projected[span, 2 * wide + h * HD : 2 * wide + (h + 1) * HD]
            scores = jnp.where(keep, dot_nt(query, keys) * SCALE, -1e30)
            raised = jnp.exp(scores - jnp.max(scores, axis=-1, keepdims=True))
            prob = raised / jnp.sum(raised, axis=-1, keepdims=True)
            probs[i * heads + h] = prob
            attended[span, h * HD : (h + 1) * HD] = dot(prob.astype(LOW), values).astype(LOW)
    partial[...] = dot(attended[...], merge[...].astype(LOW)).astype(LOW)


def middle_body(scalars, stream, part, got, bias, gain, shift, target, middle, *sends):
    value = stream[...] + part[...].astype(F32) + got[...].astype(F32) + bias[...]
    middle[...] = value
    unit, inverse = unit_of(value)
    normed = (unit * gain[...] + shift[...]).astype(LOW)
    for r, send in enumerate(sends):
        send[...] = dot(slot_marks(scalars, r, target[...], None), normed).astype(LOW)


def expert_body(offsets, count, scalars, *refs):
    own, other, bias = refs[:3]
    pieces = refs[3 : 3 + count]
    result, result_other, active, slope, up, down = refs[3 + count :]
    place_expert(scalars[0], pieces, offsets, up, down)
    half = own.shape[0]
    for at in range(0, 2 * half, ROWS):
        rows = own[at : at + ROWS, :] if at < half else other[at - half : at - half + ROWS, :]
        hidden = dot(rows, up[...]) + bias[...]
        square = hidden * hidden
        bent = jnp.tanh(0.7978845608028654 * hidden * (1.0 + 0.044715 * square))
        low = 0.5 * (1.0 + bent)
        act = (hidden * low).astype(LOW)
        active[at : at + ROWS, :] = act
        slope[at : at + ROWS, :] = (
            low
            + hidden
            * (0.5 * 0.7978845608028654)
            * (1.0 - bent * bent)
            * (1.0 + 3 * 0.044715 * square)
        ).astype(LOW)
        out = dot(act, down[...])
        if at < half:
            result[at : at + ROWS, :] = out
        else:
            result_other[at - half : at - half + ROWS, :] = out.astype(LOW)


def total_body(scalars, part, got, bias, *sends):
    for r, send in enumerate(sends):
        at = slice(r * HALF, (r + 1) * HALF)
        send[...] = (part[at, :] + got[at, :].astype(F32) + bias[...]).astype(LOW)


def output_body(scalars, middle, own, other, target, gate, slots, valid, out):
    value = middle[...] + combined(slots[...], target[...], gate[...], own[...], other[...])
    value = value * valid[...]
    rows = value.shape[0] // out.shape[0]
    for i in range(out.shape[0]):
        out[i] = value[i * rows : i * rows + out.shape[1]]


def first_grad_body(scalars, cotangent, valid, target, gate, grad, *sends):
    value = cotangent[...] * valid[...]
    grad[...] = value
    low = value.astype(LOW)
    for r, send in enumerate(sends):
        send[...] = dot(slot_marks(scalars, r, target[...], gate[...]), low).astype(LOW)


def expert_pull_body(offsets, count, scalars, *refs):
    own, other, slope = refs[:3]
    pieces = refs[3 : 3 + count]
    result, result_other, hidden_grad, up_bias, down_bias, up, down = refs[3 + count :]
    place_expert(scalars[0], pieces, offsets, up, down)
    half = own.shape[0]
    total = jnp.zeros(up_bias.shape, F32)
    for at in range(0, 2 * half, ROWS):
        rows = own[at : at + ROWS, :] if at < half else other[at - half : at - half + ROWS, :]
        pulled = dot_nt(rows, down[...]) * slope[at : at + ROWS, :].astype(F32)
        low = pulled.astype(LOW)
        hidden_grad[at : at + ROWS, :] = low
        total = total + column_sum(low.astype(F32))
        out = dot_nt(low, up[...])
        if at < half:
            result[at : at + ROWS, :] = out
        else:
            result_other[at - half : at - half + ROWS, :] = out.astype(LOW)
    up_bias[...] = total
    down_bias[...] = column_sum(own[...].astype(F32)) + column_sum(other[...].astype(F32))


def expert_grad_body(offsets, scalars, own, other, grad_own, grad_other, active, pulled, *refs):
    pieces, (up, down) = refs[: len(offsets)], refs[len(offsets) :]
    half = own.shape[0]
    step = 512
    for at in range(0, up.shape[1], step):
        span = slice(at, at + step)
        up[:, span] = (
            dot_tn(own[...], pulled[:half, span]) + dot_tn(other[...], pulled[half:, span])
        ).astype(LOW)
        down[span, :] = (
            dot_tn(active[:half, span], grad_own[...]) + dot_tn(active[half:, span], grad_other[...])
        ).astype(LOW)
    for ref, offs in zip(pieces, offsets):
        size, wide = ref.shape[1] // 2, ref.shape[2] // 2
        for r, off in enumerate(offs):
            i = scalars[0] ^ off
            ref[r, :size, :] = up[pl.ds(pl.multiple_of(i * size, min(size, 16)), size), :]
            at = pl.multiple_of(i * 2 * size, min(size, 16))
            ref[r, size:, :wide] = down[pl.ds(at, size), :]
            ref[r, size:, wide:] = down[pl.ds(at + size, size), :]


def attend_pull_body(images, offsets, count, scalars, *refs):
    own, other, target, slots, middle, grad, gain, probs, projected = refs[:9]
    pieces = refs[9 : 9 + count]
    middle_grad, merged, pulled, first, small, project, merge = refs[9 + count :]
    place_attend(scalars[0], pieces, offsets, project, merge)
    normed_grad = combined(slots[...], target[...], None, own[...], other[...])
    unit, inverse = unit_of(middle[...])
    value = grad[...] + norm_pull(normed_grad, unit, inverse, gain[...])
    middle_grad[...] = value
    low = value.astype(LOW)
    merged[...] = low
    small[0:1, :] = column_sum(normed_grad * unit)
    small[1:2, :] = column_sum(normed_grad)
    small[2:3, :] = column_sum(low.astype(F32))
    attended_grad = dot_nt(low, merge[...].astype(LOW)).astype(LOW)
    rows = value.shape[0] // images
    wide = merge.shape[0]
    heads = wide // HD
    for i in range(images):
        span = slice(i * rows, (i + 1) * rows)
        for h in range(heads):
            spans = [slice(s * wide + h * HD, s * wide + (h + 1) * HD) for s in range(3)]
            query, keys, values = (projected[span, s] for s in spans)
            head_grad = attended_grad[span, h * HD : (h + 1) * HD]
            prob = probs[i * heads + h]
            prob_grad = dot_nt(head_grad, values)
            score_grad = prob * (prob_grad - jnp.sum(prob_grad * prob, axis=-1, keepdims=True))
            score_grad = score_grad.astype(LOW)
            pulled[span, spans[0]] = (dot(score_grad, keys) * SCALE).astype(LOW)
            pulled[span, spans[1]] = (dot_tn(score_grad, query) * SCALE).astype(LOW)
            pulled[span, spans[2]] = dot_tn(prob.astype(LOW), head_grad).astype(LOW)
    first[...] = dot_nt(pulled[...], project[...]).astype(LOW)


def attend_grad_body(offsets, scalars, normed, attended, merged, pulled, *refs):
    count = len(offsets)
    pieces, (small, project, merge) = refs[:count], refs[count:]
    wide = merge.shape[0]
    project[...] = dot_tn(normed[...], pulled[...]).astype(LOW)
    merge[...] = dot_tn(attended[...], merged[...])
    small[:, :wide] = column_sum(pulled[:, :wide].astype(F32))
    small[:, wide:] = column_sum(pulled[:, 2 * wide :].astype(F32))
    for ref, offs in zip(pieces, offsets):
        size = ref.shape[1] // 4
        part = size // 2
        for r, off in enumerate(offs):
            i = scalars[0] ^ off
            at = pl.ds(pl.multiple_of(i * size, min(size, 16)), size)
            for s in range(3):
                ref[r, s * size : (s + 1) * size, :] = project[at, s * wide : (s + 1) * wide]
            rows = merge[pl.ds(pl.multiple_of(i * part, min(part, 8)), part), :]
            sides = jnp.concatenate([rows[:, :wide], rows[:, wide:]], axis=0)
            ref[r, 3 * size :, :] = sides.astype(LOW)


def stream_pull(part, got, stream, middle_grad, gain, small):
    first = part[...].astype(F32) + got[...].astype(F32)
    unit, inverse = unit_of(stream[...])
    small[0:1, :] = column_sum(first * unit)
    small[1:2, :] = column_sum(first)
    return middle_grad[...] + norm_pull(first, unit, inverse, gain[...])


def stream_pull_body(
    scalars, part, got, stream, middle_grad, gain, target, gate, grad, small, *sends
):
    value = stream_pull(part, got, stream, middle_grad, gain, small)
    grad[...] = value
    low = value.astype(LOW)
    for r, send in enumerate(sends):
        send[...] = dot(slot_marks(scalars, r, target[...], gate[...]), low).astype(LOW)


def last_pull_body(scalars, part, got, stream, middle_grad, gain, out, small):
    value = stream_pull(part, got, stream, middle_grad, gain, small)
    rows = value.shape[0] // out.shape[0]
    for i in range(out.shape[0]):
        out[i] = value[i * rows : i * rows + out.shape[1]]


class Place:
    def __init__(self, count, rows):
        self.count = count
        self.me = lax.axis_index("dp").astype(jnp.int32)
        self.core = lax.axis_index("tensor").astype(jnp.int32)
        self.expert = ((self.me >> 2) & 1) * 2 + (self.me & 1)
        powers = [1 << k for k in range(count.bit_length() - 1)]
        self.group_bits = [b for b in reversed(powers) if b not in (1, 4)]
        self.column_bits = [b for b in reversed(powers) if b not in (1, 2)]
        self.aligned = rows % 16 == 0
        self.near = self.expert ^ jnp.arange(E, dtype=jnp.int32)
        where = self.me if self.aligned else jnp.zeros((), jnp.int32)
        self.scalars = jnp.stack([where, self.expert, self.core])
        group = [[o ^ f for f in FAR] for o in doubled([0], self.group_bits)]
        column = doubled([0], self.column_bits)
        plane = [[c ^ p for c in column] for p in PLANE]
        self.group_all = [o for offs in group for o in offs]
        self.plane_all = [o for offs in plane for o in offs]
        self.group_offsets = group if self.aligned else [[0]]
        self.plane_offsets = plane if self.aligned else [[0]]

    def deal(self, chunks):
        return [chunks[0]] + [swap(chunks[r], FAR[r], self.count) for r in range(1, E)]


def fetch_small(place, pieces):
    flat = jnp.concatenate([p.reshape(-1) for p in pieces])
    used = flat.shape[0]
    room = -(-used // 2048) * 2048
    flat = jnp.pad(flat, (0, room - used)).reshape(1, room // 128, 128)
    bits = [1 << k for k in range(place.count.bit_length() - 1)]
    for bit in bits:
        flat = jnp.concatenate([flat, swap(flat, bit, place.count)], axis=0)
    full = ordered(flat, doubled([0], bits), place.me).reshape(place.count, room)
    out, at = [], 0
    for piece in pieces:
        part = full[:, at : at + piece.size].reshape((place.count,) + piece.shape)
        at += piece.size
        part = jnp.moveaxis(part, 0, -2)
        out.append(part.reshape(part.shape[:-2] + (-1,)).astype(F32))
    return out


def pack_attend(attend, merge):
    count, kinds, depth, wide = attend.shape
    rows = attend.reshape(count, 3 * depth, wide)
    return jnp.concatenate([rows, merge[:, :, :wide], merge[:, :, wide:]], axis=1)


def unpack_attend(pack):
    count, rows, wide = pack.shape
    depth = rows // 4
    attend = pack[:, : 3 * depth].reshape(count, 3, depth, wide)
    sides = pack[:, 3 * depth :]
    return attend, jnp.concatenate([sides[:, : depth // 2], sides[:, depth // 2 :]], axis=2)


def pack_expert(up, down):
    depth = up.shape[1]
    return jnp.concatenate(
        [up, jnp.concatenate([down[:, :depth], down[:, depth:]], axis=2)], axis=1
    )


def unpack_expert(pack):
    depth, wide = pack.shape[1] // 2, pack.shape[2] // 2
    low = pack[:, depth:]
    return pack[:, :depth], jnp.concatenate([low[:, :, :wide], low[:, :, wide:]], axis=1)


def whole_attend(pack):
    attend, merge = unpack_attend(pack)
    attend = jnp.swapaxes(attend, 0, 1)
    attend = attend.reshape(3, -1, attend.shape[-1])
    return pack_attend(attend[None], merge.reshape(1, -1, merge.shape[-1]))


def split_attend(pack, count):
    attend, merge = unpack_attend(pack)
    attend = jnp.swapaxes(attend.reshape(3, count, -1, attend.shape[-1]), 0, 1)
    return pack_attend(attend, merge.reshape(count, -1, merge.shape[-1]))


def whole_expert(pack):
    up, down = unpack_expert(pack)
    return pack_expert(up.reshape(1, -1, up.shape[-1]), down.reshape(1, -1, down.shape[-1]))


def split_expert(pack, count):
    up, down = unpack_expert(pack)
    return pack_expert(
        up.reshape(count, -1, up.shape[-1]), down.reshape(count, -1, down.shape[-1])
    )


def fetch_attend(place, attend, merge):
    blocks = [pack_attend(attend[None], merge[None])]
    for bit in place.column_bits:
        blocks = blocks + [swap(b, bit, place.count) for b in blocks]
    column = jnp.concatenate(blocks, axis=0)
    pieces = [column] + [swap(column, p, place.count) for p in PLANE[1:]]
    if place.aligned:
        return pieces
    return [whole_attend(ordered(jnp.concatenate(pieces), place.plane_all, place.me))]


def fetch_expert(place, up, down):
    pack = jnp.take(pack_expert(up, down), place.near, axis=0, mode="clip")
    pieces = [jnp.stack(place.deal(list(pack)))]
    for bit in place.group_bits:
        pieces = pieces + [swap(p, bit, place.count) for p in pieces]
    if place.aligned:
        return pieces
    return [whole_expert(ordered(jnp.concatenate(pieces), place.group_all, place.me))]


def add_low(*terms):
    return sum(t.astype(F32) for t in terms).astype(LOW)


def return_expert(place, pieces):
    if not place.aligned:
        full = relative(split_expert(pieces[0], place.count), place.group_all, place.me)
        pieces = list(full.reshape((-1, E) + full.shape[1:]))
    for bit in reversed(place.group_bits):
        half = len(pieces) // 2
        got = [swap(p, bit, place.count) for p in pieces[half:]]
        pieces = [add_low(p, g) for p, g in zip(pieces[:half], got)]
    return place.deal(list(pieces[0]))


def finish_expert(place, blocks):
    pack = jnp.take(jnp.stack(blocks), place.near, axis=0, mode="clip")
    up, down = unpack_expert(pack)
    return up.astype(F32), down.astype(F32)


def return_attend(place, pieces):
    if not place.aligned:
        full = relative(split_attend(pieces[0], place.count), place.plane_all, place.me)
        pieces = list(full.reshape((len(PLANE), -1) + full.shape[1:]))
    got = [swap(pieces[p], p, place.count) for p in PLANE[1:]]
    value = add_low(pieces[0], *got)
    for bit in reversed(place.column_bits):
        half = value.shape[0] // 2
        got = swap(value[half:], bit, place.count)
        value = add_low(value[:half], got)
    attend, merge = unpack_attend(value)
    return attend[0].astype(F32), merge[0].astype(F32)


def exchange(place, chunks):
    own = jnp.concatenate(place.deal(chunks), axis=0)
    return own, cross(own)


def slot_targets(routes, valid):
    chosen = (routes[..., None] == jnp.arange(E, dtype=jnp.int32)).astype(jnp.int32)
    chosen = chosen * valid.astype(jnp.int32)[None, :, None, None]
    taken = jnp.sum(chosen, axis=2)
    before = jnp.cumsum(taken, axis=1) - taken
    slot = jnp.sum(chosen * before[:, :, None, :], axis=-1)
    return jnp.where(valid[None, :, None], routes * SLOTS + slot, -1)


def on_device(
    count,
    inputs,
    image_count,
    routes,
    gates,
    norm_gain,
    norm_shift,
    attend_weight,
    attend_bias,
    merge_weight,
    merge_bias,
    up_weight,
    up_bias,
    down_weight,
    down_bias,
    cotangent,
):
    images, length, width = inputs.shape
    depth = routes.shape[0]
    wide = attend_weight.shape[-1]
    hidden = up_weight.shape[-1]
    heads = wide // HD
    place = Place(count, up_weight.shape[2])
    scalars = place.scalars
    rows = -(-length // 16) * 16
    total = images * rows

    def padded(value, fill=0):
        spare = [(0, 0)] * value.ndim
        spare[-2] = (0, rows - length)
        value = jnp.pad(value, spare, constant_values=fill)
        return value.reshape(value.shape[:-3] + (total, value.shape[-1]))

    attends = [fetch_attend(place, attend_weight[l], merge_weight[l]) for l in range(depth)]
    gain, shift, merge_shift, attend_shift, up_shift, down_shift = fetch_small(
        place, (norm_gain, norm_shift, merge_bias, attend_bias, up_bias, down_bias)
    )
    experts = [fetch_expert(place, up_weight[l], down_weight[l]) for l in range(depth)]
    project_shift = jnp.concatenate(
        [attend_shift[:, 0], jnp.zeros_like(attend_shift[:, 0]), attend_shift[:, 1]], axis=-1
    )[:, None]
    up_shift = lax.dynamic_index_in_dim(up_shift, place.expert, 1)
    down_shift = lax.dynamic_index_in_dim(down_shift, place.expert, 1)
    gain, shift, merge_shift = gain[:, :, None], shift[:, :, None], merge_shift[:, None]

    here = jnp.arange(images, dtype=jnp.int32) < image_count[0]
    valid = jnp.repeat(here, length)
    target = slot_targets(routes.reshape(depth, -1, 2), valid)
    target = padded(target.reshape(depth, images, length, 2), -1)
    gate = padded(gates)
    target_rows, gate_rows = jnp.swapaxes(target, 1, 2), jnp.swapaxes(gate, 1, 2)
    live = jnp.repeat(here, rows).astype(F32)[:, None]
    lane = jnp.arange(HALF, dtype=jnp.int32)
    sides = jnp.stack([place.core, 1 - place.core])
    slots = place.near[None, :, None] * SLOTS + sides[:, None, None] * HALF + lane
    slots = slots.reshape(1, -1)
    half = E * HALF

    chunk = ((HALF, width), LOW)
    stream = padded(inputs)
    zero = jnp.zeros((1, width), F32)
    states = []
    back = None
    for l in range(depth):
        pieces = attends[l]
        outs = [
            ((total, width), LOW),
            ((total, width), LOW),
            ((total, 3 * wide), LOW),
            ((images * heads, rows, rows), F32),
            ((total, wide), LOW),
        ]
        scratch = [((width, 3 * wide), LOW), ((wide, width), F32)]
        body = functools.partial(
            attend_body, length, images, place.plane_offsets, len(pieces), l > 0
        )
        common = (gain[l, 0], shift[l, 0], project_shift[l], *pieces)
        if l == 0:
            made = call(body, outs, scalars, stream, *common, scratch=scratch)
        else:
            made = call(
                body,
                [((total, width), F32)] + outs,
                scalars,
                middle,
                *back,
                target[l - 1],
                gate[l - 1],
                slots,
                *common,
                scratch=scratch,
            )
            stream, made = made[0], made[1:]
        part, normed, projected, probs, attended = made
        middle, *sends = call(
            middle_body,
            [((total, width), F32)] + [chunk] * E,
            scalars,
            stream,
            part,
            cross(part),
            merge_shift[l],
            gain[l, 1],
            shift[l, 1],
            target_rows[l],
        )
        taken = exchange(place, sends)
        result, result_other, active, slope = call(
            functools.partial(expert_body, place.group_offsets, len(experts[l])),
            [
                ((half, width), F32),
                ((half, width), LOW),
                ((2 * half, hidden), LOW),
                ((2 * half, hidden), LOW),
            ],
            scalars,
            *taken,
            up_shift[l],
            *experts[l],
            scratch=[((width, hidden), LOW), ((hidden, width), LOW)],
        )
        sends = call(
            total_body, [chunk] * E, scalars, result, cross(result_other), down_shift[l]
        )
        back = exchange(place, sends)
        states.append(
            (stream, middle, normed, projected, probs, attended, taken, active, slope)
        )

    (output,) = call(
        output_body,
        [(inputs.shape, F32)],
        scalars,
        middle,
        *back,
        target[-1],
        gate[-1],
        slots,
        live,
    )
    grad, *sends = call(
        first_grad_body,
        [((total, width), F32)] + [chunk] * E,
        scalars,
        padded(cotangent),
        live,
        target_rows[-1],
        gate_rows[-1],
    )

    expert_blocks, attend_grads, smalls = [None] * depth, [None] * depth, [None] * depth
    for l in reversed(range(depth)):
        stream, middle, normed, projected, probs, attended, taken, active, slope = states[l]
        slot_grad = exchange(place, sends)
        result, result_other, pulled, up_b, down_b = call(
            functools.partial(expert_pull_body, place.group_offsets, len(experts[l])),
            [
                ((half, width), F32),
                ((half, width), LOW),
                ((2 * half, hidden), LOW),
                ((1, hidden), F32),
                ((1, width), F32),
            ],
            scalars,
            *slot_grad,
            slope,
            *experts[l],
            scratch=[((width, hidden), LOW), ((hidden, width), LOW)],
        )
        sends = call(total_body, [chunk] * E, scalars, result, cross(result_other), zero)
        back = exchange(place, sends)
        pieces = call(
            functools.partial(expert_grad_body, place.group_offsets),
            [(p.shape, LOW) for p in experts[l]],
            scalars,
            *taken,
            *slot_grad,
            active,
            pulled,
            scratch=[((width, hidden), LOW), ((hidden, width), LOW)],
        )
        expert_blocks[l] = return_expert(place, pieces)
        middle_grad, merged, pulled, first, small_two = call(
            functools.partial(
                attend_pull_body, images, place.plane_offsets, len(attends[l])
            ),
            [
                ((total, width), F32),
                ((total, width), LOW),
                ((total, 3 * wide), LOW),
                ((total, width), LOW),
                ((3, width), F32),
            ],
            scalars,
            *back,
            target[l],
            slots,
            middle,
            grad,
            gain[l, 1],
            probs,
            projected,
            *attends[l],
            scratch=[((width, 3 * wide), LOW), ((wide, width), F32)],
        )
        got = cross(first)
        *pieces, small_bias = call(
            functools.partial(attend_grad_body, place.plane_offsets),
            [(p.shape, LOW) for p in attends[l]] + [((1, width), F32)],
            scalars,
            normed,
            attended,
            merged,
            pulled,
            scratch=[((width, 3 * wide), LOW), ((wide, width), F32)],
        )
        attend_grads[l] = return_attend(place, pieces)
        if l > 0:
            grad, small_one, *sends = call(
                stream_pull_body,
                [((total, width), F32), ((2, width), F32)] + [chunk] * E,
                scalars,
                first,
                got,
                stream,
                middle_grad,
                gain[l, 0],
                target_rows[l - 1],
                gate_rows[l - 1],
            )
        else:
            input_grad, small_one = call(
                last_pull_body,
                [(inputs.shape, F32), ((2, width), F32)],
                scalars,
                first,
                got,
                stream,
                middle_grad,
                gain[l, 0],
            )
        at_expert = jnp.arange(E, dtype=jnp.int32)[:, None, None] == place.expert
        expert_rows = jnp.concatenate([up_b.reshape(-1, width), down_b], axis=0)
        expert_rows = jnp.where(at_expert, expert_rows[None], 0.0)
        smalls[l] = jnp.concatenate(
            [small_one, small_two, small_bias, expert_rows.reshape(-1, width)], axis=0
        )

    small = jnp.stack(smalls)
    for bit in [1 << k for k in range(count.bit_length() - 1)]:
        small = small + swap(small, bit, count)

    def mine(value, size):
        return lax.dynamic_slice_in_dim(value, place.me * size, size, value.ndim - 1)

    share = norm_gain.shape[-1]
    gain_grad = jnp.stack([small[:, 0], small[:, 2]], axis=1)
    shift_grad = jnp.stack([small[:, 1], small[:, 3]], axis=1)
    attend_b = small[:, 5].reshape(depth, 2, wide)
    expert_rows = small[:, 6:].reshape(depth, E, -1, width)
    up_b = expert_rows[:, :, :-1].reshape(depth, E, hidden)
    finished = [finish_expert(place, blocks) for blocks in expert_blocks]
    return (
        output,
        input_grad,
        mine(gain_grad, share),
        mine(shift_grad, share),
        jnp.stack([g[0] for g in attend_grads]),
        mine(attend_b, attend_bias.shape[-1]),
        jnp.stack([g[1] for g in attend_grads]),
        mine(small[:, 4], share),
        jnp.stack([g[0] for g in finished]),
        mine(up_b, up_bias.shape[-1]),
        jnp.stack([g[1] for g in finished]),
        mine(expert_rows[:, :, -1], share),
    )


def solution(mesh):
    placed = (
        P("dp", None, None),
        P("dp"),
        P(None, "dp", None, None),
        P(None, "dp", None, None),
        P(None, None, "dp"),
        P(None, None, "dp"),
        P(None, None, "dp", "tensor"),
        P(None, None, ("tensor", "dp")),
        P(None, ("tensor", "dp"), None),
        P(None, "dp"),
        P(None, None, "dp", "tensor"),
        P(None, None, ("tensor", "dp")),
        P(None, None, ("tensor", "dp"), None),
        P(None, None, "dp"),
        P("dp", None, None),
    )
    return jax.shard_map(
        functools.partial(on_device, mesh.shape["dp"]),
        mesh=mesh,
        in_specs=placed,
        out_specs=(
            P("dp", None, None),
            P("dp", None, None),
            P(None, None, "dp"),
            P(None, None, "dp"),
            P(None, None, "dp", "tensor"),
            P(None, None, ("tensor", "dp")),
            P(None, ("tensor", "dp"), None),
            P(None, "dp"),
            P(None, None, "dp", "tensor"),
            P(None, None, ("tensor", "dp")),
            P(None, None, ("tensor", "dp"), None),
            P(None, None, "dp"),
        ),
        check_vma=False,
    )
```

```python
import functools

import jax
import jax.numpy as jnp
from jax import lax
from jax.experimental import pallas as pl
from jax.experimental.pallas import tpu as pltpu
from jax.sharding import PartitionSpec as P

HD = 64
E = 4
SLOTS = 256
HALF = SLOTS // 2
PLANE = (0, 1, 2, 3)
LINE = (0, 4, 8, 12)
ROWS = 256
STEP = 512
LONG = 60
VMEM = 24 * 2**20
LOW = jnp.bfloat16
F32 = jnp.float32
SCALE = HD ** (-0.5)


def dot(left, right):
    return jnp.dot(left, right, preferred_element_type=F32)


def dot_nt(left, right):
    return lax.dot_general(left, right, (((1,), (1,)), ((), ())), preferred_element_type=F32)


def dot_tn(left, right):
    return lax.dot_general(left, right, (((0,), (0,)), ((), ())), preferred_element_type=F32)


def swap(value, bit, count):
    return lax.ppermute(value, "dp", [(i, i ^ bit) for i in range(count)])


def after(value, *anchors):
    return lax.optimization_barrier((value, anchors))[0]


def cross(value):
    return lax.ppermute(value, "tensor", [(0, 1), (1, 0)])


def doubled(offsets, bits):
    for bit in bits:
        offsets = offsets + [o ^ bit for o in offsets]
    return offsets


def ordered(value, offsets, me):
    where = jnp.asarray([offsets.index(i) for i in range(len(offsets))], jnp.int32)
    index = where[jnp.arange(len(offsets), dtype=jnp.int32) ^ me]
    return jnp.take(value, index, axis=0, mode="clip")


def relative(value, offsets, me):
    return jnp.take(value, jnp.asarray(offsets, jnp.int32) ^ me, axis=0, mode="clip")


def call(kernel, outs, scalars, *args, saved=(), scratch=(), before=(), stored=False, us=0):
    memory = pl.BlockSpec(memory_space=pltpu.VMEM)

    def body(*refs):
        ships = saved or stored
        sems = refs[-1] if ships else None
        started, settled = [], []

        def ship(source, target):
            copy = pltpu.make_async_copy(source, target, sems.at[len(started)])
            copy.start()
            started.append(copy)
            return copy

        def wait(copies):
            for copy in copies:
                copy.wait()
            settled.extend(copies)

        ship.wait = wait
        if ships:
            kernel(ship, *refs[:-1])
        else:
            kernel(*refs)
        for copy in started:
            if not any(copy is done for done in settled):
                copy.wait()

    if before:
        scalars = after(scalars, *before)
    return pl.pallas_call(
        body,
        out_shape=[jax.ShapeDtypeStruct(shape, kind) for shape, kind in outs]
        + [pltpu.HBM(shape, kind) for shape, kind in saved],
        in_specs=[pl.BlockSpec(memory_space=pltpu.SMEM)]
        + [pl.BlockSpec(memory_space=pltpu.HBM) if stored else memory] * len(args),
        out_specs=[memory] * len(outs) + [pl.BlockSpec(memory_space=pltpu.HBM)] * len(saved),
        scratch_shapes=[pltpu.VMEM(shape, kind) for shape, kind in scratch]
        + ([pltpu.SemaphoreType.DMA((24,))] if saved or stored else []),
        compiler_params=pltpu.CompilerParams(vmem_limit_bytes=VMEM),
        cost_estimate=pl.CostEstimate(
            flops=us * 10**9, transcendentals=0, bytes_accessed=us * 10**3
        ),
    )(scalars, *args)


def unit_of(stream):
    center = stream - jnp.mean(stream, axis=-1, keepdims=True)
    inverse = lax.rsqrt(jnp.mean(center * center, axis=-1, keepdims=True) + 1e-06)
    return center * inverse, inverse


def norm_pull(grad, unit, inverse, gain):
    scaled = grad * gain
    return inverse * (
        scaled
        - jnp.mean(scaled, axis=-1, keepdims=True)
        - unit * jnp.mean(scaled * unit, axis=-1, keepdims=True)
    )


def column_sum(value):
    return jnp.sum(value, axis=0, keepdims=True)


def place_attend(where, size, pieces, offsets, project, merge):
    for ref, offs in zip(pieces, offsets):
        wide, part = ref.shape[2], size // 2
        for r, off in enumerate(offs):
            i = where ^ off
            at = pl.ds(pl.multiple_of(i * size, min(size, 16)), size)
            for s in range(3):
                project[at, s * wide : (s + 1) * wide] = ref[r, s * size : (s + 1) * size, :]
            sides = ref[r, 3 * size : 4 * size, :].astype(F32)
            at = pl.ds(pl.multiple_of(i * part, min(part, 8)), part)
            merge[at, :wide] = sides[:part]
            merge[at, wide:] = sides[part:]


def place_expert(where, pieces, offsets, up, down):
    for ref, offs in zip(pieces, offsets):
        size, wide = ref.shape[1] // 2, ref.shape[2] // 2
        for r, off in enumerate(offs):
            i = where ^ off
            up[pl.ds(pl.multiple_of(i * size, min(size, 16)), size), :] = ref[r, :size, :]
            at = pl.multiple_of(i * 2 * size, min(size, 16))
            down[pl.ds(at, size), :] = ref[r, size:, :wide]
            down[pl.ds(at + size, size), :] = ref[r, size:, wide:]


def rows_of(chunks):
    return jnp.concatenate([c[...] for c in chunks], axis=0)


def slot_marks(scalars, r, target, gate):
    base = (scalars[1] ^ r) * SLOTS + scalars[2] * HALF
    slots = lax.broadcasted_iota(jnp.int32, (HALF, target.shape[1]), 0) + base
    first, second = slots == target[0:1], slots == target[1:2]
    if gate is None:
        return jnp.where(first | second, 1.0, 0.0).astype(LOW)
    weight = jnp.where(first, gate[0:1], 0.0) + jnp.where(second, gate[1:2], 0.0)
    return weight.astype(LOW)


def row_marks(slots, target, gate):
    first, second = target[:, 0:1] == slots, target[:, 1:2] == slots
    if gate is None:
        return jnp.where(first | second, 1.0, 0.0).astype(LOW)
    weight = jnp.where(first, gate[:, 0:1], 0.0) + jnp.where(second, gate[:, 1:2], 0.0)
    return weight.astype(LOW)


def combined(scalars, target, gate, chunks):
    marks = []
    for h in range(2):
        for r in range(E):
            base = (scalars[1] ^ r) * SLOTS + (scalars[2] ^ h) * HALF
            slots = lax.broadcasted_iota(jnp.int32, (1, HALF), 1) + base
            marks.append(row_marks(slots, target, gate))
    return dot(jnp.concatenate(marks, axis=1), rows_of(chunks))


def owned(vector, owners, wide, at):
    count = vector.shape[1]
    share = count // owners
    lane = lax.broadcasted_iota(jnp.int32, (owners, count), 1)
    start = lax.broadcasted_iota(jnp.int32, (owners, count), 0) * share
    mine = jnp.where((lane >= start) & (lane < start + share), vector, 0.0).astype(LOW)
    lane = lax.broadcasted_iota(jnp.int32, (count, 128), 0)
    turn = jnp.floor((lane.astype(F32) + 0.5) * (1.0 / share)).astype(jnp.int32)
    home = lane - turn * share == lax.broadcasted_iota(jnp.int32, (count, 128), 1)
    packed = dot(mine, jnp.where(home, 1.0, 0.0).astype(LOW)).astype(LOW)
    lane = lax.broadcasted_iota(jnp.int32, (128, wide), 0)
    home = (lane + at == lax.broadcasted_iota(jnp.int32, (128, wide), 1)) & (lane < share)
    return dot(packed, jnp.where(home, 1.0, 0.0).astype(LOW))


def join_vectors(scalars, small, vectors):
    owners = small.shape[0]

    def joined(part):
        wide = part.shape[1]
        lane = lax.broadcasted_iota(jnp.int32, (wide, owners * wide), 1)
        turn = jnp.floor((lane.astype(F32) + 0.5) * (1.0 / wide)).astype(jnp.int32)
        place = lane - turn * wide == lax.broadcasted_iota(jnp.int32, lane.shape, 0)
        spread = dot(part.astype(LOW), jnp.where(place, 1.0, 0.0).astype(LOW))
        start = lax.broadcasted_iota(jnp.int32, spread.shape, 0) * wide
        lane = lax.broadcasted_iota(jnp.int32, spread.shape, 1)
        return column_sum(jnp.where((lane >= start) & (lane < start + wide), spread, 0.0))

    share = small.shape[2] // 8
    half = share // 2
    expert = scalars[1]
    for l in range(vectors.shape[0]):
        first, second, third = (small[:, 3 * l + k, :] for k in range(3))
        parts = [first[:, k * share : (k + 1) * share] for k in range(5)]
        for k, part in enumerate(parts):
            vectors[l, k : k + 1, : owners * share] = joined(part)
        at = 5 * share
        query, values = (joined(first[:, at + k * half : at + (k + 1) * half]) for k in range(2))
        vectors[l, 5:6, : 3 * owners * half] = jnp.concatenate(
            [query, jnp.zeros_like(query), values], axis=1
        )
        up = sum(
            jnp.where(expert == e, third[:, 2 * e * share : 2 * (e + 1) * share], 0.0)
            for e in range(E)
        )
        vectors[l, 6:7, :] = joined(up)
        down = sum(
            jnp.where(expert == e, second[:, e * share : (e + 1) * share], 0.0) for e in range(E)
        )
        vectors[l, 7:8, : owners * share] = joined(down)


def live_rows(scalars, rows, images):
    return lax.broadcasted_iota(jnp.int32, (rows, 1), 0) < scalars[3] * (rows // images)


def attend_body(length, images, size, offsets, from_slots, split, ship, *refs):
    count = len(offsets)
    scalars, refs = refs[0], refs[1:]
    if from_slots:
        middle, *back = refs[: 1 + 2 * E]
        target, gate, vectors = refs[1 + 2 * E : 4 + 2 * E]
        refs = refs[4 + 2 * E :]
    else:
        stream_in, refs = refs[0], refs[1:]
        if split:
            small, refs = refs[0], refs[1:]
    pieces, refs = refs[:count], refs[count:]
    if from_slots:
        stream_out, partial, stream_kept, *refs = refs
    else:
        partial, all_vectors, *refs = refs
        vectors = all_vectors.at[0]
    kept, (normed, projected, probs, attended, project, merge, *rest) = refs[:4], refs[4:]
    place_attend(scalars[0], size, pieces, offsets, project, merge)
    if not from_slots:
        if not split:
            (small,) = rest
            for ref, offs in zip(pieces, offsets):
                for r, off in enumerate(offs):
                    small[scalars[0] ^ off] = ref[r, 4 * size :, :]
        join_vectors(scalars, small[...].astype(F32), all_vectors)
    if from_slots:
        stream = middle[...] + combined(scalars, target[...], gate[...], back)
        stream_out[...] = stream
        ship(stream_out, stream_kept)
    else:
        stream = stream_in[...]
    unit, inverse = unit_of(stream)
    width = stream.shape[1]
    normed[...] = (unit * vectors[0:1, :width] + vectors[2:3, :width]).astype(LOW)
    ship(normed, kept[0])
    bias = vectors[5:6, : project.shape[1]]
    projected[...] = (dot(normed[...], project[...]) + bias).astype(LOW)
    ship(projected, kept[1])
    rows = stream.shape[0] // images
    wide = merge.shape[0]
    heads = wide // HD
    keep = lax.broadcasted_iota(jnp.int32, (rows, rows), 1) < length
    for i in range(images):
        span = slice(i * rows, (i + 1) * rows)
        for h in range(heads):
            query = projected[span, h * HD : (h + 1) * HD]
            keys = projected[span, wide + h * HD : wide + (h + 1) * HD]
            values = projected[span, 2 * wide + h * HD : 2 * wide + (h + 1) * HD]
            scores = jnp.where(keep, dot_nt(query, keys) * SCALE, -1e30)
            raised = jnp.exp(scores - jnp.max(scores, axis=-1, keepdims=True))
            prob = raised / jnp.sum(raised, axis=-1, keepdims=True)
            prob_low = prob.astype(LOW)
            probs[i * heads + h] = prob_low
            attended[span, h * HD : (h + 1) * HD] = dot(prob_low, values).astype(LOW)
        ship(probs.at[pl.ds(i * heads, heads)], kept[2].at[pl.ds(i * heads, heads)])
    ship(attended, kept[3])
    partial[...] = dot(attended[...], merge[...].astype(LOW)).astype(LOW)


def middle_body(ship, scalars, stream, part, got, vectors, target, middle, *refs):
    sends, kept = refs[:E], refs[E]
    width = stream.shape[1]
    gain, shift, bias = (vectors[k : k + 1, :width] for k in (1, 3, 4))
    value = stream[...] + part[...].astype(F32) + got[...].astype(F32) + bias
    middle[...] = value
    ship(middle, kept)
    unit, inverse = unit_of(value)
    normed = (unit * gain + shift).astype(LOW)
    for r, send in enumerate(sends):
        send[...] = dot(slot_marks(scalars, r, target[...], None), normed).astype(LOW)


def expert_body(offsets, last, ship, scalars, *refs):
    count = len(offsets)
    chunks, vectors, refs = refs[: 2 * E], refs[2 * E], refs[2 * E + 1 :]
    pieces, refs = refs[:count], refs[count:]
    if last:
        others_kept, refs = refs[0], refs[1:]
        others, refs = refs[-1], refs[:-1]
    else:
        others, refs = refs[:E], refs[E:]
    result_kept, active_kept, slope_kept, rows_kept, result, active, slope, rows, up, down = refs
    place_expert(scalars[0], pieces, offsets, up, down)
    bias = vectors[6:7, :]
    for k in reversed(range(0, 2 * E, 2)):
        at = k * HALF
        span = pl.ds(at, 2 * HALF)
        rows[span, :] = rows_of(chunks[k : k + 2])
        ship(rows.at[span], rows_kept.at[span])
        hidden = dot(rows[span, :], up[...]) + bias
        square = hidden * hidden
        bent = jnp.tanh(0.7978845608028654 * hidden * (1.0 + 0.044715 * square))
        low = 0.5 * (1.0 + bent)
        act = (hidden * low).astype(LOW)
        active[span, :] = act
        slope[span, :] = (
            low
            + hidden
            * (0.5 * 0.7978845608028654)
            * (1.0 - bent * bent)
            * (1.0 + 3 * 0.044715 * square)
        ).astype(LOW)
        ship(active.at[span], active_kept.at[span])
        ship(slope.at[span], slope_kept.at[span])
        out = dot(act, down[...])
        if k < E:
            result[span, :] = out
            ship(result.at[span], result_kept.at[span])
        elif last:
            span = pl.ds(at - E * HALF, 2 * HALF)
            others[span, :] = out.astype(LOW)
            ship(others.at[span], others_kept.at[span])
        else:
            others[k - E][...] = out[:HALF].astype(LOW)
            others[k - E + 1][...] = out[HALF:].astype(LOW)


def total_body(scalars, part, *refs):
    got, sends = refs[:-E], refs[-E:]
    vectors = None
    if got[-1].dtype == F32:
        got, vectors = got[:-1], got[-1]
    for r, send in enumerate(sends):
        span = slice(r * HALF, (r + 1) * HALF)
        more = got[r][...] if len(got) == E else got[0][span, :]
        value = part[span, :] + more.astype(F32)
        if vectors is not None:
            value = value + vectors[7:8, : value.shape[1]]
        send[...] = value.astype(LOW)


def output_body(scalars, middle, *refs):
    chunks, (target, gate, out) = refs[: 2 * E], refs[2 * E :]
    value = middle[...] + combined(scalars, target[...], gate[...], chunks)
    value = jnp.where(live_rows(scalars, value.shape[0], out.shape[0]), value, 0.0)
    rows = value.shape[0] // out.shape[0]
    for i in range(out.shape[0]):
        out[i] = value[i * rows : i * rows + out.shape[1]]


def first_grad_body(images, scalars, cotangent, target, gate, grad, *sends):
    value = jnp.where(live_rows(scalars, grad.shape[0], images), cotangent[...], 0.0)
    grad[...] = value
    low = value.astype(LOW)
    for r, send in enumerate(sends):
        send[...] = dot(slot_marks(scalars, r, target[...], gate[...]), low).astype(LOW)


def expert_pull_body(offsets, ship, scalars, *refs):
    count = len(offsets)
    chunks, slope, refs = refs[: 2 * E], refs[2 * E], refs[2 * E + 1 :]
    pieces, others, refs = refs[:count], refs[count : count + E], refs[count + E :]
    up_bias, down_bias, result_kept, hidden_kept, rows_kept, *refs = refs
    result, hidden_grad, rows, up, down = refs
    place_expert(scalars[0], pieces, offsets, up, down)
    total = jnp.zeros(up_bias.shape, F32)
    total_down = jnp.zeros(down_bias.shape, F32)
    for k in reversed(range(0, 2 * E, 2)):
        span = pl.ds(k * HALF, 2 * HALF)
        value = rows_of(chunks[k : k + 2])
        rows[span, :] = value
        ship(rows.at[span], rows_kept.at[span])
        total_down = total_down + column_sum(value.astype(F32))
        low = (dot_nt(value, down[...]) * slope[span, :].astype(F32)).astype(LOW)
        hidden_grad[span, :] = low
        ship(hidden_grad.at[span], hidden_kept.at[span])
        total = total + column_sum(low.astype(F32))
        out = dot_nt(low, up[...])
        if k < E:
            result[span, :] = out
            ship(result.at[span], result_kept.at[span])
        else:
            others[k - E][...] = out[:HALF].astype(LOW)
            others[k - E + 1][...] = out[HALF:].astype(LOW)
    up_bias[...] = total
    down_bias[...] = total_down


def expert_grad_body(offsets, scalars, slot_rows, active, rows, pulled, *refs):
    pieces, (up, down) = refs[: len(offsets)], refs[len(offsets) :]
    for at in range(0, up.shape[1], STEP):
        span = slice(at, at + STEP)
        down[span, :] = dot_tn(active[:, span], slot_rows[...]).astype(LOW)
        up[:, span] = dot_tn(rows[...], pulled[:, span]).astype(LOW)
    for ref, offs in zip(pieces, offsets):
        size, wide = ref.shape[1] // 2, ref.shape[2] // 2
        for r, off in enumerate(offs):
            i = scalars[0] ^ off
            ref[r, :size, :] = up[pl.ds(pl.multiple_of(i * size, min(size, 16)), size), :]
            at = pl.multiple_of(i * 2 * size, min(size, 16))
            ref[r, size:, :wide] = down[pl.ds(at, size), :]
            ref[r, size:, wide:] = down[pl.ds(at + size, size), :]


def attend_pull_body(images, size, offsets, ship, scalars, *refs):
    count = len(offsets)
    chunks, refs = refs[: 2 * E], refs[2 * E :]
    target, middle, grad, vectors, probs, projected = refs[:6]
    pieces = refs[6 : 6 + count]
    first, small, middle_kept, merged_kept, pulled_kept, *refs = refs[6 + count :]
    middle_grad, merged, pulled, project, merge = refs
    place_attend(scalars[0], size, pieces, offsets, project, merge)
    normed_grad = combined(scalars, target[...], None, chunks)
    unit, inverse = unit_of(middle[...])
    value = grad[...] + norm_pull(normed_grad, unit, inverse, vectors[1:2, : grad.shape[1]])
    middle_grad[...] = value
    ship(middle_grad, middle_kept)
    low = value.astype(LOW)
    merged[...] = low
    ship(merged, merged_kept)
    small[0:1, :] = column_sum(normed_grad * unit)
    small[1:2, :] = column_sum(normed_grad)
    small[2:3, :] = column_sum(low.astype(F32))
    attended_grad = dot_nt(low, merge[...].astype(LOW)).astype(LOW)
    rows = value.shape[0] // images
    wide = merge.shape[0]
    heads = wide // HD
    for i in range(images):
        span = slice(i * rows, (i + 1) * rows)
        for h in range(heads):
            spans = [slice(s * wide + h * HD, s * wide + (h + 1) * HD) for s in range(3)]
            query, keys, values = (projected[span, s] for s in spans)
            head_grad = attended_grad[span, h * HD : (h + 1) * HD]
            prob_low = probs[i * heads + h]
            prob = prob_low.astype(F32)
            prob_grad = dot_nt(head_grad, values)
            score_grad = prob * (prob_grad - jnp.sum(prob_grad * prob, axis=-1, keepdims=True))
            score_grad = score_grad.astype(LOW)
            pulled[span, spans[0]] = (dot(score_grad, keys) * SCALE).astype(LOW)
            pulled[span, spans[1]] = (dot_tn(score_grad, query) * SCALE).astype(LOW)
            pulled[span, spans[2]] = dot_tn(prob_low, head_grad).astype(LOW)
    ship(pulled, pulled_kept)
    first[...] = dot_nt(pulled[...], project[...]).astype(LOW)


def attend_grad_body(size, offsets, scalars, normed, attended, merged, pulled, *refs):
    *refs, project, merge = refs
    small_rows = refs.pop() if len(refs) > len(offsets) + 1 else None
    *given, bias_out = refs
    given, pieces = given[: -len(offsets)], given[-len(offsets) :]
    wide = merge.shape[0]
    project[...] = dot_tn(normed[...], pulled[...]).astype(LOW)
    merge[...] = dot_tn(attended[...], merged[...])
    bias = [column_sum(pulled[:, k * wide : (k + 1) * wide].astype(F32)) for k in (0, 2)]
    bias_out[...] = jnp.concatenate(bias, axis=1)
    if small_rows is not None:
        owners = small_rows.shape[1]
        depth = (len(given) + 1) // 5
        for l in range(depth):
            one, two, up, down = given[4 * l : 4 * l + 4]
            pair = bias if l == 0 else [
                given[4 * depth + l - 1][:, k * wide : (k + 1) * wide] for k in range(2)
            ]
            norms = [one[0:1, :], two[0:1, :], one[1:2, :], two[1:2, :], two[2:3, :]]
            share = norms[0].shape[1] // owners
            first = sum(
                owned(v, owners, wide, k * share) for k, v in enumerate(norms)
            ) + sum(
                owned(v, owners, wide, 5 * share + k * share // 2) for k, v in enumerate(pair)
            )
            small_rows[3 * l] = first
            small_rows[3 * l + 1] = owned(down[...], owners, wide, scalars[1] * share)
            small_rows[3 * l + 2] = owned(up[...], owners, wide, scalars[1] * 2 * share)
    for ref, offs in zip(pieces, offsets):
        part = size // 2
        for r, off in enumerate(offs):
            i = scalars[0] ^ off
            at = pl.ds(pl.multiple_of(i * size, min(size, 16)), size)
            for s in range(3):
                ref[r, s * size : (s + 1) * size, :] = project[at, s * wide : (s + 1) * wide]
            rows = merge[pl.ds(pl.multiple_of(i * part, min(part, 8)), part), :]
            sides = jnp.concatenate([rows[:, :wide], rows[:, wide:]], axis=0)
            ref[r, 3 * size : 4 * size, :] = sides.astype(LOW)
            if small_rows is not None:
                lines = [small_rows[k, pl.ds(i, 1), :] for k in range(small_rows.shape[0])]
                lines.append(jnp.zeros((16 - len(lines), wide), F32))
                ref[r, 4 * size :, :] = jnp.concatenate(lines, axis=0).astype(LOW)


def stream_pull(part, got, stream, middle_grad, vectors, small):
    first = part[...].astype(F32) + got[...].astype(F32)
    unit, inverse = unit_of(stream[...])
    small[0:1, :] = column_sum(first * unit)
    small[1:2, :] = column_sum(first)
    return middle_grad[...] + norm_pull(first, unit, inverse, vectors[0:1, : first.shape[1]])


def stream_pull_body(
    scalars, part, got, stream, middle_grad, vectors, target, gate, grad, small, *sends
):
    value = stream_pull(part, got, stream, middle_grad, vectors, small)
    grad[...] = value
    low = value.astype(LOW)
    for r, send in enumerate(sends):
        send[...] = dot(slot_marks(scalars, r, target[...], gate[...]), low).astype(LOW)


def last_pull_body(scalars, part, got, stream, middle_grad, vectors, out, small):
    value = stream_pull(part, got, stream, middle_grad, vectors, small)
    rows = value.shape[0] // out.shape[0]
    for i in range(out.shape[0]):
        out[i] = value[i * rows : i * rows + out.shape[1]]


def pack_body(count, ship, scalars, *refs):
    given, packs, held = refs[:8], refs[8 : 8 + count], refs[8 + count :]
    ship.wait([ship(a, b) for a, b in zip(given, held)])
    attend, merge, *smalls = held
    depth, _, size, wide = attend.shape
    for l, pack in enumerate(packs):
        for k in range(3):
            pack[0, k * size : (k + 1) * size, :] = attend[l, k]
        rows = merge[l].astype(F32)
        sides = jnp.concatenate([rows[:, :wide], rows[:, wide:]], axis=0)
        pack[0, 3 * size : 4 * size, :] = sides.astype(LOW)

    def row(*parts):
        total, at = jnp.zeros((1, wide), F32), 0
        for part in parts:
            lane = lax.broadcasted_iota(jnp.int32, (part.shape[1], wide), 1)
            home = lax.broadcasted_iota(jnp.int32, lane.shape, 0) + at
            total = total + dot(part, jnp.where(lane == home, 1.0, 0.0).astype(LOW))
            at += part.shape[1]
        return total

    gain, shift, merge_bias, attend_bias, up_bias, down_bias = smalls
    rows = []
    for l in range(depth):
        norms = [v[l, k : k + 1, :] for v in (gain, shift) for k in range(2)]
        rows.append(
            row(*norms, merge_bias[l : l + 1, :], *(attend_bias[l, k : k + 1, :] for k in range(2)))
        )
        rows.append(row(*(down_bias[l, e : e + 1, :] for e in range(E))))
        rows.append(row(*(up_bias[l, e : e + 1, :] for e in range(E))))
    rows.append(jnp.zeros((16 - 3 * depth, wide), F32))
    packs[0][0, 4 * size :, :] = jnp.concatenate(rows, axis=0).astype(LOW)


def deal_body(layer, ship, scalars, up, down, *chunks):
    size, wide = up.shape[2], down.shape[3]
    for r, chunk in enumerate(chunks):
        e = scalars[1] ^ r
        ship(up.at[layer, e], chunk.at[pl.ds(0, size), :])
        for side in range(2):
            ship(
                down.at[layer, e, pl.ds(side * size, size), :],
                chunk.at[pl.ds(size, size), pl.ds(side * wide, wide)],
            )


def prepare_body(images, scalars, routes, gates, columns, rows_out, gate_rows):
    depth, total, _ = routes.shape
    live = live_rows(scalars, total, images)
    square = lax.broadcasted_iota(jnp.int32, (total, total), 0), lax.broadcasted_iota(
        jnp.int32, (total, total), 1
    )
    earlier = jnp.where(square[0] > square[1], 1.0, 0.0).astype(LOW)
    same = jnp.where(square[0] == square[1], 1.0, 0.0).astype(LOW)
    lane = lax.broadcasted_iota(jnp.int32, (total, 128), 1)
    for l in range(depth):
        picks = [routes[l, :, k : k + 1] for k in range(2)]
        chosen = ((lane == picks[0]) | (lane == picks[1])) & live
        taken = dot(earlier, jnp.where(chosen, 1.0, 0.0).astype(LOW))
        mixed = jnp.zeros((total, 128), F32)
        for k, pick in enumerate(picks):
            slot = jnp.sum(jnp.where(lane == pick, taken, 0.0), axis=1, keepdims=True)
            target = jnp.where(live & (pick >= 0), pick * SLOTS + slot.astype(jnp.int32), -1)
            columns[l, :, k : k + 1] = target
            high = (target + 1) >> 5
            mixed = jnp.where(lane == 3 * k, high.astype(F32), mixed)
            mixed = jnp.where(lane == 3 * k + 1, (target + 1 - (high << 5)).astype(F32), mixed)
            mixed = jnp.where(lane == 3 * k + 2, gates[l, :, k : k + 1], mixed)
        turned = dot_tn(mixed.astype(LOW), same)
        for k in range(2):
            high, low, gate = (turned[3 * k + j : 3 * k + j + 1] for j in range(3))
            rows_out[l, k : k + 1, :] = (high * 32.0 + low).astype(jnp.int32) - 1
            gate_rows[l, k : k + 1, :] = gate


def finish_body(depth, scalars, *refs):
    blocks, attends, outs = refs[: E * depth], refs[E * depth : (E + 1) * depth], refs[-10:]
    gain, shift, attend, attend_bias, merge, merge_bias, up, up_bias, down, down_bias = outs
    size, wide = up.shape[2], down.shape[3]
    part, share = size // 2, gain.shape[2]
    small = attends[0][0, 4 * size :, :].astype(F32)
    for l in range(depth):
        for r in range(E):
            e = scalars[1] ^ r
            value = blocks[l * E + r][...].astype(F32)
            up[l, e] = value[:size]
            both = value[size:]
            down[l, e] = jnp.concatenate([both[:, :wide], both[:, wide:]], axis=0)
        for k in range(3):
            attend[l, k] = attends[l][0, k * size : (k + 1) * size, :].astype(F32)
        sides = attends[l][0, 3 * size : 4 * size, :].astype(F32)
        merge[l] = jnp.concatenate([sides[:part], sides[part:]], axis=1)
        first, second, third = (small[3 * l + k : 3 * l + k + 1, :] for k in range(3))
        for k in range(2):
            gain[l, k : k + 1, :] = first[:, k * share : (k + 1) * share]
            shift[l, k : k + 1, :] = first[:, (2 + k) * share : (3 + k) * share]
            at = 5 * share + k * share // 2
            attend_bias[l, k : k + 1, :] = first[:, at : at + share // 2]
        merge_bias[l : l + 1, :] = first[:, 4 * share : 5 * share]
        for e in range(E):
            down_bias[l, e : e + 1, :] = second[:, e * share : (e + 1) * share]
            up_bias[l, e : e + 1, :] = third[:, 2 * e * share : 2 * (e + 1) * share]


class Place:
    def __init__(self, count, rows, live):
        self.count = count
        self.me = lax.axis_index("dp").astype(jnp.int32)
        core = lax.axis_index("tensor").astype(jnp.int32)
        self.expert = (self.me >> 2) & 3
        self.near = self.expert ^ jnp.arange(E, dtype=jnp.int32)
        powers = [1 << k for k in range(count.bit_length() - 1)]
        self.powers, self.beyond = powers, [b for b in reversed(powers) if b > 8]
        self.aligned = rows % 16 == 0
        where = self.me if self.aligned else jnp.zeros((), jnp.int32)
        self.scalars = jnp.stack([where, self.expert, core, live, self.me])
        far = doubled([0], self.beyond)
        self.parts = [[f ^ l ^ p for f in far for l in LINE] for p in PLANE]
        self.all = [o for offs in self.parts for o in offs]
        blocks = [f ^ l for f in far for l in LINE]
        middle = len(blocks) // 2
        rounds = [(0, blocks), (1, blocks), (2, blocks), (3, blocks[:middle]), (3, blocks[middle:])]
        self.arrivals = [[b ^ p for b in some] for p, some in rounds]
        self.all_arrivals = [o for offs in self.arrivals for o in offs]
        self.fetched = self.arrivals if self.aligned else [[0]]
        self.offsets = self.parts if self.aligned else [[0]]

    def spread(self, value, offsets):
        return [value] + [swap(value, o, self.count) for o in offsets[1:]]

    def near_of(self, value):
        return [swap(value, p, self.count) for p in (1, 2)]

    def gather(self, value, near, anchor=()):
        half = value.shape[0] // 2
        one, two = after(near, anchor)
        return [value, *near, swap(two[:half], 1, self.count), swap(one[half:], 2, self.count)]

    def reduce_onward(self, pieces):
        own, one, two, far = pieces
        half = far.shape[0] // 2
        onward = swap(far[:half], 1, self.count), swap(far[half:], 2, self.count)
        two = jnp.concatenate([add_low(two[:half], onward[0]), two[half:]], axis=0)
        one = jnp.concatenate([one[:half], add_low(one[half:], onward[1])], axis=0)
        return own, one, two

    def reduce(self, own, one, two):
        return add_low(own, swap(one, 1, self.count), swap(two, 2, self.count))

    def deal(self, chunks):
        return [chunks[0]] + [swap(chunks[r], LINE[r], self.count) for r in range(1, E)]

    def exchange(self, chunks, hold=()):
        return self.crossed(self.deal(chunks), hold)

    def crossed(self, own, hold=()):
        return own + [cross(c) for c in (after(own, hold) if hold else own)]

    def doubled(self, value):
        for bit in self.beyond:
            value = jnp.concatenate([value, swap(value, bit, self.count)], axis=0)
        return value

    def halved(self, value):
        for bit in reversed(self.beyond):
            half = value.shape[0] // 2
            value = add_low(value[:half], swap(value[half:], bit, self.count))
        return value


def pack_small(gain, shift, merge, attend, up, down):
    depth, _, share = gain.shape
    spare = jnp.zeros((depth, 2 * share), LOW)
    first = [gain, shift, merge, attend, spare]
    first = jnp.concatenate([p.reshape(depth, -1) for p in first], axis=1)
    second = jnp.pad(down.reshape(depth, -1), ((0, 0), (0, 4 * share)))
    rows = jnp.stack([first, second, up.reshape(depth, -1)], axis=1).reshape(3 * depth, -1)
    return jnp.pad(rows, ((0, -(3 * depth) % 16), (0, 0)))[None]


def pack_attend(attend, merge):
    count, kinds, depth, wide = attend.shape
    rows = attend.reshape(count, 3 * depth, wide)
    return jnp.concatenate([rows, merge[:, :, :wide], merge[:, :, wide:]], axis=1)


def unpack_attend(pack):
    count, rows, wide = pack.shape
    depth = rows // 4
    attend = pack[:, : 3 * depth].reshape(count, 3, depth, wide)
    sides = pack[:, 3 * depth :]
    return attend, jnp.concatenate([sides[:, : depth // 2], sides[:, depth // 2 :]], axis=2)


def whole_attend(pack):
    attend, merge = unpack_attend(pack)
    attend = jnp.swapaxes(attend, 0, 1)
    attend = attend.reshape(3, -1, attend.shape[-1])
    return pack_attend(attend[None], merge.reshape(1, -1, merge.shape[-1]))


def split_attend(pack, count):
    attend, merge = unpack_attend(pack)
    attend = jnp.swapaxes(attend.reshape(3, count, -1, attend.shape[-1]), 0, 1)
    return pack_attend(attend, merge.reshape(count, -1, merge.shape[-1]))


def fetch_column(place, value):
    blocks = place.spread(place.doubled(value), LINE)
    value = jnp.stack(blocks, axis=1)
    return value.reshape((-1,) + value.shape[2:])


def attend_pieces_of(place, pieces):
    if place.aligned:
        return pieces
    return [whole_attend(ordered(jnp.concatenate(pieces), place.all_arrivals, place.me))]


def chunks_of(place, layer, up_weight, down_weight):
    depth, hidden = up_weight.shape[2:]
    if place.aligned:
        return call(
            functools.partial(deal_body, layer),
            [((2 * depth, hidden), LOW)] * E,
            place.scalars,
            up_weight,
            down_weight,
            stored=True,
        )
    sent = []
    for r in range(E):
        one = lax.dynamic_index_in_dim(up_weight[layer], place.near[r], 0, False)
        two = lax.dynamic_index_in_dim(down_weight[layer], place.near[r], 0, False)
        two = jnp.concatenate([two[:depth], two[depth:]], axis=1)
        sent.append(jnp.concatenate([one, two], axis=0))
    return sent


def fetch_base(place, chunks):
    return place.doubled(jnp.stack(place.deal(chunks)))


def expert_pieces_of(place, pieces):
    if place.aligned:
        return pieces
    pack = ordered(jnp.concatenate(pieces), place.all_arrivals, place.me)
    depth, wide = pack.shape[1] // 2, pack.shape[2] // 2
    up, down = pack[:, :depth], pack[:, depth:]
    down = jnp.concatenate([down[..., :wide], down[..., wide:]], axis=1).reshape(2, -1, wide)
    down = jnp.concatenate([down[0], down[1]], axis=1)
    return [jnp.concatenate([up.reshape(-1, up.shape[-1]), down])[None]]


def add_low(*terms):
    return sum(t.astype(F32) for t in terms).astype(LOW)


def spread_expert(place, pieces):
    if place.aligned:
        return pieces
    pack = pieces[0][0]
    depth, wide = pack.shape[0] // 2, pack.shape[1] // 2
    up = pack[:depth].reshape(place.count, -1, 2 * wide)
    down = jnp.concatenate([pack[depth:, :wide], pack[depth:, wide:]], axis=0)
    down = down.reshape(place.count, 2, -1, wide)
    down = jnp.concatenate([down[:, 0], down[:, 1]], axis=-1)
    value = relative(jnp.concatenate([up, down], axis=1), place.all, place.me)
    return list(value.reshape((len(PLANE), -1) + value.shape[1:]))


def finish_expert(place, blocks):
    pack = jnp.take(jnp.stack(blocks), place.near, axis=0, mode="clip").astype(F32)
    depth, wide = pack.shape[1] // 2, pack.shape[2] // 2
    low = pack[:, depth:]
    return pack[:, :depth], jnp.concatenate([low[..., :wide], low[..., wide:]], axis=1)


def spread_plane(place, full):
    value = relative(split_attend(full, place.count), place.all, place.me)
    return list(value.reshape((len(PLANE), -1) + value.shape[1:]))


def fold_column(place, value):
    value = place.halved(value)
    got = [swap(value[r : r + 1], LINE[r], place.count) for r in range(1, len(LINE))]
    return add_low(value[:1], *got)


def finish_attend(value):
    attend, merge = unpack_attend(value)
    return attend[0].astype(F32), merge[0].astype(F32)


def on_device(
    count,
    inputs,
    image_count,
    routes,
    gates,
    norm_gain,
    norm_shift,
    attend_weight,
    attend_bias,
    merge_weight,
    merge_bias,
    up_weight,
    up_bias,
    down_weight,
    down_bias,
    cotangent,
):
    images, length, width = inputs.shape
    depth = routes.shape[0]
    wide = attend_weight.shape[-1]
    hidden = up_weight.shape[-1]
    heads = wide // HD
    place = Place(count, up_weight.shape[2], image_count[0])
    scalars = place.scalars
    rows = -(-length // 16) * 16
    total = images * rows
    half = E * HALF
    size = width // count if place.aligned else width

    def padded(value, fill=0):
        spare = [(0, 0)] * value.ndim
        spare[-2] = (0, rows - length)
        value = jnp.pad(value, spare, constant_values=fill)
        return value.reshape(value.shape[:-3] + (total, value.shape[-1]))

    chunk = ((HALF, width), LOW)
    wide_rows = ((total, width), F32)
    low_rows = ((total, width), LOW)
    wide_half, low_slots = ((half, width), F32), ((2 * half, width), LOW)
    low_half = ((half, width), LOW)
    low_hidden = ((2 * half, hidden), LOW)
    low_project = ((total, 3 * wide), LOW)
    attend_scratch = [((width, 3 * wide), LOW), ((wide, width), F32)]
    expert_scratch = [((width, hidden), LOW), ((hidden, width), LOW)]

    smalls = (norm_gain, norm_shift, merge_bias, attend_bias, up_bias, down_bias)
    small = []
    if place.aligned:
        given = (attend_weight, merge_weight, *smalls)
        sizes = [4 * size + (16 if l == 0 else 0) for l in range(depth)]
        packs = call(
            functools.partial(pack_body, depth),
            [((1, n, wide), LOW) for n in sizes],
            scalars,
            *given,
            scratch=[(g.shape, LOW) for g in given],
            stored=True,
        )
    else:
        packs = [pack_attend(attend_weight[l][None], merge_weight[l][None]) for l in range(depth)]
        small = place.spread(fetch_column(place, pack_small(*smalls)), PLANE)
        small = [ordered(jnp.concatenate(small), place.all, place.me)]
    column = fetch_column(place, packs[0])
    chunks = chunks_of(place, 0, up_weight, down_weight)
    base = fetch_base(place, after(chunks, column))
    near = place.near_of(column)
    attend_pieces = attend_pieces_of(place, place.gather(column, near))
    target, target_rows, gate_rows = call(
        functools.partial(prepare_body, images),
        [((depth, total, 2), jnp.int32)]
        + [((depth, 2, total), jnp.int32), ((depth, 2, total), F32)],
        scalars,
        *after((padded(routes, -1), padded(gates)), column),
    )
    gate = padded(gates)
    stream = padded(after(inputs, column))
    states = []
    back, first_own = None, ()
    for l in range(depth):
        more = l + 1 < depth
        base = after(base, attend_pieces)
        near = place.near_of(base)
        kinds = [low_rows, low_project, ((images * heads, rows, rows), LOW), ((total, wide), LOW)]
        body = functools.partial(
            attend_body, length, images, size, place.fetched, l > 0, not place.aligned
        )
        if l == 0:
            table = [((count, 16, wide), LOW)] if place.aligned else []
            part, vectors, *keeps = call(
                body,
                [low_rows, ((depth, 8, hidden), F32)],
                scalars,
                stream,
                *small,
                *attend_pieces,
                saved=kinds,
                scratch=kinds + attend_scratch + table,
                before=(base,),
                us=LONG,
            )
            stream_kept = stream
        else:
            stream, part, stream_kept, *keeps = call(
                body,
                [wide_rows, low_rows],
                scalars,
                middle,
                *back,
                target[l - 1],
                gate[l - 1],
                vectors[l],
                *attend_pieces,
                saved=[wide_rows] + kinds,
                scratch=kinds + attend_scratch,
                us=LONG,
            )
        normed, projected, probs, attended = keeps
        if more:
            column = fetch_column(place, after(packs[l + 1], base))
        middle, *sends, middle_kept = call(
            middle_body,
            [wide_rows] + [chunk] * E,
            scalars,
            stream,
            part,
            cross(part),
            vectors[l],
            target_rows[l],
            saved=[wide_rows],
            before=(column,) if more else (),
        )
        expert_pieces = expert_pieces_of(place, place.gather(base, near, sends))
        own = place.deal(sends)
        taken = place.crossed(own, (expert_pieces, first_own))
        kept = attend_pieces
        if more:
            chunks = chunks_of(place, l + 1, up_weight, down_weight)
            base = fetch_base(place, after(chunks, own))
            near = place.near_of(after(column, expert_pieces))
        *others, result, active, slope, taken_rows = call(
            functools.partial(expert_body, place.fetched, not more),
            [chunk] * E if more else [],
            scalars,
            *taken,
            vectors[l],
            *expert_pieces,
            saved=([] if more else [low_half]) + [wide_half, low_hidden, low_hidden, low_slots],
            scratch=[wide_half, low_hidden, low_hidden, low_slots]
            + expert_scratch
            + ([] if more else [low_half]),
            us=LONG,
        )
        states.append(
            (stream_kept, middle_kept, normed, projected, probs, attended, taken_rows, active, slope)
            + (kept, expert_pieces)
        )
        if more:
            sends = call(
                total_body, [chunk] * E, scalars, result, *map(cross, others), vectors[l]
            )
            attend_pieces = attend_pieces_of(place, place.gather(column, near, sends))
            back = place.exchange(sends, (attend_pieces, base))
            if l + 2 == depth:
                grad, *first_sends = call(
                    functools.partial(first_grad_body, images),
                    [wide_rows] + [chunk] * E,
                    scalars,
                    padded(after(cotangent, sends)),
                    target_rows[-1],
                    gate_rows[-1],
                )
                first_own = place.deal(after(first_sends, back[:E]))

    slot_grad = place.crossed(first_own)
    last, last_others = result, others
    blocks = [None] * depth
    attend_grads, smalls, biases = [None] * depth, [None] * depth, [None] * depth
    waiting, before_expert, before_total, ends = [], (), (), ()
    for l in reversed(range(depth)):
        stream, middle, normed, projected, probs, attended, taken, active, slope = states[l][:9]
        attend_pieces, expert_pieces = states[l][9:]
        *others, up_b, down_b, result, pulled, slot_rows = call(
            functools.partial(expert_pull_body, place.fetched),
            [chunk] * E + [((1, hidden), F32), ((1, width), F32)],
            scalars,
            *slot_grad,
            slope,
            *expert_pieces,
            saved=[wide_half, low_hidden, low_slots],
            scratch=[wide_half, low_hidden, low_slots] + expert_scratch,
            before=before_expert,
            us=LONG,
        )
        sends = call(
            total_body,
            [chunk] * E,
            scalars,
            result,
            *map(cross, others),
            before=before_total,
        )
        own = place.deal(sends)
        before_attend = ()
        if waiting:
            attend_sum = place.reduce(*after(before_total, sends))
            before_attend = (attend_sum,)
            waiting.append(attend_sum)
        back = place.crossed(own)
        active, pulled_late = after((active, pulled), own[1])
        pieces = call(
            functools.partial(expert_grad_body, place.offsets),
            [((len(o), 2 * size, hidden), LOW) for o in place.offsets],
            scalars,
            slot_rows,
            active,
            taken,
            pulled_late,
            scratch=expert_scratch,
            us=7,
        )
        expert_onward = place.reduce_onward(spread_expert(place, pieces))
        if l + 1 == depth:
            last, last_others = after((last, last_others), own)
            ends = call(
                total_body, [chunk] * E, scalars, last, *map(cross, last_others), vectors[l]
            )
            ends = place.deal(ends)
        if waiting:
            done, value, total_sum = waiting
            blocks[done] = place.deal(list(place.halved(after(value, own))))
            attend_grads[done] = fold_column(place, after(total_sum, own))
            waiting = []
        pull_kinds = [wide_rows, low_rows, low_project]
        first, small_two, middle_grad, merged, pulled = call(
            functools.partial(attend_pull_body, images, size, place.fetched),
            [low_rows, ((3, width), F32)],
            scalars,
            *back,
            target[l],
            middle,
            grad,
            vectors[l],
            probs,
            projected,
            *attend_pieces,
            saved=pull_kinds,
            scratch=pull_kinds + attend_scratch,
            before=before_attend,
            us=LONG,
        )
        got = cross(first)
        if l > 0:
            grad, small_one, *sends = call(
                stream_pull_body,
                [wide_rows, ((2, width), F32)] + [chunk] * E,
                scalars,
                first,
                got,
                stream,
                middle_grad,
                vectors[l],
                target_rows[l - 1],
                gate_rows[l - 1],
                before=expert_onward,
            )
            own = place.deal(sends)
            slot_grad = place.crossed(own, ends)
            pulled_late = after(pulled, own[3])
        else:
            input_grad, small_one = call(
                last_pull_body,
                [(inputs.shape, F32), ((2, width), F32)],
                scalars,
                first,
                got,
                stream,
                middle_grad,
                vectors[l],
                before=expert_onward,
            )
            pulled_late = pulled
        smalls[l] = (small_one, small_two, up_b, down_b)
        extra = []
        joint = place.aligned and l == 0
        if joint:
            extra = [v for some in smalls for v in some] + biases[1:]
        height = 4 * size + (16 if joint else 0)
        *pieces, biases[l] = call(
            functools.partial(attend_grad_body, size, place.offsets),
            [((len(o), height, wide), LOW) for o in place.offsets] + [((1, width), F32)],
            scalars,
            normed,
            attended,
            merged,
            pulled_late,
            *extra,
            scratch=([((3 * depth, count, wide), F32)] if joint else []) + attend_scratch,
            us=4,
        )
        if not place.aligned:
            pieces = spread_plane(place, pieces[0])
        before_total = place.reduce_onward(pieces)
        expert_sum = place.reduce(*expert_onward)
        before_expert = (expert_sum,)
        waiting = [l, expert_sum]
    blocks[0] = place.deal(list(place.halved(expert_sum)))
    attend_grads[0] = fold_column(place, place.reduce(*before_total))
    ends = after(ends, pieces)
    (output,) = call(
        output_body,
        [(inputs.shape, F32)],
        scalars,
        states[-1][1],
        *ends,
        *map(cross, ends),
        target[-1],
        gate[-1],
    )
    if place.aligned:
        grads = (norm_gain, norm_shift, attend_weight, attend_bias, merge_weight, merge_bias)
        grads += (up_weight, up_bias, down_weight, down_bias)
        return output, input_grad, *call(
            functools.partial(finish_body, depth),
            [(g.shape, F32) for g in grads],
            scalars,
            *[b for layer in blocks for b in layer],
            *attend_grads,
        )

    tables = []
    at_expert = jnp.arange(E, dtype=jnp.int32)[:, None, None] == place.expert
    for (small_one, small_two, up_b, down_b), bias in zip(smalls, biases):
        expert_rows = jnp.concatenate([up_b.reshape(-1, width), down_b], axis=0)
        expert_rows = jnp.where(at_expert, expert_rows[None], 0.0).reshape(-1, width)
        tables.append(jnp.concatenate([small_one, small_two, bias, expert_rows], axis=0))
    small = jnp.stack(tables)
    for bit in place.beyond:
        small = small + swap(small, bit, count)
    for offsets in (PLANE, LINE):
        terms = place.spread(small, offsets)
        small = (terms[0] + terms[1]) + (terms[2] + terms[3])

    def mine(value, size):
        return lax.dynamic_slice_in_dim(value, place.me * size, size, value.ndim - 1)

    share = norm_gain.shape[-1]
    gain_grad = jnp.stack([small[:, 0], small[:, 2]], axis=1)
    shift_grad = jnp.stack([small[:, 1], small[:, 3]], axis=1)
    attend_b = small[:, 5].reshape(depth, 2, wide)
    expert_rows = small[:, 6:].reshape(depth, E, -1, width)
    up_b = expert_rows[:, :, :-1].reshape(depth, E, hidden)
    finished = [finish_expert(place, b) + finish_attend(a) for b, a in zip(blocks, attend_grads)]
    up_grad, down_grad, attend_grad, merge_grad = (
        jnp.stack([f[k] for f in finished]) for k in range(4)
    )
    return (
        output,
        input_grad,
        mine(gain_grad, share),
        mine(shift_grad, share),
        attend_grad,
        mine(attend_b, attend_bias.shape[-1]),
        merge_grad,
        mine(small[:, 4], share),
        up_grad,
        mine(up_b, up_bias.shape[-1]),
        down_grad,
        mine(expert_rows[:, :, -1], share),
    )


def solution(mesh):
    placed = (
        P("dp", None, None),
        P("dp"),
        P(None, "dp", None, None),
        P(None, "dp", None, None),
        P(None, None, "dp"),
        P(None, None, "dp"),
        P(None, None, "dp", "tensor"),
        P(None, None, ("tensor", "dp")),
        P(None, ("tensor", "dp"), None),
        P(None, "dp"),
        P(None, None, "dp", "tensor"),
        P(None, None, ("tensor", "dp")),
        P(None, None, ("tensor", "dp"), None),
        P(None, None, "dp"),
        P("dp", None, None),
    )
    return jax.shard_map(
        functools.partial(on_device, mesh.shape["dp"]),
        mesh=mesh,
        in_specs=placed,
        out_specs=(
            P("dp", None, None),
            P("dp", None, None),
            P(None, None, "dp"),
            P(None, None, "dp"),
            P(None, None, "dp", "tensor"),
            P(None, None, ("tensor", "dp")),
            P(None, ("tensor", "dp"), None),
            P(None, "dp"),
            P(None, None, "dp", "tensor"),
            P(None, None, ("tensor", "dp")),
            P(None, None, ("tensor", "dp"), None),
            P(None, None, "dp"),
        ),
        check_vma=False,
    )
```

```python
import functools

import jax
import jax.numpy as jnp
from jax import lax
from jax.experimental import pallas as pl
from jax.experimental.pallas import tpu as pltpu
from jax.sharding import PartitionSpec as P

HD = 64
E = 4
SLOTS = 256
HALF = SLOTS // 2
PLANE = (0, 1, 2, 3)
LINE = (0, 4, 8, 12)
ROWS = 256
STEP = 512
LONG = 60
VMEM = 32 * 2**20
LOW = jnp.bfloat16
F32 = jnp.float32
SCALE = HD ** (-0.5)


def dot(left, right):
    return jnp.dot(left, right, preferred_element_type=F32)


def dot_nt(left, right):
    return lax.dot_general(left, right, (((1,), (1,)), ((), ())), preferred_element_type=F32)


def dot_tn(left, right):
    return lax.dot_general(left, right, (((0,), (0,)), ((), ())), preferred_element_type=F32)


def swap(value, bit, count):
    return lax.ppermute(value, "dp", [(i, i ^ bit) for i in range(count)])


def after(value, *anchors):
    return lax.optimization_barrier((value, anchors))[0]


def cross(value):
    return lax.ppermute(value, "tensor", [(0, 1), (1, 0)])


def doubled(offsets, bits):
    for bit in bits:
        offsets = offsets + [o ^ bit for o in offsets]
    return offsets


def ordered(value, offsets, me):
    where = jnp.asarray([offsets.index(i) for i in range(len(offsets))], jnp.int32)
    index = where[jnp.arange(len(offsets), dtype=jnp.int32) ^ me]
    return jnp.take(value, index, axis=0, mode="clip")


def relative(value, offsets, me):
    return jnp.take(value, jnp.asarray(offsets, jnp.int32) ^ me, axis=0, mode="clip")


def call(kernel, outs, scalars, *args, saved=(), scratch=(), before=(), stored=(), us=0):
    memory = pl.BlockSpec(memory_space=pltpu.VMEM)

    def body(*refs):
        ships = saved or stored
        sems = refs[-1] if ships else None
        started, settled = [], []

        def ship(source, target):
            copy = pltpu.make_async_copy(source, target, sems.at[len(started)])
            copy.start()
            started.append(copy)
            return copy

        def wait(copies):
            for copy in copies:
                copy.wait()
            settled.extend(copies)

        ship.wait = wait
        if ships:
            kernel(ship, *refs[:-1])
        else:
            kernel(*refs)
        for copy in started:
            if not any(copy is done for done in settled):
                copy.wait()

    if before:
        scalars = after(scalars, *before)
    args = [
        pltpu.with_memory_space_constraint(a, pltpu.HBM) if k in stored else a
        for k, a in enumerate(args)
    ]
    return pl.pallas_call(
        body,
        out_shape=[jax.ShapeDtypeStruct(shape, kind) for shape, kind in outs]
        + [pltpu.HBM(shape, kind) for shape, kind in saved],
        in_specs=[pl.BlockSpec(memory_space=pltpu.SMEM)]
        + [pl.BlockSpec(memory_space=pltpu.HBM) if k in stored else memory for k in range(len(args))],
        out_specs=[memory] * len(outs) + [pl.BlockSpec(memory_space=pltpu.HBM)] * len(saved),
        scratch_shapes=[pltpu.VMEM(shape, kind) for shape, kind in scratch]
        + ([pltpu.SemaphoreType.DMA((24,))] if saved or stored else []),
        compiler_params=pltpu.CompilerParams(vmem_limit_bytes=VMEM),
        cost_estimate=pl.CostEstimate(
            flops=us * 10**9, transcendentals=0, bytes_accessed=us * 10**3
        ),
    )(scalars, *args)


def unit_of(stream):
    center = stream - jnp.mean(stream, axis=-1, keepdims=True)
    inverse = lax.rsqrt(jnp.mean(center * center, axis=-1, keepdims=True) + 1e-06)
    return center * inverse, inverse


def norm_pull(grad, unit, inverse, gain):
    scaled = grad * gain
    return inverse * (
        scaled
        - jnp.mean(scaled, axis=-1, keepdims=True)
        - unit * jnp.mean(scaled * unit, axis=-1, keepdims=True)
    )


def column_sum(value):
    return jnp.sum(value, axis=0, keepdims=True)


def place_attend(where, size, pieces, offsets, project, merge):
    for ref, offs in zip(pieces, offsets):
        wide, part = ref.shape[2], size // 2
        for r, off in enumerate(offs):
            i = where ^ off
            at = pl.ds(pl.multiple_of(i * size, min(size, 16)), size)
            for s in range(3):
                project[at, s * wide : (s + 1) * wide] = ref[r, s * size : (s + 1) * size, :]
            sides = ref[r, 3 * size : 4 * size, :].astype(F32)
            at = pl.ds(pl.multiple_of(i * part, min(part, 8)), part)
            merge[at, :wide] = sides[:part]
            merge[at, wide:] = sides[part:]


def place_expert(where, pieces, offsets, up, down):
    for ref, offs in zip(pieces, offsets):
        size, wide = ref.shape[1] // 2, ref.shape[2] // 2
        for r, off in enumerate(offs):
            i = where ^ off
            up[pl.ds(pl.multiple_of(i * size, min(size, 16)), size), :] = ref[r, :size, :]
            at = pl.multiple_of(i * 2 * size, min(size, 16))
            down[pl.ds(at, size), :] = ref[r, size:, :wide]
            down[pl.ds(at + size, size), :] = ref[r, size:, wide:]


def rows_of(chunks):
    return jnp.concatenate([c[...] for c in chunks], axis=0)


def slot_marks(scalars, r, target, gate):
    base = (scalars[1] ^ r) * SLOTS + scalars[2] * HALF
    slots = lax.broadcasted_iota(jnp.int32, (HALF, target.shape[1]), 0) + base
    first, second = slots == target[0:1], slots == target[1:2]
    if gate is None:
        return jnp.where(first | second, 1.0, 0.0).astype(LOW)
    weight = jnp.where(first, gate[0:1], 0.0) + jnp.where(second, gate[1:2], 0.0)
    return weight.astype(LOW)


def row_marks(slots, target, gate):
    first, second = target[:, 0:1] == slots, target[:, 1:2] == slots
    if gate is None:
        return jnp.where(first | second, 1.0, 0.0).astype(LOW)
    weight = jnp.where(first, gate[:, 0:1], 0.0) + jnp.where(second, gate[:, 1:2], 0.0)
    return weight.astype(LOW)


def combined(scalars, target, gate, chunks):
    marks = []
    for h in range(2):
        for r in range(E):
            base = (scalars[1] ^ r) * SLOTS + (scalars[2] ^ h) * HALF
            slots = lax.broadcasted_iota(jnp.int32, (1, HALF), 1) + base
            marks.append(row_marks(slots, target, gate))
    return dot(jnp.concatenate(marks, axis=1), rows_of(chunks))


def owned(vector, owners, wide, at):
    count = vector.shape[1]
    share = count // owners
    lane = lax.broadcasted_iota(jnp.int32, (owners, count), 1)
    start = lax.broadcasted_iota(jnp.int32, (owners, count), 0) * share
    mine = jnp.where((lane >= start) & (lane < start + share), vector, 0.0).astype(LOW)
    lane = lax.broadcasted_iota(jnp.int32, (count, 128), 0)
    turn = jnp.floor((lane.astype(F32) + 0.5) * (1.0 / share)).astype(jnp.int32)
    home = lane - turn * share == lax.broadcasted_iota(jnp.int32, (count, 128), 1)
    packed = dot(mine, jnp.where(home, 1.0, 0.0).astype(LOW)).astype(LOW)
    lane = lax.broadcasted_iota(jnp.int32, (128, wide), 0)
    home = (lane + at == lax.broadcasted_iota(jnp.int32, (128, wide), 1)) & (lane < share)
    return dot(packed, jnp.where(home, 1.0, 0.0).astype(LOW))


def join_vectors(scalars, small, vectors):
    owners = small.shape[0]

    def joined(part):
        wide = part.shape[1]
        lane = lax.broadcasted_iota(jnp.int32, (wide, owners * wide), 1)
        turn = jnp.floor((lane.astype(F32) + 0.5) * (1.0 / wide)).astype(jnp.int32)
        place = lane - turn * wide == lax.broadcasted_iota(jnp.int32, lane.shape, 0)
        spread = dot(part.astype(LOW), jnp.where(place, 1.0, 0.0).astype(LOW))
        start = lax.broadcasted_iota(jnp.int32, spread.shape, 0) * wide
        lane = lax.broadcasted_iota(jnp.int32, spread.shape, 1)
        return column_sum(jnp.where((lane >= start) & (lane < start + wide), spread, 0.0))

    share = small.shape[2] // 8
    half = share // 2
    expert = scalars[1]
    for l in range(vectors.shape[0]):
        first, second, third = (small[:, 3 * l + k, :] for k in range(3))
        parts = [first[:, k * share : (k + 1) * share] for k in range(5)]
        for k, part in enumerate(parts):
            vectors[l, k : k + 1, : owners * share] = joined(part)
        at = 5 * share
        query, values = (joined(first[:, at + k * half : at + (k + 1) * half]) for k in range(2))
        vectors[l, 5:6, : 3 * owners * half] = jnp.concatenate(
            [query, jnp.zeros_like(query), values], axis=1
        )
        up = sum(
            jnp.where(expert == e, third[:, 2 * e * share : 2 * (e + 1) * share], 0.0)
            for e in range(E)
        )
        vectors[l, 6:7, :] = joined(up)
        down = sum(
            jnp.where(expert == e, second[:, e * share : (e + 1) * share], 0.0) for e in range(E)
        )
        vectors[l, 7:8, : owners * share] = joined(down)


def live_rows(scalars, rows, images):
    return lax.broadcasted_iota(jnp.int32, (rows, 1), 0) < scalars[3] * (rows // images)


def attend_body(length, images, size, offsets, from_slots, split, ship, *refs):
    count = len(offsets)
    scalars, refs = refs[0], refs[1:]
    if from_slots:
        middle, *back = refs[: 1 + 2 * E]
        target, gate, vectors = refs[1 + 2 * E : 4 + 2 * E]
        refs = refs[4 + 2 * E :]
    else:
        stream_in, refs = refs[0], refs[1:]
        if split:
            small, refs = refs[0], refs[1:]
    pieces, refs = refs[:count], refs[count:]
    if from_slots:
        stream_out, partial, stream_kept, *refs = refs
    else:
        partial, all_vectors, *refs = refs
        vectors = all_vectors.at[0]
    kept, (normed, projected, probs, attended, project, merge, *rest) = refs[:4], refs[4:]
    place_attend(scalars[0], size, pieces, offsets, project, merge)
    if not from_slots:
        if not split:
            (small,) = rest
            for ref, offs in zip(pieces, offsets):
                for r, off in enumerate(offs):
                    small[scalars[0] ^ off] = ref[r, 4 * size :, :]
        join_vectors(scalars, small[...].astype(F32), all_vectors)
    if from_slots:
        stream = middle[...] + combined(scalars, target[...], gate[...], back)
        stream_out[...] = stream
        ship(stream_out, stream_kept)
    else:
        stream = stream_in[...]
    unit, inverse = unit_of(stream)
    width = stream.shape[1]
    normed[...] = (unit * vectors[0:1, :width] + vectors[2:3, :width]).astype(LOW)
    ship(normed, kept[0])
    bias = vectors[5:6, : project.shape[1]]
    projected[...] = (dot(normed[...], project[...]) + bias).astype(LOW)
    ship(projected, kept[1])
    rows = stream.shape[0] // images
    wide = merge.shape[0]
    heads = wide // HD
    keep = lax.broadcasted_iota(jnp.int32, (rows, rows), 1) < length
    for i in range(images):
        span = slice(i * rows, (i + 1) * rows)
        for h in range(heads):
            query = projected[span, h * HD : (h + 1) * HD]
            keys = projected[span, wide + h * HD : wide + (h + 1) * HD]
            values = projected[span, 2 * wide + h * HD : 2 * wide + (h + 1) * HD]
            scores = jnp.where(keep, dot_nt(query, keys) * SCALE, -1e30)
            raised = jnp.exp(scores - jnp.max(scores, axis=-1, keepdims=True))
            prob = raised / jnp.sum(raised, axis=-1, keepdims=True)
            prob_low = prob.astype(LOW)
            probs[i * heads + h] = prob_low
            attended[span, h * HD : (h + 1) * HD] = dot(prob_low, values).astype(LOW)
        ship(probs.at[pl.ds(i * heads, heads)], kept[2].at[pl.ds(i * heads, heads)])
    ship(attended, kept[3])
    partial[...] = dot(attended[...], merge[...].astype(LOW)).astype(LOW)


def middle_body(ship, scalars, stream, part, got, vectors, target, middle, *refs):
    sends, kept = refs[:E], refs[E]
    width = stream.shape[1]
    gain, shift, bias = (vectors[k : k + 1, :width] for k in (1, 3, 4))
    value = stream[...] + part[...].astype(F32) + got[...].astype(F32) + bias
    middle[...] = value
    ship(middle, kept)
    unit, inverse = unit_of(value)
    normed = (unit * gain + shift).astype(LOW)
    for r, send in enumerate(sends):
        send[...] = dot(slot_marks(scalars, r, target[...], None), normed).astype(LOW)


def expert_body(offsets, last, ship, scalars, *refs):
    count = len(offsets)
    chunks, vectors, refs = refs[: 2 * E], refs[2 * E], refs[2 * E + 1 :]
    pieces, refs = refs[:count], refs[count:]
    if last:
        others_kept, refs = refs[0], refs[1:]
        others, refs = refs[-1], refs[:-1]
    else:
        others, refs = refs[0], refs[1:]
    result_kept, active_kept, slope_kept, rows_kept, result, active, slope, rows, up, down = refs
    place_expert(scalars[0], pieces, offsets, up, down)
    bias = vectors[6:7, :]
    for k in reversed(range(0, 2 * E, 2)):
        at = k * HALF
        span = pl.ds(at, 2 * HALF)
        rows[span, :] = rows_of(chunks[k : k + 2])
        ship(rows.at[span], rows_kept.at[span])
        hidden = dot(rows[span, :], up[...]) + bias
        square = hidden * hidden
        bent = jnp.tanh(0.7978845608028654 * hidden * (1.0 + 0.044715 * square))
        low = 0.5 * (1.0 + bent)
        act = (hidden * low).astype(LOW)
        active[span, :] = act
        slope[span, :] = (
            low
            + hidden
            * (0.5 * 0.7978845608028654)
            * (1.0 - bent * bent)
            * (1.0 + 3 * 0.044715 * square)
        ).astype(LOW)
        ship(active.at[span], active_kept.at[span])
        ship(slope.at[span], slope_kept.at[span])
        out = dot(act, down[...])
        if k < E:
            result[span, :] = out
            ship(result.at[span], result_kept.at[span])
        else:
            span = pl.ds(at - E * HALF, 2 * HALF)
            others[span, :] = out.astype(LOW)
            if last:
                ship(others.at[span], others_kept.at[span])


def total_body(scalars, part, *refs):
    got, sends = refs[:-E], refs[-E:]
    vectors = None
    if got[-1].dtype == F32:
        got, vectors = got[:-1], got[-1]
    for r, send in enumerate(sends):
        span = slice(r * HALF, (r + 1) * HALF)
        value = part[span, :] + got[0][span, :].astype(F32)
        if vectors is not None:
            value = value + vectors[7:8, : value.shape[1]]
        send[...] = value.astype(LOW)


def output_body(scalars, middle, *refs):
    chunks, (target, gate, out) = refs[: 2 * E], refs[2 * E :]
    value = middle[...] + combined(scalars, target[...], gate[...], chunks)
    value = jnp.where(live_rows(scalars, value.shape[0], out.shape[0]), value, 0.0)
    rows = value.shape[0] // out.shape[0]
    for i in range(out.shape[0]):
        out[i] = value[i * rows : i * rows + out.shape[1]]


def first_grad_body(images, scalars, cotangent, target, gate, grad, *sends):
    value = jnp.where(live_rows(scalars, grad.shape[0], images), cotangent[...], 0.0)
    grad[...] = value
    low = value.astype(LOW)
    for r, send in enumerate(sends):
        send[...] = dot(slot_marks(scalars, r, target[...], gate[...]), low).astype(LOW)


def expert_pull_body(offsets, ship, scalars, *refs):
    count = len(offsets)
    chunks, slope, refs = refs[: 2 * E], refs[2 * E], refs[2 * E + 1 :]
    pieces, others, refs = refs[:count], refs[count], refs[count + 1 :]
    up_bias, down_bias, result_kept, hidden_kept, rows_kept, *refs = refs
    result, hidden_grad, rows, slope_here, up, down = refs
    spans = [pl.ds(k * HALF, 2 * HALF) for k in range(0, 2 * E, 2)]
    loads = [ship(slope.at[s], slope_here.at[s]) for s in reversed(spans)][::-1]
    place_expert(scalars[0], pieces, offsets, up, down)
    total = jnp.zeros(up_bias.shape, F32)
    total_down = jnp.zeros(down_bias.shape, F32)
    for k in reversed(range(0, 2 * E, 2)):
        span = pl.ds(k * HALF, 2 * HALF)
        value = rows_of(chunks[k : k + 2])
        rows[span, :] = value
        ship(rows.at[span], rows_kept.at[span])
        total_down = total_down + column_sum(value.astype(F32))
        ship.wait([loads[k // 2]])
        low = (dot_nt(value, down[...]) * slope_here[span, :].astype(F32)).astype(LOW)
        hidden_grad[span, :] = low
        ship(hidden_grad.at[span], hidden_kept.at[span])
        total = total + column_sum(low.astype(F32))
        out = dot_nt(low, up[...])
        if k < E:
            result[span, :] = out
            ship(result.at[span], result_kept.at[span])
        else:
            others[pl.ds((k - E) * HALF, 2 * HALF), :] = out.astype(LOW)
    up_bias[...] = total
    down_bias[...] = total_down


def expert_grad_body(offsets, ship, scalars, *refs):
    given, refs = refs[:4], refs[4:]
    pieces, (up, down, *held) = refs[: len(offsets)], refs[len(offsets) :]
    loads = []
    for a, b in zip(given, held):
        step = a.shape[0] // 4
        spans = [pl.ds(k * step, step) for k in range(4)]
        loads += [ship(a.at[span], b.at[span]) for span in spans]
    slot_rows, active, rows, pulled = held
    ship.wait(loads[:8])
    for at in range(0, up.shape[1], STEP):
        span = slice(at, at + STEP)
        down[span, :] = dot_tn(active[:, span], slot_rows[...]).astype(LOW)
    ship.wait(loads[8:])
    for at in range(0, up.shape[1], STEP):
        span = slice(at, at + STEP)
        up[:, span] = dot_tn(rows[...], pulled[:, span]).astype(LOW)
    for ref, offs in zip(pieces, offsets):
        size, wide = ref.shape[1] // 2, ref.shape[2] // 2
        for r, off in enumerate(offs):
            i = scalars[0] ^ off
            ref[r, :size, :] = up[pl.ds(pl.multiple_of(i * size, min(size, 16)), size), :]
            at = pl.multiple_of(i * 2 * size, min(size, 16))
            ref[r, size:, :wide] = down[pl.ds(at, size), :]
            ref[r, size:, wide:] = down[pl.ds(at + size, size), :]


def attend_pull_body(images, size, offsets, ship, scalars, *refs):
    count = len(offsets)
    chunks, refs = refs[: 2 * E], refs[2 * E :]
    target, middle, grad, vectors, probs, projected = refs[:6]
    pieces = refs[6 : 6 + count]
    first, small, middle_kept, merged_kept, pulled_kept, *refs = refs[6 + count :]
    middle_grad, merged, pulled, project, merge = refs
    place_attend(scalars[0], size, pieces, offsets, project, merge)
    normed_grad = combined(scalars, target[...], None, chunks)
    unit, inverse = unit_of(middle[...])
    value = grad[...] + norm_pull(normed_grad, unit, inverse, vectors[1:2, : grad.shape[1]])
    middle_grad[...] = value
    ship(middle_grad, middle_kept)
    low = value.astype(LOW)
    merged[...] = low
    ship(merged, merged_kept)
    small[0:1, :] = column_sum(normed_grad * unit)
    small[1:2, :] = column_sum(normed_grad)
    small[2:3, :] = column_sum(low.astype(F32))
    attended_grad = dot_nt(low, merge[...].astype(LOW)).astype(LOW)
    rows = value.shape[0] // images
    wide = merge.shape[0]
    heads = wide // HD
    for i in range(images):
        span = slice(i * rows, (i + 1) * rows)
        for h in range(heads):
            spans = [slice(s * wide + h * HD, s * wide + (h + 1) * HD) for s in range(3)]
            query, keys, values = (projected[span, s] for s in spans)
            head_grad = attended_grad[span, h * HD : (h + 1) * HD]
            prob_low = probs[i * heads + h]
            prob = prob_low.astype(F32)
            prob_grad = dot_nt(head_grad, values)
            score_grad = prob * (prob_grad - jnp.sum(prob_grad * prob, axis=-1, keepdims=True))
            score_grad = score_grad.astype(LOW)
            pulled[span, spans[0]] = (dot(score_grad, keys) * SCALE).astype(LOW)
            pulled[span, spans[1]] = (dot_tn(score_grad, query) * SCALE).astype(LOW)
            pulled[span, spans[2]] = dot_tn(prob_low, head_grad).astype(LOW)
    ship(pulled, pulled_kept)
    first[...] = dot_nt(pulled[...], project[...]).astype(LOW)


def attend_grad_body(size, offsets, scalars, normed, attended, merged, pulled, *refs):
    *refs, project, merge = refs
    small_rows = refs.pop() if len(refs) > len(offsets) + 1 else None
    *given, bias_out = refs
    given, pieces = given[: -len(offsets)], given[-len(offsets) :]
    wide = merge.shape[0]
    project[...] = dot_tn(normed[...], pulled[...]).astype(LOW)
    merge[...] = dot_tn(attended[...], merged[...])
    bias = [column_sum(pulled[:, k * wide : (k + 1) * wide].astype(F32)) for k in (0, 2)]
    bias_out[...] = jnp.concatenate(bias, axis=1)
    if small_rows is not None:
        owners = small_rows.shape[1]
        depth = (len(given) + 1) // 5
        for l in range(depth):
            one, two, up, down = given[4 * l : 4 * l + 4]
            pair = bias if l == 0 else [
                given[4 * depth + l - 1][:, k * wide : (k + 1) * wide] for k in range(2)
            ]
            norms = [one[0:1, :], two[0:1, :], one[1:2, :], two[1:2, :], two[2:3, :]]
            share = norms[0].shape[1] // owners
            first = sum(
                owned(v, owners, wide, k * share) for k, v in enumerate(norms)
            ) + sum(
                owned(v, owners, wide, 5 * share + k * share // 2) for k, v in enumerate(pair)
            )
            small_rows[3 * l] = first
            small_rows[3 * l + 1] = owned(down[...], owners, wide, scalars[1] * share)
            small_rows[3 * l + 2] = owned(up[...], owners, wide, scalars[1] * 2 * share)
    for ref, offs in zip(pieces, offsets):
        part = size // 2
        for r, off in enumerate(offs):
            i = scalars[0] ^ off
            at = pl.ds(pl.multiple_of(i * size, min(size, 16)), size)
            for s in range(3):
                ref[r, s * size : (s + 1) * size, :] = project[at, s * wide : (s + 1) * wide]
            rows = merge[pl.ds(pl.multiple_of(i * part, min(part, 8)), part), :]
            sides = jnp.concatenate([rows[:, :wide], rows[:, wide:]], axis=0)
            ref[r, 3 * size : 4 * size, :] = sides.astype(LOW)
            if small_rows is not None:
                lines = [small_rows[k, pl.ds(i, 1), :] for k in range(small_rows.shape[0])]
                lines.append(jnp.zeros((16 - len(lines), wide), F32))
                ref[r, 4 * size :, :] = jnp.concatenate(lines, axis=0).astype(LOW)


def stream_pull(part, got, stream, middle_grad, vectors, small):
    first = part[...].astype(F32) + got[...].astype(F32)
    unit, inverse = unit_of(stream[...])
    small[0:1, :] = column_sum(first * unit)
    small[1:2, :] = column_sum(first)
    return middle_grad[...] + norm_pull(first, unit, inverse, vectors[0:1, : first.shape[1]])


def stream_pull_body(
    scalars, part, got, stream, middle_grad, vectors, target, gate, grad, small, *sends
):
    value = stream_pull(part, got, stream, middle_grad, vectors, small)
    grad[...] = value
    low = value.astype(LOW)
    for r, send in enumerate(sends):
        send[...] = dot(slot_marks(scalars, r, target[...], gate[...]), low).astype(LOW)


def last_pull_body(scalars, part, got, stream, middle_grad, vectors, out, small):
    value = stream_pull(part, got, stream, middle_grad, vectors, small)
    rows = value.shape[0] // out.shape[0]
    for i in range(out.shape[0]):
        out[i] = value[i * rows : i * rows + out.shape[1]]


def pack_body(count, ship, scalars, *refs):
    given, packs, held = refs[:8], refs[8 : 8 + count], refs[8 + count :]
    ship.wait([ship(a, b) for a, b in zip(given, held)])
    attend, merge, *smalls = held
    depth, _, size, wide = attend.shape
    for l, pack in enumerate(packs):
        for k in range(3):
            pack[0, k * size : (k + 1) * size, :] = attend[l, k]
        rows = merge[l].astype(F32)
        sides = jnp.concatenate([rows[:, :wide], rows[:, wide:]], axis=0)
        pack[0, 3 * size : 4 * size, :] = sides.astype(LOW)

    def row(*parts):
        total, at = jnp.zeros((1, wide), F32), 0
        for part in parts:
            lane = lax.broadcasted_iota(jnp.int32, (part.shape[1], wide), 1)
            home = lax.broadcasted_iota(jnp.int32, lane.shape, 0) + at
            total = total + dot(part, jnp.where(lane == home, 1.0, 0.0).astype(LOW))
            at += part.shape[1]
        return total

    gain, shift, merge_bias, attend_bias, up_bias, down_bias = smalls
    rows = []
    for l in range(depth):
        norms = [v[l, k : k + 1, :] for v in (gain, shift) for k in range(2)]
        rows.append(
            row(*norms, merge_bias[l : l + 1, :], *(attend_bias[l, k : k + 1, :] for k in range(2)))
        )
        rows.append(row(*(down_bias[l, e : e + 1, :] for e in range(E))))
        rows.append(row(*(up_bias[l, e : e + 1, :] for e in range(E))))
    rows.append(jnp.zeros((16 - 3 * depth, wide), F32))
    packs[0][0, 4 * size :, :] = jnp.concatenate(rows, axis=0).astype(LOW)


def deal_body(layer, ship, scalars, up, down, *chunks):
    size, wide = up.shape[2], down.shape[3]
    for r, chunk in enumerate(chunks):
        e = scalars[1] ^ r
        ship(up.at[layer, e], chunk.at[pl.ds(0, size), :])
        for side in range(2):
            ship(
                down.at[layer, e, pl.ds(side * size, size), :],
                chunk.at[pl.ds(size, size), pl.ds(side * wide, wide)],
            )


def prepare_body(images, scalars, routes, gates, columns, rows_out, gate_rows):
    depth, total, _ = routes.shape
    live = live_rows(scalars, total, images)
    square = lax.broadcasted_iota(jnp.int32, (total, total), 0), lax.broadcasted_iota(
        jnp.int32, (total, total), 1
    )
    earlier = jnp.where(square[0] > square[1], 1.0, 0.0).astype(LOW)
    same = jnp.where(square[0] == square[1], 1.0, 0.0).astype(LOW)
    lane = lax.broadcasted_iota(jnp.int32, (total, 128), 1)
    for l in range(depth):
        picks = [routes[l, :, k : k + 1] for k in range(2)]
        chosen = ((lane == picks[0]) | (lane == picks[1])) & live
        taken = dot(earlier, jnp.where(chosen, 1.0, 0.0).astype(LOW))
        mixed = jnp.zeros((total, 128), F32)
        for k, pick in enumerate(picks):
            slot = jnp.sum(jnp.where(lane == pick, taken, 0.0), axis=1, keepdims=True)
            target = jnp.where(live & (pick >= 0), pick * SLOTS + slot.astype(jnp.int32), -1)
            columns[l, :, k : k + 1] = target
            high = (target + 1) >> 5
            mixed = jnp.where(lane == 3 * k, high.astype(F32), mixed)
            mixed = jnp.where(lane == 3 * k + 1, (target + 1 - (high << 5)).astype(F32), mixed)
            mixed = jnp.where(lane == 3 * k + 2, gates[l, :, k : k + 1], mixed)
        turned = dot_tn(mixed.astype(LOW), same)
        for k in range(2):
            high, low, gate = (turned[3 * k + j : 3 * k + j + 1] for j in range(3))
            rows_out[l, k : k + 1, :] = (high * 32.0 + low).astype(jnp.int32) - 1
            gate_rows[l, k : k + 1, :] = gate


def finish_body(depth, scalars, *refs):
    blocks, attends, outs = refs[: E * depth], refs[E * depth], refs[-10:]
    gain, shift, attend, attend_bias, merge, merge_bias, up, up_bias, down, down_bias = outs
    size, wide = up.shape[2], down.shape[3]
    part, share = size // 2, gain.shape[2]
    small = attends[0, 4 * size : 4 * size + 16, :].astype(F32)
    for l in range(depth):
        base = l * 4 * size + (16 if l else 0)
        for r in range(E):
            e = scalars[1] ^ r
            value = blocks[l * E + r][...].astype(F32)
            up[l, e] = value[:size]
            both = value[size:]
            down[l, e] = jnp.concatenate([both[:, :wide], both[:, wide:]], axis=0)
        for k in range(3):
            at = base + k * size
            attend[l, k] = attends[0, at : at + size, :].astype(F32)
        sides = attends[0, base + 3 * size : base + 4 * size, :].astype(F32)
        merge[l] = jnp.concatenate([sides[:part], sides[part:]], axis=1)
        first, second, third = (small[3 * l + k : 3 * l + k + 1, :] for k in range(3))
        for k in range(2):
            gain[l, k : k + 1, :] = first[:, k * share : (k + 1) * share]
            shift[l, k : k + 1, :] = first[:, (2 + k) * share : (3 + k) * share]
            at = 5 * share + k * share // 2
            attend_bias[l, k : k + 1, :] = first[:, at : at + share // 2]
        merge_bias[l : l + 1, :] = first[:, 4 * share : 5 * share]
        for e in range(E):
            down_bias[l, e : e + 1, :] = second[:, e * share : (e + 1) * share]
            up_bias[l, e : e + 1, :] = third[:, 2 * e * share : 2 * (e + 1) * share]


class Place:
    def __init__(self, count, rows, live):
        self.count = count
        self.me = lax.axis_index("dp").astype(jnp.int32)
        core = lax.axis_index("tensor").astype(jnp.int32)
        self.expert = (self.me >> 2) & 3
        self.near = self.expert ^ jnp.arange(E, dtype=jnp.int32)
        powers = [1 << k for k in range(count.bit_length() - 1)]
        self.powers, self.beyond = powers, [b for b in reversed(powers) if b > 8]
        self.aligned = rows % 16 == 0
        where = self.me if self.aligned else jnp.zeros((), jnp.int32)
        self.scalars = jnp.stack([where, self.expert, core, live, self.me])
        far = doubled([0], self.beyond)
        self.parts = [[f ^ l ^ p for f in far for l in LINE] for p in PLANE]
        self.all = [o for offs in self.parts for o in offs]
        blocks = [f ^ l for f in far for l in LINE]
        middle = len(blocks) // 2
        rounds = [(0, blocks), (1, blocks), (2, blocks), (3, blocks[:middle]), (3, blocks[middle:])]
        self.arrivals = [[b ^ p for b in some] for p, some in rounds]
        self.all_arrivals = [o for offs in self.arrivals for o in offs]
        self.fetched = self.arrivals if self.aligned else [[0]]
        self.offsets = self.parts if self.aligned else [[0]]

    def spread(self, value, offsets):
        return [value] + [swap(value, o, self.count) for o in offsets[1:]]

    def near_of(self, value):
        return [swap(value, p, self.count) for p in (1, 2)]

    def gather(self, value, near, anchor=()):
        half = value.shape[0] // 2
        one, two = after(near, anchor)
        return [value, *near, swap(two[:half], 1, self.count), swap(one[half:], 2, self.count)]

    def reduce_onward(self, pieces):
        own, one, two, far = pieces
        half = far.shape[0] // 2
        onward = swap(far[:half], 1, self.count), swap(far[half:], 2, self.count)
        two = jnp.concatenate([add_low(two[:half], onward[0]), two[half:]], axis=0)
        one = jnp.concatenate([one[:half], add_low(one[half:], onward[1])], axis=0)
        return own, one, two

    def reduce(self, own, one, two):
        return add_low(own, swap(one, 1, self.count), swap(two, 2, self.count))

    def deal(self, chunks):
        return [chunks[0]] + [swap(chunks[r], LINE[r], self.count) for r in range(1, E)]

    def exchange(self, chunks, hold=()):
        return self.crossed(self.deal(chunks), hold)

    def crossed(self, own, hold=()):
        return own + [cross(c) for c in (after(own, hold) if hold else own)]

    def doubled(self, value):
        for bit in self.beyond:
            value = jnp.concatenate([value, swap(value, bit, self.count)], axis=0)
        return value

    def halved(self, value):
        for bit in reversed(self.beyond):
            half = value.shape[0] // 2
            value = add_low(value[:half], swap(value[half:], bit, self.count))
        return value


def pack_small(gain, shift, merge, attend, up, down):
    depth, _, share = gain.shape
    spare = jnp.zeros((depth, 2 * share), LOW)
    first = [gain, shift, merge, attend, spare]
    first = jnp.concatenate([p.reshape(depth, -1) for p in first], axis=1)
    second = jnp.pad(down.reshape(depth, -1), ((0, 0), (0, 4 * share)))
    rows = jnp.stack([first, second, up.reshape(depth, -1)], axis=1).reshape(3 * depth, -1)
    return jnp.pad(rows, ((0, -(3 * depth) % 16), (0, 0)))[None]


def pack_attend(attend, merge):
    count, kinds, depth, wide = attend.shape
    rows = attend.reshape(count, 3 * depth, wide)
    return jnp.concatenate([rows, merge[:, :, :wide], merge[:, :, wide:]], axis=1)


def unpack_attend(pack):
    count, rows, wide = pack.shape
    depth = rows // 4
    attend = pack[:, : 3 * depth].reshape(count, 3, depth, wide)
    sides = pack[:, 3 * depth :]
    return attend, jnp.concatenate([sides[:, : depth // 2], sides[:, depth // 2 :]], axis=2)


def whole_attend(pack):
    attend, merge = unpack_attend(pack)
    attend = jnp.swapaxes(attend, 0, 1)
    attend = attend.reshape(3, -1, attend.shape[-1])
    return pack_attend(attend[None], merge.reshape(1, -1, merge.shape[-1]))


def split_attend(pack, count):
    attend, merge = unpack_attend(pack)
    attend = jnp.swapaxes(attend.reshape(3, count, -1, attend.shape[-1]), 0, 1)
    return pack_attend(attend, merge.reshape(count, -1, merge.shape[-1]))


def fetch_column(place, value):
    blocks = place.spread(place.doubled(value), LINE)
    value = jnp.stack(blocks, axis=1)
    return value.reshape((-1,) + value.shape[2:])


def attend_pieces_of(place, pieces):
    if place.aligned:
        return pieces
    return [whole_attend(ordered(jnp.concatenate(pieces), place.all_arrivals, place.me))]


def chunks_of(place, layer, up_weight, down_weight):
    depth, hidden = up_weight.shape[2:]
    if place.aligned:
        return call(
            functools.partial(deal_body, layer),
            [((2 * depth, hidden), LOW)] * E,
            place.scalars,
            up_weight,
            down_weight,
            stored=(0, 1),
        )
    sent = []
    for r in range(E):
        one = lax.dynamic_index_in_dim(up_weight[layer], place.near[r], 0, False)
        two = lax.dynamic_index_in_dim(down_weight[layer], place.near[r], 0, False)
        two = jnp.concatenate([two[:depth], two[depth:]], axis=1)
        sent.append(jnp.concatenate([one, two], axis=0))
    return sent


def fetch_base(place, chunks):
    return place.doubled(jnp.stack(place.deal(chunks)))


def expert_pieces_of(place, pieces):
    if place.aligned:
        return pieces
    pack = ordered(jnp.concatenate(pieces), place.all_arrivals, place.me)
    depth, wide = pack.shape[1] // 2, pack.shape[2] // 2
    up, down = pack[:, :depth], pack[:, depth:]
    down = jnp.concatenate([down[..., :wide], down[..., wide:]], axis=1).reshape(2, -1, wide)
    down = jnp.concatenate([down[0], down[1]], axis=1)
    return [jnp.concatenate([up.reshape(-1, up.shape[-1]), down])[None]]


def add_low(*terms):
    return sum(t.astype(F32) for t in terms).astype(LOW)


def spread_expert(place, pieces):
    if place.aligned:
        return pieces
    pack = pieces[0][0]
    depth, wide = pack.shape[0] // 2, pack.shape[1] // 2
    up = pack[:depth].reshape(place.count, -1, 2 * wide)
    down = jnp.concatenate([pack[depth:, :wide], pack[depth:, wide:]], axis=0)
    down = down.reshape(place.count, 2, -1, wide)
    down = jnp.concatenate([down[:, 0], down[:, 1]], axis=-1)
    value = relative(jnp.concatenate([up, down], axis=1), place.all, place.me)
    return list(value.reshape((len(PLANE), -1) + value.shape[1:]))


def finish_expert(place, blocks):
    pack = jnp.take(jnp.stack(blocks), place.near, axis=0, mode="clip").astype(F32)
    depth, wide = pack.shape[1] // 2, pack.shape[2] // 2
    low = pack[:, depth:]
    return pack[:, :depth], jnp.concatenate([low[..., :wide], low[..., wide:]], axis=1)


def spread_plane(place, full):
    value = relative(split_attend(full, place.count), place.all, place.me)
    return list(value.reshape((len(PLANE), -1) + value.shape[1:]))


def fold_column(place, value):
    value = place.halved(value)
    got = [swap(value[r : r + 1], LINE[r], place.count) for r in range(1, len(LINE))]
    return add_low(value[:1], *got)


def finish_attend(value):
    attend, merge = unpack_attend(value)
    return attend[0].astype(F32), merge[0].astype(F32)


def on_device(
    count,
    inputs,
    image_count,
    routes,
    gates,
    norm_gain,
    norm_shift,
    attend_weight,
    attend_bias,
    merge_weight,
    merge_bias,
    up_weight,
    up_bias,
    down_weight,
    down_bias,
    cotangent,
):
    images, length, width = inputs.shape
    depth = routes.shape[0]
    wide = attend_weight.shape[-1]
    hidden = up_weight.shape[-1]
    heads = wide // HD
    place = Place(count, up_weight.shape[2], image_count[0])
    scalars = place.scalars
    rows = -(-length // 16) * 16
    total = images * rows
    half = E * HALF
    size = width // count if place.aligned else width

    def padded(value, fill=0):
        spare = [(0, 0)] * value.ndim
        spare[-2] = (0, rows - length)
        value = jnp.pad(value, spare, constant_values=fill)
        return value.reshape(value.shape[:-3] + (total, value.shape[-1]))

    chunk = ((HALF, width), LOW)
    wide_rows = ((total, width), F32)
    low_rows = ((total, width), LOW)
    wide_half, low_slots = ((half, width), F32), ((2 * half, width), LOW)
    low_half = ((half, width), LOW)
    low_hidden = ((2 * half, hidden), LOW)
    low_project = ((total, 3 * wide), LOW)
    attend_scratch = [((width, 3 * wide), LOW), ((wide, width), F32)]
    expert_scratch = [((width, hidden), LOW), ((hidden, width), LOW)]

    smalls = (norm_gain, norm_shift, merge_bias, attend_bias, up_bias, down_bias)
    small = []
    if place.aligned:
        given = (attend_weight, merge_weight, *smalls)
        sizes = [4 * size + (16 if l == 0 else 0) for l in range(depth)]
        packs = call(
            functools.partial(pack_body, depth),
            [((1, n, wide), LOW) for n in sizes],
            scalars,
            *given,
            scratch=[(g.shape, LOW) for g in given],
            stored=range(len(given)),
        )
    else:
        packs = [pack_attend(attend_weight[l][None], merge_weight[l][None]) for l in range(depth)]
        small = place.spread(fetch_column(place, pack_small(*smalls)), PLANE)
        small = [ordered(jnp.concatenate(small), place.all, place.me)]
    column = fetch_column(place, packs[0])
    chunks = chunks_of(place, 0, up_weight, down_weight)
    base = fetch_base(place, after(chunks, column))
    near = place.near_of(column)
    attend_pieces = attend_pieces_of(place, place.gather(column, near))
    target, target_rows, gate_rows = call(
        functools.partial(prepare_body, images),
        [((depth, total, 2), jnp.int32)]
        + [((depth, 2, total), jnp.int32), ((depth, 2, total), F32)],
        scalars,
        *after((padded(routes, -1), padded(gates)), column),
    )
    gate = padded(gates)
    stream = padded(after(inputs, column))
    states = []
    back, first_sends = None, ()
    for l in range(depth):
        more = l + 1 < depth
        base = after(base, attend_pieces)
        near = place.near_of(base)
        kinds = [low_rows, low_project, ((images * heads, rows, rows), LOW), ((total, wide), LOW)]
        body = functools.partial(
            attend_body, length, images, size, place.fetched, l > 0, not place.aligned
        )
        if l == 0:
            table = [((count, 16, wide), LOW)] if place.aligned else []
            part, vectors, *keeps = call(
                body,
                [low_rows, ((depth, 8, hidden), F32)],
                scalars,
                stream,
                *small,
                *attend_pieces,
                saved=kinds,
                scratch=kinds + attend_scratch + table,
                before=(base,),
                us=LONG,
            )
            stream_kept = stream
        else:
            stream, part, stream_kept, *keeps = call(
                body,
                [wide_rows, low_rows],
                scalars,
                middle,
                *back,
                target[l - 1],
                gate[l - 1],
                vectors[l],
                *attend_pieces,
                saved=[wide_rows] + kinds,
                scratch=kinds + attend_scratch,
                before=first_sends,
                us=LONG,
            )
        normed, projected, probs, attended = keeps
        if more:
            chunks = chunks_of(place, l + 1, up_weight, down_weight)
            next_base = fetch_base(place, after(chunks, base))
        middle, *sends, middle_kept = call(
            middle_body,
            [wide_rows] + [chunk] * E,
            scalars,
            stream,
            part,
            cross(part),
            vectors[l],
            target_rows[l],
            saved=[wide_rows],
            before=(next_base,) if more else (),
        )
        own = place.deal(sends)
        expert_pieces = expert_pieces_of(place, place.gather(base, near, own[2]))
        taken = place.crossed(own, expert_pieces)
        kept = attend_pieces
        if more:
            base = next_base
            column = fetch_column(place, after(packs[l + 1], own))
        others, result, active, slope, taken_rows = call(
            functools.partial(expert_body, place.fetched, not more),
            [low_half] if more else [],
            scalars,
            *taken,
            vectors[l],
            *expert_pieces,
            saved=([] if more else [low_half]) + [wide_half, low_hidden, low_hidden, low_slots],
            scratch=[wide_half, low_hidden, low_hidden, low_slots]
            + expert_scratch
            + ([] if more else [low_half]),
            us=LONG,
        )
        states.append(
            (stream_kept, middle_kept, normed, projected, probs, attended, taken_rows, active, slope)
            + (kept, expert_pieces)
        )
        if more:
            near = place.near_of(after(column, others))
            sends = call(
                total_body,
                [chunk] * E,
                scalars,
                result,
                cross(others),
                vectors[l],
                before=(column,),
            )
            attend_pieces = attend_pieces_of(place, place.gather(column, near, sends))
            back = place.exchange(sends, attend_pieces)
            if l + 2 == depth:
                grad, *first_sends = call(
                    functools.partial(first_grad_body, images),
                    [wide_rows] + [chunk] * E,
                    scalars,
                    padded(after(cotangent, sends)),
                    target_rows[-1],
                    gate_rows[-1],
                )

    last, last_others = result, others
    slot_grad = place.crossed(place.deal(after(first_sends, own)), (result,))
    blocks = [None] * depth
    attend_sums, smalls, biases = [None] * depth, [None] * depth, [None] * depth
    waiting, before_expert, before_total, before_grad = [], (), (), ()
    for l in reversed(range(depth)):
        stream, middle, normed, projected, probs, attended, taken, active, slope = states[l][:9]
        attend_pieces, expert_pieces = states[l][9:]
        others, up_b, down_b, result, pulled, slot_rows = call(
            functools.partial(expert_pull_body, place.fetched),
            [low_half, ((1, hidden), F32), ((1, width), F32)],
            scalars,
            *slot_grad,
            slope,
            *expert_pieces,
            saved=[wide_half, low_hidden, low_slots],
            scratch=[wide_half, low_hidden, low_slots, low_hidden] + expert_scratch,
            before=before_expert,
            stored=(2 * E,),
            us=LONG,
        )
        sends = call(
            total_body,
            [chunk] * E,
            scalars,
            result,
            cross(others),
        )
        own = place.deal(sends)
        before_attend = ()
        if waiting:
            attend_sum = place.reduce(*after(before_total, sends))
            before_attend = (attend_sum,)
            waiting.append(attend_sum)
        active, pulled_late = after((active, pulled), own[1])
        pieces = call(
            functools.partial(expert_grad_body, place.offsets),
            [((len(o), 2 * size, hidden), LOW) for o in place.offsets],
            scalars,
            slot_rows,
            active,
            taken,
            pulled_late,
            scratch=expert_scratch + [low_slots, low_hidden, low_slots, low_hidden],
            stored=range(4),
            us=7,
        )
        back = place.crossed(own, pieces)
        expert_onward = place.reduce_onward(spread_expert(place, pieces))
        if waiting:
            done, value, total_sum = waiting
            blocks[done] = place.deal(list(place.halved(after(value, back))))
            before_grad = blocks[done]
            waiting = [done, total_sum]
        pull_kinds = [wide_rows, low_rows, low_project]
        first, small_two, middle_grad, merged, pulled = call(
            functools.partial(attend_pull_body, images, size, place.fetched),
            [low_rows, ((3, width), F32)],
            scalars,
            *back,
            target[l],
            middle,
            grad,
            vectors[l],
            probs,
            projected,
            *attend_pieces,
            saved=pull_kinds,
            scratch=pull_kinds + attend_scratch,
            before=before_attend,
            us=LONG,
        )
        got = cross(first)
        if l > 0:
            grad, small_one, *sends = call(
                stream_pull_body,
                [wide_rows, ((2, width), F32)] + [chunk] * E,
                scalars,
                first,
                got,
                stream,
                middle_grad,
                vectors[l],
                target_rows[l - 1],
                gate_rows[l - 1],
                before=expert_onward,
            )
            own = place.deal(sends)
            slot_grad = place.crossed(own)
            pulled_late = after(pulled, own[3])
        else:
            input_grad, small_one = call(
                last_pull_body,
                [(inputs.shape, F32), ((2, width), F32)],
                scalars,
                first,
                got,
                stream,
                middle_grad,
                vectors[l],
                before=expert_onward,
            )
            pulled_late = pulled
        smalls[l] = (small_one, small_two, up_b, down_b)
        extra = []
        joint = place.aligned and l == 0
        if joint:
            extra = [v for some in smalls for v in some] + biases[1:]
        height = 4 * size + (16 if joint else 0)
        *pieces, biases[l] = call(
            functools.partial(attend_grad_body, size, place.offsets),
            [((len(o), height, wide), LOW) for o in place.offsets] + [((1, width), F32)],
            scalars,
            normed,
            attended,
            merged,
            pulled_late,
            *extra,
            scratch=([((3 * depth, count, wide), F32)] if joint else []) + attend_scratch,
            before=before_grad,
            us=4 if l else LONG,
        )
        if not place.aligned:
            pieces = spread_plane(place, pieces[0])
        if l == 0:
            ends = after((last, last_others), before_grad)
            ends = call(
                total_body, [chunk] * E, scalars, ends[0], cross(ends[1]), vectors[-1]
            )
            ends = place.deal(ends)
            pieces = after(pieces, ends)
        before_total = place.reduce_onward(pieces)
        expert_sum = place.reduce(*expert_onward)
        before_expert = (expert_sum,)
        if waiting:
            done, total_sum = waiting
            attend_sums[done] = total_sum
        waiting = [l, expert_sum]
    blocks[0] = place.deal(list(place.halved(expert_sum)))
    attend_sums[0] = place.reduce(*after(before_total, expert_sum))
    heights = [v.shape[1] for v in attend_sums]
    attend_grads = fold_column(place, jnp.concatenate(attend_sums, axis=1))
    starts = [sum(heights[:l]) for l in range(depth)]
    ends = after(ends, pieces)
    (output,) = call(
        output_body,
        [(inputs.shape, F32)],
        scalars,
        states[-1][1],
        *ends,
        *map(cross, ends),
        target[-1],
        gate[-1],
    )
    if place.aligned:
        grads = (norm_gain, norm_shift, attend_weight, attend_bias, merge_weight, merge_bias)
        grads += (up_weight, up_bias, down_weight, down_bias)
        return output, input_grad, *call(
            functools.partial(finish_body, depth),
            [(g.shape, F32) for g in grads],
            scalars,
            *[b for layer in blocks for b in layer],
            attend_grads,
        )

    tables = []
    at_expert = jnp.arange(E, dtype=jnp.int32)[:, None, None] == place.expert
    for (small_one, small_two, up_b, down_b), bias in zip(smalls, biases):
        expert_rows = jnp.concatenate([up_b.reshape(-1, width), down_b], axis=0)
        expert_rows = jnp.where(at_expert, expert_rows[None], 0.0).reshape(-1, width)
        tables.append(jnp.concatenate([small_one, small_two, bias, expert_rows], axis=0))
    small = jnp.stack(tables)
    for bit in place.beyond:
        small = small + swap(small, bit, count)
    for offsets in (PLANE, LINE):
        terms = place.spread(small, offsets)
        small = (terms[0] + terms[1]) + (terms[2] + terms[3])

    def mine(value, size):
        return lax.dynamic_slice_in_dim(value, place.me * size, size, value.ndim - 1)

    share = norm_gain.shape[-1]
    gain_grad = jnp.stack([small[:, 0], small[:, 2]], axis=1)
    shift_grad = jnp.stack([small[:, 1], small[:, 3]], axis=1)
    attend_b = small[:, 5].reshape(depth, 2, wide)
    expert_rows = small[:, 6:].reshape(depth, E, -1, width)
    up_b = expert_rows[:, :, :-1].reshape(depth, E, hidden)
    parts = [attend_grads[:, a : a + n] for a, n in zip(starts, heights)]
    finished = [finish_expert(place, b) + finish_attend(a) for b, a in zip(blocks, parts)]
    up_grad, down_grad, attend_grad, merge_grad = (
        jnp.stack([f[k] for f in finished]) for k in range(4)
    )
    return (
        output,
        input_grad,
        mine(gain_grad, share),
        mine(shift_grad, share),
        attend_grad,
        mine(attend_b, attend_bias.shape[-1]),
        merge_grad,
        mine(small[:, 4], share),
        up_grad,
        mine(up_b, up_bias.shape[-1]),
        down_grad,
        mine(expert_rows[:, :, -1], share),
    )


def solution(mesh):
    placed = (
        P("dp", None, None),
        P("dp"),
        P(None, "dp", None, None),
        P(None, "dp", None, None),
        P(None, None, "dp"),
        P(None, None, "dp"),
        P(None, None, "dp", "tensor"),
        P(None, None, ("tensor", "dp")),
        P(None, ("tensor", "dp"), None),
        P(None, "dp"),
        P(None, None, "dp", "tensor"),
        P(None, None, ("tensor", "dp")),
        P(None, None, ("tensor", "dp"), None),
        P(None, None, "dp"),
        P("dp", None, None),
    )
    return jax.shard_map(
        functools.partial(on_device, mesh.shape["dp"]),
        mesh=mesh,
        in_specs=placed,
        out_specs=(
            P("dp", None, None),
            P("dp", None, None),
            P(None, None, "dp"),
            P(None, None, "dp"),
            P(None, None, "dp", "tensor"),
            P(None, None, ("tensor", "dp")),
            P(None, ("tensor", "dp"), None),
            P(None, "dp"),
            P(None, None, "dp", "tensor"),
            P(None, None, ("tensor", "dp")),
            P(None, None, ("tensor", "dp"), None),
            P(None, None, "dp"),
        ),
        check_vma=False,
    )
```

```python
import functools

import jax
import jax.numpy as jnp
from jax import lax
from jax.experimental import pallas as pl
from jax.experimental.pallas import tpu as pltpu
from jax.sharding import PartitionSpec as P

HD = 64
E = 4
SLOTS = 256
HALF = SLOTS // 2
PLANE = (0, 1, 2, 3)
LINE = (0, 4, 8, 12)
ROWS = 256
STEP = 512
LONG = 60
VMEM = 32 * 2**20
LOW = jnp.bfloat16
F32 = jnp.float32
SCALE = HD ** (-0.5)


def dot(left, right):
    return jnp.dot(left, right, preferred_element_type=F32)


def dot_nt(left, right):
    return lax.dot_general(left, right, (((1,), (1,)), ((), ())), preferred_element_type=F32)


def dot_tn(left, right):
    return lax.dot_general(left, right, (((0,), (0,)), ((), ())), preferred_element_type=F32)


def swap(value, bit, count):
    return lax.ppermute(value, "dp", [(i, i ^ bit) for i in range(count)])


def after(value, *anchors):
    return lax.optimization_barrier((value, anchors))[0]


def cross(value):
    return lax.ppermute(value, "tensor", [(0, 1), (1, 0)])


def doubled(offsets, bits):
    for bit in bits:
        offsets = offsets + [o ^ bit for o in offsets]
    return offsets


def ordered(value, offsets, me):
    where = jnp.asarray([offsets.index(i) for i in range(len(offsets))], jnp.int32)
    index = where[jnp.arange(len(offsets), dtype=jnp.int32) ^ me]
    return jnp.take(value, index, axis=0, mode="clip")


def relative(value, offsets, me):
    return jnp.take(value, jnp.asarray(offsets, jnp.int32) ^ me, axis=0, mode="clip")


def call(kernel, outs, scalars, *args, saved=(), scratch=(), before=(), stored=(), us=0):
    memory = pl.BlockSpec(memory_space=pltpu.VMEM)

    def body(*refs):
        ships = saved or stored
        sems = refs[-1] if ships else None
        started, settled = [], []

        def ship(source, target):
            copy = pltpu.make_async_copy(source, target, sems.at[len(started)])
            copy.start()
            started.append(copy)
            return copy

        def wait(copies):
            for copy in copies:
                copy.wait()
            settled.extend(copies)

        ship.wait = wait
        if ships:
            kernel(ship, *refs[:-1])
        else:
            kernel(*refs)
        for copy in started:
            if not any(copy is done for done in settled):
                copy.wait()

    if before:
        scalars = after(scalars, *before)
    args = [
        pltpu.with_memory_space_constraint(a, pltpu.HBM) if k in stored else a
        for k, a in enumerate(args)
    ]
    return pl.pallas_call(
        body,
        out_shape=[jax.ShapeDtypeStruct(shape, kind) for shape, kind in outs]
        + [pltpu.HBM(shape, kind) for shape, kind in saved],
        in_specs=[pl.BlockSpec(memory_space=pltpu.SMEM)]
        + [pl.BlockSpec(memory_space=pltpu.HBM) if k in stored else memory for k in range(len(args))],
        out_specs=[memory] * len(outs) + [pl.BlockSpec(memory_space=pltpu.HBM)] * len(saved),
        scratch_shapes=[pltpu.VMEM(shape, kind) for shape, kind in scratch]
        + ([pltpu.SemaphoreType.DMA((24,))] if saved or stored else []),
        compiler_params=pltpu.CompilerParams(vmem_limit_bytes=VMEM),
        cost_estimate=pl.CostEstimate(
            flops=us * 10**9, transcendentals=0, bytes_accessed=us * 10**3
        ),
    )(scalars, *args)


def unit_of(stream):
    center = stream - jnp.mean(stream, axis=-1, keepdims=True)
    inverse = lax.rsqrt(jnp.mean(center * center, axis=-1, keepdims=True) + 1e-06)
    return center * inverse, inverse


def norm_pull(grad, unit, inverse, gain):
    scaled = grad * gain
    return inverse * (
        scaled
        - jnp.mean(scaled, axis=-1, keepdims=True)
        - unit * jnp.mean(scaled * unit, axis=-1, keepdims=True)
    )


def column_sum(value):
    return jnp.sum(value, axis=0, keepdims=True)


def place_attend(where, size, pieces, offsets, project, merge):
    for ref, offs in zip(pieces, offsets):
        wide, part = ref.shape[2], size // 2
        for r, off in enumerate(offs):
            i = where ^ off
            at = pl.ds(pl.multiple_of(i * size, min(size, 16)), size)
            for s in range(3):
                project[at, s * wide : (s + 1) * wide] = ref[r, s * size : (s + 1) * size, :]
            sides = ref[r, 3 * size : 4 * size, :].astype(F32)
            at = pl.ds(pl.multiple_of(i * part, min(part, 8)), part)
            merge[at, :wide] = sides[:part]
            merge[at, wide:] = sides[part:]


def place_expert(where, pieces, offsets, up, down):
    for ref, offs in zip(pieces, offsets):
        size, wide = ref.shape[1] // 2, ref.shape[2] // 2
        for r, off in enumerate(offs):
            i = where ^ off
            up[pl.ds(pl.multiple_of(i * size, min(size, 16)), size), :] = ref[r, :size, :]
            at = pl.multiple_of(i * 2 * size, min(size, 16))
            down[pl.ds(at, size), :] = ref[r, size:, :wide]
            down[pl.ds(at + size, size), :] = ref[r, size:, wide:]


def rows_of(chunks):
    return jnp.concatenate([c[...] for c in chunks], axis=0)


def slot_marks(scalars, r, target, gate):
    base = (scalars[1] ^ r) * SLOTS + scalars[2] * HALF
    slots = lax.broadcasted_iota(jnp.int32, (HALF, target.shape[1]), 0) + base
    first, second = slots == target[0:1], slots == target[1:2]
    if gate is None:
        return jnp.where(first | second, 1.0, 0.0).astype(LOW)
    weight = jnp.where(first, gate[0:1], 0.0) + jnp.where(second, gate[1:2], 0.0)
    return weight.astype(LOW)


def row_marks(slots, target, gate):
    first, second = target[:, 0:1] == slots, target[:, 1:2] == slots
    if gate is None:
        return jnp.where(first | second, 1.0, 0.0).astype(LOW)
    weight = jnp.where(first, gate[:, 0:1], 0.0) + jnp.where(second, gate[:, 1:2], 0.0)
    return weight.astype(LOW)


def combined(scalars, target, gate, chunks):
    marks = []
    for h in range(2):
        for r in range(E):
            base = (scalars[1] ^ r) * SLOTS + (scalars[2] ^ h) * HALF
            slots = lax.broadcasted_iota(jnp.int32, (1, HALF), 1) + base
            marks.append(row_marks(slots, target, gate))
    return dot(jnp.concatenate(marks, axis=1), rows_of(chunks))


def owned(vector, owners, wide, at):
    count = vector.shape[1]
    share = count // owners
    lane = lax.broadcasted_iota(jnp.int32, (owners, count), 1)
    start = lax.broadcasted_iota(jnp.int32, (owners, count), 0) * share
    mine = jnp.where((lane >= start) & (lane < start + share), vector, 0.0).astype(LOW)
    lane = lax.broadcasted_iota(jnp.int32, (count, 128), 0)
    turn = jnp.floor((lane.astype(F32) + 0.5) * (1.0 / share)).astype(jnp.int32)
    home = lane - turn * share == lax.broadcasted_iota(jnp.int32, (count, 128), 1)
    packed = dot(mine, jnp.where(home, 1.0, 0.0).astype(LOW)).astype(LOW)
    lane = lax.broadcasted_iota(jnp.int32, (128, wide), 0)
    home = (lane + at == lax.broadcasted_iota(jnp.int32, (128, wide), 1)) & (lane < share)
    return dot(packed, jnp.where(home, 1.0, 0.0).astype(LOW))


def join_vectors(scalars, small, vectors):
    owners = small.shape[0]

    def joined(part):
        wide = part.shape[1]
        lane = lax.broadcasted_iota(jnp.int32, (wide, owners * wide), 1)
        turn = jnp.floor((lane.astype(F32) + 0.5) * (1.0 / wide)).astype(jnp.int32)
        place = lane - turn * wide == lax.broadcasted_iota(jnp.int32, lane.shape, 0)
        spread = dot(part.astype(LOW), jnp.where(place, 1.0, 0.0).astype(LOW))
        start = lax.broadcasted_iota(jnp.int32, spread.shape, 0) * wide
        lane = lax.broadcasted_iota(jnp.int32, spread.shape, 1)
        return column_sum(jnp.where((lane >= start) & (lane < start + wide), spread, 0.0))

    share = small.shape[2] // 8
    half = share // 2
    expert = scalars[1]
    for l in range(vectors.shape[0]):
        first, second, third = (small[:, 3 * l + k, :] for k in range(3))
        parts = [first[:, k * share : (k + 1) * share] for k in range(5)]
        for k, part in enumerate(parts):
            vectors[l, k : k + 1, : owners * share] = joined(part)
        at = 5 * share
        query, values = (joined(first[:, at + k * half : at + (k + 1) * half]) for k in range(2))
        vectors[l, 5:6, : 3 * owners * half] = jnp.concatenate(
            [query, jnp.zeros_like(query), values], axis=1
        )
        up = sum(
            jnp.where(expert == e, third[:, 2 * e * share : 2 * (e + 1) * share], 0.0)
            for e in range(E)
        )
        vectors[l, 6:7, :] = joined(up)
        down = sum(
            jnp.where(expert == e, second[:, e * share : (e + 1) * share], 0.0) for e in range(E)
        )
        vectors[l, 7:8, : owners * share] = joined(down)


def live_rows(scalars, rows, images):
    return lax.broadcasted_iota(jnp.int32, (rows, 1), 0) < scalars[3] * (rows // images)


def attend_body(length, images, size, offsets, from_slots, split, ship, *refs):
    count = len(offsets)
    scalars, refs = refs[0], refs[1:]
    if from_slots:
        middle, *back = refs[: 1 + 2 * E]
        target, gate, vectors = refs[1 + 2 * E : 4 + 2 * E]
        refs = refs[4 + 2 * E :]
    else:
        stream_in, refs = refs[0], refs[1:]
        if split:
            small, refs = refs[0], refs[1:]
    pieces, refs = refs[:count], refs[count:]
    if from_slots:
        stream_out, partial, stream_kept, *refs = refs
    else:
        partial, all_vectors, *refs = refs
        vectors = all_vectors.at[0]
    kept, (normed, projected, probs, attended, project, merge, *rest) = refs[:4], refs[4:]
    place_attend(scalars[0], size, pieces, offsets, project, merge)
    if not from_slots:
        if not split:
            (small,) = rest
            for ref, offs in zip(pieces, offsets):
                for r, off in enumerate(offs):
                    small[scalars[0] ^ off] = ref[r, 4 * size :, :]
        join_vectors(scalars, small[...].astype(F32), all_vectors)
    if from_slots:
        stream = middle[...] + combined(scalars, target[...], gate[...], back)
        stream_out[...] = stream
        ship(stream_out, stream_kept)
    else:
        stream = stream_in[...]
    unit, inverse = unit_of(stream)
    width = stream.shape[1]
    normed[...] = (unit * vectors[0:1, :width] + vectors[2:3, :width]).astype(LOW)
    ship(normed, kept[0])
    bias = vectors[5:6, : project.shape[1]]
    projected[...] = (dot(normed[...], project[...]) + bias).astype(LOW)
    ship(projected, kept[1])
    rows = stream.shape[0] // images
    wide = merge.shape[0]
    heads = wide // HD
    keep = lax.broadcasted_iota(jnp.int32, (rows, rows), 1) < length
    for i in range(images):
        span = slice(i * rows, (i + 1) * rows)
        for h in range(heads):
            query = projected[span, h * HD : (h + 1) * HD]
            keys = projected[span, wide + h * HD : wide + (h + 1) * HD]
            values = projected[span, 2 * wide + h * HD : 2 * wide + (h + 1) * HD]
            scores = jnp.where(keep, dot_nt(query, keys) * SCALE, -1e30)
            raised = jnp.exp(scores - jnp.max(scores, axis=-1, keepdims=True))
            prob = raised / jnp.sum(raised, axis=-1, keepdims=True)
            prob_low = prob.astype(LOW)
            probs[i * heads + h] = prob_low
            attended[span, h * HD : (h + 1) * HD] = dot(prob_low, values).astype(LOW)
        ship(probs.at[pl.ds(i * heads, heads)], kept[2].at[pl.ds(i * heads, heads)])
    ship(attended, kept[3])
    partial[...] = dot(attended[...], merge[...].astype(LOW)).astype(LOW)


def middle_body(ship, scalars, stream, part, got, vectors, target, middle, *refs):
    sends, kept = refs[:E], refs[E]
    width = stream.shape[1]
    gain, shift, bias = (vectors[k : k + 1, :width] for k in (1, 3, 4))
    value = stream[...] + part[...].astype(F32) + got[...].astype(F32) + bias
    middle[...] = value
    ship(middle, kept)
    unit, inverse = unit_of(value)
    normed = (unit * gain + shift).astype(LOW)
    for r, send in enumerate(sends):
        send[...] = dot(slot_marks(scalars, r, target[...], None), normed).astype(LOW)


def expert_body(offsets, last, ship, scalars, *refs):
    count = len(offsets)
    chunks, vectors, refs = refs[: 2 * E], refs[2 * E], refs[2 * E + 1 :]
    pieces, refs = refs[:count], refs[count:]
    if last:
        others_kept, refs = refs[0], refs[1:]
        others, refs = refs[-1], refs[:-1]
    else:
        others, refs = refs[0], refs[1:]
    result_kept, active_kept, slope_kept, rows_kept, result, active, slope, rows, up, down = refs
    place_expert(scalars[0], pieces, offsets, up, down)
    bias = vectors[6:7, :]
    for k in reversed(range(0, 2 * E, 2)):
        at = k * HALF
        span = pl.ds(at, 2 * HALF)
        rows[span, :] = rows_of(chunks[k : k + 2])
        ship(rows.at[span], rows_kept.at[span])
        hidden = dot(rows[span, :], up[...]) + bias
        square = hidden * hidden
        bent = jnp.tanh(0.7978845608028654 * hidden * (1.0 + 0.044715 * square))
        low = 0.5 * (1.0 + bent)
        act = (hidden * low).astype(LOW)
        active[span, :] = act
        slope[span, :] = (
            low
            + hidden
            * (0.5 * 0.7978845608028654)
            * (1.0 - bent * bent)
            * (1.0 + 3 * 0.044715 * square)
        ).astype(LOW)
        ship(active.at[span], active_kept.at[span])
        ship(slope.at[span], slope_kept.at[span])
        out = dot(act, down[...])
        if k < E:
            result[span, :] = out
            ship(result.at[span], result_kept.at[span])
        else:
            span = pl.ds(at - E * HALF, 2 * HALF)
            others[span, :] = out.astype(LOW)
            if last:
                ship(others.at[span], others_kept.at[span])


def total_body(scalars, part, *refs):
    got, sends = refs[:-E], refs[-E:]
    vectors = None
    if got[-1].dtype == F32:
        got, vectors = got[:-1], got[-1]
    for r, send in enumerate(sends):
        span = slice(r * HALF, (r + 1) * HALF)
        value = part[span, :] + got[0][span, :].astype(F32)
        if vectors is not None:
            value = value + vectors[7:8, : value.shape[1]]
        send[...] = value.astype(LOW)


def output_body(scalars, middle, *refs):
    chunks, (target, gate, out) = refs[: 2 * E], refs[2 * E :]
    value = middle[...] + combined(scalars, target[...], gate[...], chunks)
    value = jnp.where(live_rows(scalars, value.shape[0], out.shape[0]), value, 0.0)
    rows = value.shape[0] // out.shape[0]
    for i in range(out.shape[0]):
        out[i] = value[i * rows : i * rows + out.shape[1]]


def first_grad_body(images, scalars, cotangent, target, gate, grad, *sends):
    value = jnp.where(live_rows(scalars, grad.shape[0], images), cotangent[...], 0.0)
    grad[...] = value
    low = value.astype(LOW)
    for r, send in enumerate(sends):
        send[...] = dot(slot_marks(scalars, r, target[...], gate[...]), low).astype(LOW)


def expert_pull_body(offsets, ship, scalars, *refs):
    count = len(offsets)
    chunks, slope, refs = refs[: 2 * E], refs[2 * E], refs[2 * E + 1 :]
    pieces, others, refs = refs[:count], refs[count], refs[count + 1 :]
    up_bias, down_bias, result_kept, hidden_kept, rows_kept, *refs = refs
    result, hidden_grad, rows, slope_here, up, down = refs
    spans = [pl.ds(k * HALF, 2 * HALF) for k in range(0, 2 * E, 2)]
    loads = [ship(slope.at[s], slope_here.at[s]) for s in reversed(spans)][::-1]
    place_expert(scalars[0], pieces, offsets, up, down)
    total = jnp.zeros(up_bias.shape, F32)
    total_down = jnp.zeros(down_bias.shape, F32)
    for k in reversed(range(0, 2 * E, 2)):
        span = pl.ds(k * HALF, 2 * HALF)
        value = rows_of(chunks[k : k + 2])
        rows[span, :] = value
        ship(rows.at[span], rows_kept.at[span])
        total_down = total_down + column_sum(value.astype(F32))
        ship.wait([loads[k // 2]])
        low = (dot_nt(value, down[...]) * slope_here[span, :].astype(F32)).astype(LOW)
        hidden_grad[span, :] = low
        ship(hidden_grad.at[span], hidden_kept.at[span])
        total = total + column_sum(low.astype(F32))
        out = dot_nt(low, up[...])
        if k < E:
            result[span, :] = out
            ship(result.at[span], result_kept.at[span])
        else:
            others[pl.ds((k - E) * HALF, 2 * HALF), :] = out.astype(LOW)
    up_bias[...] = total
    down_bias[...] = total_down


def expert_grad_body(offsets, ship, scalars, *refs):
    given, refs = refs[:4], refs[4:]
    pieces, (up, down, *held) = refs[: len(offsets)], refs[len(offsets) :]
    loads = []
    for a, b in zip(given, held):
        step = a.shape[0] // 4
        spans = [pl.ds(k * step, step) for k in range(4)]
        loads += [ship(a.at[span], b.at[span]) for span in spans]
    slot_rows, active, rows, pulled = held
    ship.wait(loads[:8])
    for at in range(0, up.shape[1], STEP):
        span = slice(at, at + STEP)
        down[span, :] = dot_tn(active[:, span], slot_rows[...]).astype(LOW)
    ship.wait(loads[8:])
    for at in range(0, up.shape[1], STEP):
        span = slice(at, at + STEP)
        up[:, span] = dot_tn(rows[...], pulled[:, span]).astype(LOW)
    for ref, offs in zip(pieces, offsets):
        size, wide = ref.shape[1] // 2, ref.shape[2] // 2
        for r, off in enumerate(offs):
            i = scalars[0] ^ off
            ref[r, :size, :] = up[pl.ds(pl.multiple_of(i * size, min(size, 16)), size), :]
            at = pl.multiple_of(i * 2 * size, min(size, 16))
            ref[r, size:, :wide] = down[pl.ds(at, size), :]
            ref[r, size:, wide:] = down[pl.ds(at + size, size), :]


def attend_pull_body(images, size, offsets, ship, scalars, *refs):
    count = len(offsets)
    chunks, refs = refs[: 2 * E], refs[2 * E :]
    target, middle, grad, vectors, probs, projected = refs[:6]
    pieces = refs[6 : 6 + count]
    first, small, middle_kept, merged_kept, pulled_kept, *refs = refs[6 + count :]
    middle_grad, merged, pulled, project, merge = refs
    place_attend(scalars[0], size, pieces, offsets, project, merge)
    normed_grad = combined(scalars, target[...], None, chunks)
    unit, inverse = unit_of(middle[...])
    value = grad[...] + norm_pull(normed_grad, unit, inverse, vectors[1:2, : grad.shape[1]])
    middle_grad[...] = value
    ship(middle_grad, middle_kept)
    low = value.astype(LOW)
    merged[...] = low
    ship(merged, merged_kept)
    small[0:1, :] = column_sum(normed_grad * unit)
    small[1:2, :] = column_sum(normed_grad)
    small[2:3, :] = column_sum(low.astype(F32))
    attended_grad = dot_nt(low, merge[...].astype(LOW)).astype(LOW)
    rows = value.shape[0] // images
    wide = merge.shape[0]
    heads = wide // HD
    for i in range(images):
        span = slice(i * rows, (i + 1) * rows)
        for h in range(heads):
            spans = [slice(s * wide + h * HD, s * wide + (h + 1) * HD) for s in range(3)]
            query, keys, values = (projected[span, s] for s in spans)
            head_grad = attended_grad[span, h * HD : (h + 1) * HD]
            prob_low = probs[i * heads + h]
            prob = prob_low.astype(F32)
            prob_grad = dot_nt(head_grad, values)
            score_grad = prob * (prob_grad - jnp.sum(prob_grad * prob, axis=-1, keepdims=True))
            score_grad = score_grad.astype(LOW)
            pulled[span, spans[0]] = (dot(score_grad, keys) * SCALE).astype(LOW)
            pulled[span, spans[1]] = (dot_tn(score_grad, query) * SCALE).astype(LOW)
            pulled[span, spans[2]] = dot_tn(prob_low, head_grad).astype(LOW)
    ship(pulled, pulled_kept)
    first[...] = dot_nt(pulled[...], project[...]).astype(LOW)


def attend_grad_body(size, offsets, scalars, normed, attended, merged, pulled, *refs):
    *refs, project, merge = refs
    small_rows = refs.pop() if len(refs) > len(offsets) + 1 else None
    *given, bias_out = refs
    given, pieces = given[: -len(offsets)], given[-len(offsets) :]
    wide = merge.shape[0]
    project[...] = dot_tn(normed[...], pulled[...]).astype(LOW)
    merge[...] = dot_tn(attended[...], merged[...])
    bias = [column_sum(pulled[:, k * wide : (k + 1) * wide].astype(F32)) for k in (0, 2)]
    bias_out[...] = jnp.concatenate(bias, axis=1)
    if small_rows is not None:
        owners = small_rows.shape[1]
        depth = (len(given) + 1) // 5
        for l in range(depth):
            one, two, up, down = given[4 * l : 4 * l + 4]
            pair = bias if l == 0 else [
                given[4 * depth + l - 1][:, k * wide : (k + 1) * wide] for k in range(2)
            ]
            norms = [one[0:1, :], two[0:1, :], one[1:2, :], two[1:2, :], two[2:3, :]]
            share = norms[0].shape[1] // owners
            first = sum(
                owned(v, owners, wide, k * share) for k, v in enumerate(norms)
            ) + sum(
                owned(v, owners, wide, 5 * share + k * share // 2) for k, v in enumerate(pair)
            )
            small_rows[3 * l] = first
            small_rows[3 * l + 1] = owned(down[...], owners, wide, scalars[1] * share)
            small_rows[3 * l + 2] = owned(up[...], owners, wide, scalars[1] * 2 * share)
    for ref, offs in zip(pieces, offsets):
        part = size // 2
        for r, off in enumerate(offs):
            i = scalars[0] ^ off
            at = pl.ds(pl.multiple_of(i * size, min(size, 16)), size)
            for s in range(3):
                ref[r, s * size : (s + 1) * size, :] = project[at, s * wide : (s + 1) * wide]
            rows = merge[pl.ds(pl.multiple_of(i * part, min(part, 8)), part), :]
            sides = jnp.concatenate([rows[:, :wide], rows[:, wide:]], axis=0)
            ref[r, 3 * size : 4 * size, :] = sides.astype(LOW)
            if small_rows is not None:
                lines = [small_rows[k, pl.ds(i, 1), :] for k in range(small_rows.shape[0])]
                lines.append(jnp.zeros((16 - len(lines), wide), F32))
                ref[r, 4 * size :, :] = jnp.concatenate(lines, axis=0).astype(LOW)


def stream_pull(part, got, stream, middle_grad, vectors, small):
    first = part[...].astype(F32) + got[...].astype(F32)
    unit, inverse = unit_of(stream[...])
    small[0:1, :] = column_sum(first * unit)
    small[1:2, :] = column_sum(first)
    return middle_grad[...] + norm_pull(first, unit, inverse, vectors[0:1, : first.shape[1]])


def stream_pull_body(
    scalars, part, got, stream, middle_grad, vectors, target, gate, grad, small, *sends
):
    value = stream_pull(part, got, stream, middle_grad, vectors, small)
    grad[...] = value
    low = value.astype(LOW)
    for r, send in enumerate(sends):
        send[...] = dot(slot_marks(scalars, r, target[...], gate[...]), low).astype(LOW)


def last_pull_body(scalars, part, got, stream, middle_grad, vectors, out, small):
    value = stream_pull(part, got, stream, middle_grad, vectors, small)
    rows = value.shape[0] // out.shape[0]
    for i in range(out.shape[0]):
        out[i] = value[i * rows : i * rows + out.shape[1]]


def pack_body(count, ship, scalars, *refs):
    given, packs, held = refs[:8], refs[8 : 8 + count], refs[8 + count :]
    ship.wait([ship(a, b) for a, b in zip(given, held)])
    attend, merge, *smalls = held
    depth, _, size, wide = attend.shape
    for l, pack in enumerate(packs):
        for k in range(3):
            pack[0, k * size : (k + 1) * size, :] = attend[l, k]
        rows = merge[l].astype(F32)
        sides = jnp.concatenate([rows[:, :wide], rows[:, wide:]], axis=0)
        pack[0, 3 * size : 4 * size, :] = sides.astype(LOW)

    def row(*parts):
        total, at = jnp.zeros((1, wide), F32), 0
        for part in parts:
            lane = lax.broadcasted_iota(jnp.int32, (part.shape[1], wide), 1)
            home = lax.broadcasted_iota(jnp.int32, lane.shape, 0) + at
            total = total + dot(part, jnp.where(lane == home, 1.0, 0.0).astype(LOW))
            at += part.shape[1]
        return total

    gain, shift, merge_bias, attend_bias, up_bias, down_bias = smalls
    rows = []
    for l in range(depth):
        norms = [v[l, k : k + 1, :] for v in (gain, shift) for k in range(2)]
        rows.append(
            row(*norms, merge_bias[l : l + 1, :], *(attend_bias[l, k : k + 1, :] for k in range(2)))
        )
        rows.append(row(*(down_bias[l, e : e + 1, :] for e in range(E))))
        rows.append(row(*(up_bias[l, e : e + 1, :] for e in range(E))))
    rows.append(jnp.zeros((16 - 3 * depth, wide), F32))
    packs[0][0, 4 * size :, :] = jnp.concatenate(rows, axis=0).astype(LOW)


def deal_body(layer, ship, scalars, up, down, *chunks):
    size, wide = up.shape[2], down.shape[3]
    for r, chunk in enumerate(chunks):
        e = scalars[1] ^ r
        ship(up.at[layer, e], chunk.at[pl.ds(0, size), :])
        for side in range(2):
            ship(
                down.at[layer, e, pl.ds(side * size, size), :],
                chunk.at[pl.ds(size, size), pl.ds(side * wide, wide)],
            )


def prepare_body(images, scalars, routes, gates, columns, rows_out, gate_rows):
    depth, total, _ = routes.shape
    live = live_rows(scalars, total, images)
    square = lax.broadcasted_iota(jnp.int32, (total, total), 0), lax.broadcasted_iota(
        jnp.int32, (total, total), 1
    )
    earlier = jnp.where(square[0] > square[1], 1.0, 0.0).astype(LOW)
    same = jnp.where(square[0] == square[1], 1.0, 0.0).astype(LOW)
    lane = lax.broadcasted_iota(jnp.int32, (total, 128), 1)
    for l in range(depth):
        picks = [routes[l, :, k : k + 1] for k in range(2)]
        chosen = ((lane == picks[0]) | (lane == picks[1])) & live
        taken = dot(earlier, jnp.where(chosen, 1.0, 0.0).astype(LOW))
        mixed = jnp.zeros((total, 128), F32)
        for k, pick in enumerate(picks):
            slot = jnp.sum(jnp.where(lane == pick, taken, 0.0), axis=1, keepdims=True)
            target = jnp.where(live & (pick >= 0), pick * SLOTS + slot.astype(jnp.int32), -1)
            columns[l, :, k : k + 1] = target
            high = (target + 1) >> 5
            mixed = jnp.where(lane == 3 * k, high.astype(F32), mixed)
            mixed = jnp.where(lane == 3 * k + 1, (target + 1 - (high << 5)).astype(F32), mixed)
            mixed = jnp.where(lane == 3 * k + 2, gates[l, :, k : k + 1], mixed)
        turned = dot_tn(mixed.astype(LOW), same)
        for k in range(2):
            high, low, gate = (turned[3 * k + j : 3 * k + j + 1] for j in range(3))
            rows_out[l, k : k + 1, :] = (high * 32.0 + low).astype(jnp.int32) - 1
            gate_rows[l, k : k + 1, :] = gate


def finish_body(depth, scalars, *refs):
    blocks, attends, outs = refs[: E * depth], refs[E * depth], refs[-10:]
    gain, shift, attend, attend_bias, merge, merge_bias, up, up_bias, down, down_bias = outs
    size, wide = up.shape[2], down.shape[3]
    part, share = size // 2, gain.shape[2]
    small = attends[0, 4 * size : 4 * size + 16, :].astype(F32)
    for l in range(depth):
        base = l * 4 * size + (16 if l else 0)
        for r in range(E):
            e = scalars[1] ^ r
            value = blocks[l * E + r][...].astype(F32)
            up[l, e] = value[:size]
            both = value[size:]
            down[l, e] = jnp.concatenate([both[:, :wide], both[:, wide:]], axis=0)
        for k in range(3):
            at = base + k * size
            attend[l, k] = attends[0, at : at + size, :].astype(F32)
        sides = attends[0, base + 3 * size : base + 4 * size, :].astype(F32)
        merge[l] = jnp.concatenate([sides[:part], sides[part:]], axis=1)
        first, second, third = (small[3 * l + k : 3 * l + k + 1, :] for k in range(3))
        for k in range(2):
            gain[l, k : k + 1, :] = first[:, k * share : (k + 1) * share]
            shift[l, k : k + 1, :] = first[:, (2 + k) * share : (3 + k) * share]
            at = 5 * share + k * share // 2
            attend_bias[l, k : k + 1, :] = first[:, at : at + share // 2]
        merge_bias[l : l + 1, :] = first[:, 4 * share : 5 * share]
        for e in range(E):
            down_bias[l, e : e + 1, :] = second[:, e * share : (e + 1) * share]
            up_bias[l, e : e + 1, :] = third[:, 2 * e * share : 2 * (e + 1) * share]


class Place:
    def __init__(self, count, rows, live):
        self.count = count
        self.me = lax.axis_index("dp").astype(jnp.int32)
        core = lax.axis_index("tensor").astype(jnp.int32)
        self.expert = (self.me >> 2) & 3
        self.near = self.expert ^ jnp.arange(E, dtype=jnp.int32)
        powers = [1 << k for k in range(count.bit_length() - 1)]
        self.powers, self.beyond = powers, [b for b in reversed(powers) if b > 8]
        self.aligned = rows % 16 == 0
        where = self.me if self.aligned else jnp.zeros((), jnp.int32)
        self.scalars = jnp.stack([where, self.expert, core, live, self.me])
        far = doubled([0], self.beyond)
        self.parts = [[f ^ l ^ p for f in far for l in LINE] for p in PLANE]
        self.all = [o for offs in self.parts for o in offs]
        blocks = [f ^ l for f in far for l in LINE]
        middle = len(blocks) // 2
        rounds = [(0, blocks), (1, blocks), (2, blocks), (3, blocks[:middle]), (3, blocks[middle:])]
        self.arrivals = [[b ^ p for b in some] for p, some in rounds]
        self.all_arrivals = [o for offs in self.arrivals for o in offs]
        self.fetched = self.arrivals if self.aligned else [[0]]
        self.offsets = self.parts if self.aligned else [[0]]

    def spread(self, value, offsets):
        return [value] + [swap(value, o, self.count) for o in offsets[1:]]

    def near_of(self, value):
        return [swap(value, p, self.count) for p in (1, 2)]

    def gather(self, value, near, anchor=()):
        half = value.shape[0] // 2
        one, two = after(near, anchor)
        return [value, *near, swap(two[:half], 1, self.count), swap(one[half:], 2, self.count)]

    def reduce_onward(self, pieces):
        own, one, two, far = pieces
        half = far.shape[0] // 2
        onward = swap(far[:half], 1, self.count), swap(far[half:], 2, self.count)
        two = jnp.concatenate([add_low(two[:half], onward[0]), two[half:]], axis=0)
        one = jnp.concatenate([one[:half], add_low(one[half:], onward[1])], axis=0)
        return own, one, two

    def reduce(self, own, one, two):
        return add_low(own, swap(one, 1, self.count), swap(two, 2, self.count))

    def deal(self, chunks):
        return [chunks[0]] + [swap(chunks[r], LINE[r], self.count) for r in range(1, E)]

    def exchange(self, chunks, hold=()):
        return self.crossed(self.deal(chunks), hold)

    def crossed(self, own, hold=()):
        return own + [cross(c) for c in (after(own, hold) if hold else own)]

    def doubled(self, value):
        for bit in self.beyond:
            value = jnp.concatenate([value, swap(value, bit, self.count)], axis=0)
        return value

    def halved(self, value):
        for bit in reversed(self.beyond):
            half = value.shape[0] // 2
            value = add_low(value[:half], swap(value[half:], bit, self.count))
        return value


def pack_small(gain, shift, merge, attend, up, down):
    depth, _, share = gain.shape
    spare = jnp.zeros((depth, 2 * share), LOW)
    first = [gain, shift, merge, attend, spare]
    first = jnp.concatenate([p.reshape(depth, -1) for p in first], axis=1)
    second = jnp.pad(down.reshape(depth, -1), ((0, 0), (0, 4 * share)))
    rows = jnp.stack([first, second, up.reshape(depth, -1)], axis=1).reshape(3 * depth, -1)
    return jnp.pad(rows, ((0, -(3 * depth) % 16), (0, 0)))[None]


def pack_attend(attend, merge):
    count, kinds, depth, wide = attend.shape
    rows = attend.reshape(count, 3 * depth, wide)
    return jnp.concatenate([rows, merge[:, :, :wide], merge[:, :, wide:]], axis=1)


def unpack_attend(pack):
    count, rows, wide = pack.shape
    depth = rows // 4
    attend = pack[:, : 3 * depth].reshape(count, 3, depth, wide)
    sides = pack[:, 3 * depth :]
    return attend, jnp.concatenate([sides[:, : depth // 2], sides[:, depth // 2 :]], axis=2)


def whole_attend(pack):
    attend, merge = unpack_attend(pack)
    attend = jnp.swapaxes(attend, 0, 1)
    attend = attend.reshape(3, -1, attend.shape[-1])
    return pack_attend(attend[None], merge.reshape(1, -1, merge.shape[-1]))


def split_attend(pack, count):
    attend, merge = unpack_attend(pack)
    attend = jnp.swapaxes(attend.reshape(3, count, -1, attend.shape[-1]), 0, 1)
    return pack_attend(attend, merge.reshape(count, -1, merge.shape[-1]))


def fetch_column(place, value):
    blocks = place.spread(place.doubled(value), LINE)
    value = jnp.stack(blocks, axis=1)
    return value.reshape((-1,) + value.shape[2:])


def attend_pieces_of(place, pieces):
    if place.aligned:
        return pieces
    return [whole_attend(ordered(jnp.concatenate(pieces), place.all_arrivals, place.me))]


def chunks_of(place, layer, up_weight, down_weight):
    depth, hidden = up_weight.shape[2:]
    if place.aligned:
        return call(
            functools.partial(deal_body, layer),
            [((2 * depth, hidden), LOW)] * E,
            place.scalars,
            up_weight,
            down_weight,
            stored=(0, 1),
        )
    sent = []
    for r in range(E):
        one = lax.dynamic_index_in_dim(up_weight[layer], place.near[r], 0, False)
        two = lax.dynamic_index_in_dim(down_weight[layer], place.near[r], 0, False)
        two = jnp.concatenate([two[:depth], two[depth:]], axis=1)
        sent.append(jnp.concatenate([one, two], axis=0))
    return sent


def fetch_base(place, chunks):
    return place.doubled(jnp.stack(place.deal(chunks)))


def expert_pieces_of(place, pieces):
    if place.aligned:
        return pieces
    pack = ordered(jnp.concatenate(pieces), place.all_arrivals, place.me)
    depth, wide = pack.shape[1] // 2, pack.shape[2] // 2
    up, down = pack[:, :depth], pack[:, depth:]
    down = jnp.concatenate([down[..., :wide], down[..., wide:]], axis=1).reshape(2, -1, wide)
    down = jnp.concatenate([down[0], down[1]], axis=1)
    return [jnp.concatenate([up.reshape(-1, up.shape[-1]), down])[None]]


def add_low(*terms):
    return sum(t.astype(F32) for t in terms).astype(LOW)


def spread_expert(place, pieces):
    if place.aligned:
        return pieces
    pack = pieces[0][0]
    depth, wide = pack.shape[0] // 2, pack.shape[1] // 2
    up = pack[:depth].reshape(place.count, -1, 2 * wide)
    down = jnp.concatenate([pack[depth:, :wide], pack[depth:, wide:]], axis=0)
    down = down.reshape(place.count, 2, -1, wide)
    down = jnp.concatenate([down[:, 0], down[:, 1]], axis=-1)
    value = relative(jnp.concatenate([up, down], axis=1), place.all, place.me)
    return list(value.reshape((len(PLANE), -1) + value.shape[1:]))


def finish_expert(place, blocks):
    pack = jnp.take(jnp.stack(blocks), place.near, axis=0, mode="clip").astype(F32)
    depth, wide = pack.shape[1] // 2, pack.shape[2] // 2
    low = pack[:, depth:]
    return pack[:, :depth], jnp.concatenate([low[..., :wide], low[..., wide:]], axis=1)


def spread_plane(place, full):
    value = relative(split_attend(full, place.count), place.all, place.me)
    return list(value.reshape((len(PLANE), -1) + value.shape[1:]))


def fold_column(place, value):
    value = place.halved(value)
    got = [swap(value[r : r + 1], LINE[r], place.count) for r in range(1, len(LINE))]
    return add_low(value[:1], *got)


def finish_attend(value):
    attend, merge = unpack_attend(value)
    return attend[0].astype(F32), merge[0].astype(F32)


def on_device(
    count,
    inputs,
    image_count,
    routes,
    gates,
    norm_gain,
    norm_shift,
    attend_weight,
    attend_bias,
    merge_weight,
    merge_bias,
    up_weight,
    up_bias,
    down_weight,
    down_bias,
    cotangent,
):
    images, length, width = inputs.shape
    depth = routes.shape[0]
    wide = attend_weight.shape[-1]
    hidden = up_weight.shape[-1]
    heads = wide // HD
    place = Place(count, up_weight.shape[2], image_count[0])
    scalars = place.scalars
    rows = -(-length // 16) * 16
    total = images * rows
    half = E * HALF
    size = width // count if place.aligned else width

    def padded(value, fill=0):
        spare = [(0, 0)] * value.ndim
        spare[-2] = (0, rows - length)
        value = jnp.pad(value, spare, constant_values=fill)
        return value.reshape(value.shape[:-3] + (total, value.shape[-1]))

    chunk = ((HALF, width), LOW)
    wide_rows = ((total, width), F32)
    low_rows = ((total, width), LOW)
    wide_half, low_slots = ((half, width), F32), ((2 * half, width), LOW)
    low_half = ((half, width), LOW)
    low_hidden = ((2 * half, hidden), LOW)
    low_project = ((total, 3 * wide), LOW)
    attend_scratch = [((width, 3 * wide), LOW), ((wide, width), F32)]
    expert_scratch = [((width, hidden), LOW), ((hidden, width), LOW)]

    smalls = (norm_gain, norm_shift, merge_bias, attend_bias, up_bias, down_bias)
    small = []
    if place.aligned:
        given = (attend_weight, merge_weight, *smalls)
        sizes = [4 * size + (16 if l == 0 else 0) for l in range(depth)]
        packs = call(
            functools.partial(pack_body, depth),
            [((1, n, wide), LOW) for n in sizes],
            scalars,
            *given,
            scratch=[(g.shape, LOW) for g in given],
            stored=range(len(given)),
        )
    else:
        packs = [pack_attend(attend_weight[l][None], merge_weight[l][None]) for l in range(depth)]
        small = place.spread(fetch_column(place, pack_small(*smalls)), PLANE)
        small = [ordered(jnp.concatenate(small), place.all, place.me)]
    column = fetch_column(place, packs[0])
    chunks = chunks_of(place, 0, up_weight, down_weight)
    base = fetch_base(place, after(chunks, column))
    near = place.near_of(column)
    attend_pieces = attend_pieces_of(place, place.gather(column, near))
    target, target_rows, gate_rows = call(
        functools.partial(prepare_body, images),
        [((depth, total, 2), jnp.int32)]
        + [((depth, 2, total), jnp.int32), ((depth, 2, total), F32)],
        scalars,
        *after((padded(routes, -1), padded(gates)), column),
    )
    gate = padded(gates)
    stream = padded(after(inputs, column))
    states = []
    back, first_sends = None, ()
    for l in range(depth):
        more = l + 1 < depth
        base = after(base, attend_pieces)
        near = place.near_of(base)
        kinds = [low_rows, low_project, ((images * heads, rows, rows), LOW), ((total, wide), LOW)]
        body = functools.partial(
            attend_body, length, images, size, place.fetched, l > 0, not place.aligned
        )
        if l == 0:
            table = [((count, 16, wide), LOW)] if place.aligned else []
            part, vectors, *keeps = call(
                body,
                [low_rows, ((depth, 8, hidden), F32)],
                scalars,
                stream,
                *small,
                *attend_pieces,
                saved=kinds,
                scratch=kinds + attend_scratch + table,
                before=(base,),
                us=LONG,
            )
            stream_kept = stream
        else:
            stream, part, stream_kept, *keeps = call(
                body,
                [wide_rows, low_rows],
                scalars,
                middle,
                *back,
                target[l - 1],
                gate[l - 1],
                vectors[l],
                *attend_pieces,
                saved=[wide_rows] + kinds,
                scratch=kinds + attend_scratch,
                before=first_sends,
                us=LONG,
            )
        normed, projected, probs, attended = keeps
        if more:
            chunks = chunks_of(place, l + 1, up_weight, down_weight)
            next_base = fetch_base(place, after(chunks, base))
        middle, *sends, middle_kept = call(
            middle_body,
            [wide_rows] + [chunk] * E,
            scalars,
            stream,
            part,
            cross(part),
            vectors[l],
            target_rows[l],
            saved=[wide_rows],
            before=(next_base,) if more else (),
        )
        own = place.deal(sends)
        expert_pieces = expert_pieces_of(place, place.gather(base, near, own[2]))
        taken = place.crossed(own)
        kept = attend_pieces
        if more:
            base = next_base
            column = fetch_column(place, after(packs[l + 1], own))
        others, result, active, slope, taken_rows = call(
            functools.partial(expert_body, place.fetched, not more),
            [low_half] if more else [],
            scalars,
            *taken,
            vectors[l],
            *expert_pieces,
            saved=([] if more else [low_half]) + [wide_half, low_hidden, low_hidden, low_slots],
            scratch=[wide_half, low_hidden, low_hidden, low_slots]
            + expert_scratch
            + ([] if more else [low_half]),
            us=LONG,
        )
        states.append(
            (stream_kept, middle_kept, normed, projected, probs, attended, taken_rows, active, slope)
            + (kept, expert_pieces)
        )
        if more:
            near = place.near_of(after(column, others))
            sends = call(
                total_body,
                [chunk] * E,
                scalars,
                result,
                cross(others),
                vectors[l],
                before=(column,),
            )
            attend_pieces = attend_pieces_of(place, place.gather(column, near, sends))
            back = place.exchange(sends)
            if l + 2 == depth:
                grad, *first_sends = call(
                    functools.partial(first_grad_body, images),
                    [wide_rows] + [chunk] * E,
                    scalars,
                    padded(after(cotangent, sends)),
                    target_rows[-1],
                    gate_rows[-1],
                )

    last, last_others = result, others
    slot_grad = place.crossed(place.deal(after(first_sends, own)), (result,))
    blocks = [None] * depth
    attend_sums, smalls, biases = [None] * depth, [None] * depth, [None] * depth
    waiting, before_expert, before_total, before_grad = [], (), (), ()
    for l in reversed(range(depth)):
        stream, middle, normed, projected, probs, attended, taken, active, slope = states[l][:9]
        attend_pieces, expert_pieces = states[l][9:]
        others, up_b, down_b, result, pulled, slot_rows = call(
            functools.partial(expert_pull_body, place.fetched),
            [low_half, ((1, hidden), F32), ((1, width), F32)],
            scalars,
            *slot_grad,
            slope,
            *expert_pieces,
            saved=[wide_half, low_hidden, low_slots],
            scratch=[wide_half, low_hidden, low_slots, low_hidden] + expert_scratch,
            stored=(2 * E,),
            us=LONG,
        )
        sends = call(
            total_body,
            [chunk] * E,
            scalars,
            result,
            cross(others),
        )
        own = place.deal(sends)
        before_attend = ()
        if waiting:
            attend_sum = place.reduce(*after(before_total, sends))
            before_attend = (attend_sum,)
            waiting.append(attend_sum)
        active, pulled_late = after((active, pulled), own[1])
        pieces = call(
            functools.partial(expert_grad_body, place.offsets),
            [((len(o), 2 * size, hidden), LOW) for o in place.offsets],
            scalars,
            slot_rows,
            active,
            taken,
            pulled_late,
            scratch=expert_scratch + [low_slots, low_hidden, low_slots, low_hidden],
            stored=range(4),
            us=7,
        )
        back = place.crossed(own, pieces)
        expert_onward = place.reduce_onward(spread_expert(place, pieces))
        if waiting:
            done, value, total_sum = waiting
            blocks[done] = place.deal(list(place.halved(after(value, back))))
            before_grad = blocks[done]
            waiting = [done, total_sum]
        pull_kinds = [wide_rows, low_rows, low_project]
        first, small_two, middle_grad, merged, pulled = call(
            functools.partial(attend_pull_body, images, size, place.fetched),
            [low_rows, ((3, width), F32)],
            scalars,
            *back,
            target[l],
            middle,
            grad,
            vectors[l],
            probs,
            projected,
            *attend_pieces,
            saved=pull_kinds,
            scratch=pull_kinds + attend_scratch,
            before=before_attend,
            us=LONG,
        )
        got = cross(first)
        if l > 0:
            grad, small_one, *sends = call(
                stream_pull_body,
                [wide_rows, ((2, width), F32)] + [chunk] * E,
                scalars,
                first,
                got,
                stream,
                middle_grad,
                vectors[l],
                target_rows[l - 1],
                gate_rows[l - 1],
                before=expert_onward,
            )
            own = place.deal(sends)
            slot_grad = place.crossed(own)
            pulled_late = after(pulled, own[3])
        else:
            input_grad, small_one = call(
                last_pull_body,
                [(inputs.shape, F32), ((2, width), F32)],
                scalars,
                first,
                got,
                stream,
                middle_grad,
                vectors[l],
                before=expert_onward,
            )
            pulled_late = pulled
        smalls[l] = (small_one, small_two, up_b, down_b)
        extra = []
        joint = place.aligned and l == 0
        if joint:
            extra = [v for some in smalls for v in some] + biases[1:]
        height = 4 * size + (16 if joint else 0)
        *pieces, biases[l] = call(
            functools.partial(attend_grad_body, size, place.offsets),
            [((len(o), height, wide), LOW) for o in place.offsets] + [((1, width), F32)],
            scalars,
            normed,
            attended,
            merged,
            pulled_late,
            *extra,
            scratch=([((3 * depth, count, wide), F32)] if joint else []) + attend_scratch,
            before=before_grad,
            us=4 if l else LONG,
        )
        if not place.aligned:
            pieces = spread_plane(place, pieces[0])
        if l == 0:
            ends = after((last, last_others), before_grad)
            ends = call(
                total_body, [chunk] * E, scalars, ends[0], cross(ends[1]), vectors[-1]
            )
            ends = place.deal(ends)
            pieces = after(pieces, ends)
        before_total = place.reduce_onward(pieces)
        expert_sum = place.reduce(*expert_onward)
        before_expert = (expert_sum,)
        if waiting:
            done, total_sum = waiting
            attend_sums[done] = total_sum
        waiting = [l, expert_sum]
    blocks[0] = place.deal(list(place.halved(expert_sum)))
    attend_sums[0] = place.reduce(*after(before_total, expert_sum))
    heights = [v.shape[1] for v in attend_sums]
    attend_grads = fold_column(place, jnp.concatenate(attend_sums, axis=1))
    starts = [sum(heights[:l]) for l in range(depth)]
    ends = after(ends, pieces)
    (output,) = call(
        output_body,
        [(inputs.shape, F32)],
        scalars,
        states[-1][1],
        *ends,
        *map(cross, ends),
        target[-1],
        gate[-1],
    )
    if place.aligned:
        grads = (norm_gain, norm_shift, attend_weight, attend_bias, merge_weight, merge_bias)
        grads += (up_weight, up_bias, down_weight, down_bias)
        return output, input_grad, *call(
            functools.partial(finish_body, depth),
            [(g.shape, F32) for g in grads],
            scalars,
            *[b for layer in blocks for b in layer],
            attend_grads,
        )

    tables = []
    at_expert = jnp.arange(E, dtype=jnp.int32)[:, None, None] == place.expert
    for (small_one, small_two, up_b, down_b), bias in zip(smalls, biases):
        expert_rows = jnp.concatenate([up_b.reshape(-1, width), down_b], axis=0)
        expert_rows = jnp.where(at_expert, expert_rows[None], 0.0).reshape(-1, width)
        tables.append(jnp.concatenate([small_one, small_two, bias, expert_rows], axis=0))
    small = jnp.stack(tables)
    for bit in place.beyond:
        small = small + swap(small, bit, count)
    for offsets in (PLANE, LINE):
        terms = place.spread(small, offsets)
        small = (terms[0] + terms[1]) + (terms[2] + terms[3])

    def mine(value, size):
        return lax.dynamic_slice_in_dim(value, place.me * size, size, value.ndim - 1)

    share = norm_gain.shape[-1]
    gain_grad = jnp.stack([small[:, 0], small[:, 2]], axis=1)
    shift_grad = jnp.stack([small[:, 1], small[:, 3]], axis=1)
    attend_b = small[:, 5].reshape(depth, 2, wide)
    expert_rows = small[:, 6:].reshape(depth, E, -1, width)
    up_b = expert_rows[:, :, :-1].reshape(depth, E, hidden)
    parts = [attend_grads[:, a : a + n] for a, n in zip(starts, heights)]
    finished = [finish_expert(place, b) + finish_attend(a) for b, a in zip(blocks, parts)]
    up_grad, down_grad, attend_grad, merge_grad = (
        jnp.stack([f[k] for f in finished]) for k in range(4)
    )
    return (
        output,
        input_grad,
        mine(gain_grad, share),
        mine(shift_grad, share),
        attend_grad,
        mine(attend_b, attend_bias.shape[-1]),
        merge_grad,
        mine(small[:, 4], share),
        up_grad,
        mine(up_b, up_bias.shape[-1]),
        down_grad,
        mine(expert_rows[:, :, -1], share),
    )


def solution(mesh):
    placed = (
        P("dp", None, None),
        P("dp"),
        P(None, "dp", None, None),
        P(None, "dp", None, None),
        P(None, None, "dp"),
        P(None, None, "dp"),
        P(None, None, "dp", "tensor"),
        P(None, None, ("tensor", "dp")),
        P(None, ("tensor", "dp"), None),
        P(None, "dp"),
        P(None, None, "dp", "tensor"),
        P(None, None, ("tensor", "dp")),
        P(None, None, ("tensor", "dp"), None),
        P(None, None, "dp"),
        P("dp", None, None),
    )
    return jax.shard_map(
        functools.partial(on_device, mesh.shape["dp"]),
        mesh=mesh,
        in_specs=placed,
        out_specs=(
            P("dp", None, None),
            P("dp", None, None),
            P(None, None, "dp"),
            P(None, None, "dp"),
            P(None, None, "dp", "tensor"),
            P(None, None, ("tensor", "dp")),
            P(None, ("tensor", "dp"), None),
            P(None, "dp"),
            P(None, None, "dp", "tensor"),
            P(None, None, ("tensor", "dp")),
            P(None, None, ("tensor", "dp"), None),
            P(None, None, "dp"),
        ),
        check_vma=False,
    )
```

```python
import functools

import jax
import jax.numpy as jnp
from jax import lax
from jax.experimental import pallas as pl
from jax.experimental.pallas import tpu as pltpu
from jax.sharding import PartitionSpec as P

HD = 64
E = 4
SLOTS = 256
HALF = SLOTS // 2
PLANE = (0, 1, 2, 3)
LINE = (0, 4, 8, 12)
ROWS = 256
STEP = 512
LONG = 60
VMEM = 32 * 2**20
LOW = jnp.bfloat16
F32 = jnp.float32
SCALE = HD ** (-0.5)


def dot(left, right):
    return jnp.dot(left, right, preferred_element_type=F32)


def dot_nt(left, right):
    return lax.dot_general(left, right, (((1,), (1,)), ((), ())), preferred_element_type=F32)


def dot_tn(left, right):
    return lax.dot_general(left, right, (((0,), (0,)), ((), ())), preferred_element_type=F32)


def swap(value, bit, count):
    return lax.ppermute(value, "dp", [(i, i ^ bit) for i in range(count)])


def after(value, *anchors):
    return lax.optimization_barrier((value, anchors))[0]


def cross(value):
    return lax.ppermute(value, "tensor", [(0, 1), (1, 0)])


def doubled(offsets, bits):
    for bit in bits:
        offsets = offsets + [o ^ bit for o in offsets]
    return offsets


def ordered(value, offsets, me):
    where = jnp.asarray([offsets.index(i) for i in range(len(offsets))], jnp.int32)
    index = where[jnp.arange(len(offsets), dtype=jnp.int32) ^ me]
    return jnp.take(value, index, axis=0, mode="clip")


def relative(value, offsets, me):
    return jnp.take(value, jnp.asarray(offsets, jnp.int32) ^ me, axis=0, mode="clip")


def call(kernel, outs, scalars, *args, saved=(), scratch=(), before=(), stored=(), us=0):
    memory = pl.BlockSpec(memory_space=pltpu.VMEM)

    def body(*refs):
        ships = saved or stored
        sems = refs[-1] if ships else None
        started, settled = [], []

        def ship(source, target):
            copy = pltpu.make_async_copy(source, target, sems.at[len(started)])
            copy.start()
            started.append(copy)
            return copy

        def wait(copies):
            for copy in copies:
                copy.wait()
            settled.extend(copies)

        ship.wait = wait
        if ships:
            kernel(ship, *refs[:-1])
        else:
            kernel(*refs)
        for copy in started:
            if not any(copy is done for done in settled):
                copy.wait()

    if before:
        scalars = after(scalars, *before)
    args = [
        pltpu.with_memory_space_constraint(a, pltpu.HBM) if k in stored else a
        for k, a in enumerate(args)
    ]
    return pl.pallas_call(
        body,
        out_shape=[jax.ShapeDtypeStruct(shape, kind) for shape, kind in outs]
        + [pltpu.HBM(shape, kind) for shape, kind in saved],
        in_specs=[pl.BlockSpec(memory_space=pltpu.SMEM)]
        + [pl.BlockSpec(memory_space=pltpu.HBM) if k in stored else memory for k in range(len(args))],
        out_specs=[memory] * len(outs) + [pl.BlockSpec(memory_space=pltpu.HBM)] * len(saved),
        scratch_shapes=[pltpu.VMEM(shape, kind) for shape, kind in scratch]
        + ([pltpu.SemaphoreType.DMA((24,))] if saved or stored else []),
        compiler_params=pltpu.CompilerParams(vmem_limit_bytes=VMEM),
        cost_estimate=pl.CostEstimate(
            flops=us * 10**9, transcendentals=0, bytes_accessed=us * 10**3
        ),
    )(scalars, *args)


def unit_of(stream):
    center = stream - jnp.mean(stream, axis=-1, keepdims=True)
    inverse = lax.rsqrt(jnp.mean(center * center, axis=-1, keepdims=True) + 1e-06)
    return center * inverse, inverse


def norm_pull(grad, unit, inverse, gain):
    scaled = grad * gain
    return inverse * (
        scaled
        - jnp.mean(scaled, axis=-1, keepdims=True)
        - unit * jnp.mean(scaled * unit, axis=-1, keepdims=True)
    )


def column_sum(value):
    return jnp.sum(value, axis=0, keepdims=True)


def place_attend(where, size, pieces, offsets, project, merge):
    for ref, offs in zip(pieces, offsets):
        wide, part = ref.shape[2], size // 2
        for r, off in enumerate(offs):
            i = where ^ off
            at = pl.ds(pl.multiple_of(i * size, min(size, 16)), size)
            for s in range(3):
                project[at, s * wide : (s + 1) * wide] = ref[r, s * size : (s + 1) * size, :]
            sides = ref[r, 3 * size : 4 * size, :].astype(F32)
            at = pl.ds(pl.multiple_of(i * part, min(part, 8)), part)
            merge[at, :wide] = sides[:part]
            merge[at, wide:] = sides[part:]


def place_expert(where, pieces, offsets, up, down):
    for ref, offs in zip(pieces, offsets):
        size, wide = ref.shape[1] // 2, ref.shape[2] // 2
        for r, off in enumerate(offs):
            i = where ^ off
            up[pl.ds(pl.multiple_of(i * size, min(size, 16)), size), :] = ref[r, :size, :]
            at = pl.multiple_of(i * 2 * size, min(size, 16))
            down[pl.ds(at, size), :] = ref[r, size:, :wide]
            down[pl.ds(at + size, size), :] = ref[r, size:, wide:]


def rows_of(chunks):
    return jnp.concatenate([c[...] for c in chunks], axis=0)


def slot_marks(scalars, r, target, gate):
    base = (scalars[1] ^ r) * SLOTS + scalars[2] * HALF
    slots = lax.broadcasted_iota(jnp.int32, (HALF, target.shape[1]), 0) + base
    first, second = slots == target[0:1], slots == target[1:2]
    if gate is None:
        return jnp.where(first | second, 1.0, 0.0).astype(LOW)
    weight = jnp.where(first, gate[0:1], 0.0) + jnp.where(second, gate[1:2], 0.0)
    return weight.astype(LOW)


def row_marks(slots, target, gate):
    first, second = target[:, 0:1] == slots, target[:, 1:2] == slots
    if gate is None:
        return jnp.where(first | second, 1.0, 0.0).astype(LOW)
    weight = jnp.where(first, gate[:, 0:1], 0.0) + jnp.where(second, gate[:, 1:2], 0.0)
    return weight.astype(LOW)


def combined(scalars, target, gate, chunks):
    marks = []
    for h in range(2):
        for r in range(E):
            base = (scalars[1] ^ r) * SLOTS + (scalars[2] ^ h) * HALF
            slots = lax.broadcasted_iota(jnp.int32, (1, HALF), 1) + base
            marks.append(row_marks(slots, target, gate))
    return dot(jnp.concatenate(marks, axis=1), rows_of(chunks))


def owned(vector, owners, wide, at):
    count = vector.shape[1]
    share = count // owners
    lane = lax.broadcasted_iota(jnp.int32, (owners, count), 1)
    start = lax.broadcasted_iota(jnp.int32, (owners, count), 0) * share
    mine = jnp.where((lane >= start) & (lane < start + share), vector, 0.0).astype(LOW)
    lane = lax.broadcasted_iota(jnp.int32, (count, 128), 0)
    turn = jnp.floor((lane.astype(F32) + 0.5) * (1.0 / share)).astype(jnp.int32)
    home = lane - turn * share == lax.broadcasted_iota(jnp.int32, (count, 128), 1)
    packed = dot(mine, jnp.where(home, 1.0, 0.0).astype(LOW)).astype(LOW)
    lane = lax.broadcasted_iota(jnp.int32, (128, wide), 0)
    home = (lane + at == lax.broadcasted_iota(jnp.int32, (128, wide), 1)) & (lane < share)
    return dot(packed, jnp.where(home, 1.0, 0.0).astype(LOW))


def join_vectors(scalars, small, vectors):
    owners = small.shape[0]

    def joined(part):
        wide = part.shape[1]
        lane = lax.broadcasted_iota(jnp.int32, (wide, owners * wide), 1)
        turn = jnp.floor((lane.astype(F32) + 0.5) * (1.0 / wide)).astype(jnp.int32)
        place = lane - turn * wide == lax.broadcasted_iota(jnp.int32, lane.shape, 0)
        spread = dot(part.astype(LOW), jnp.where(place, 1.0, 0.0).astype(LOW))
        start = lax.broadcasted_iota(jnp.int32, spread.shape, 0) * wide
        lane = lax.broadcasted_iota(jnp.int32, spread.shape, 1)
        return column_sum(jnp.where((lane >= start) & (lane < start + wide), spread, 0.0))

    share = small.shape[2] // 8
    half = share // 2
    expert = scalars[1]
    for l in range(vectors.shape[0]):
        first, second, third = (small[:, 3 * l + k, :] for k in range(3))
        parts = [first[:, k * share : (k + 1) * share] for k in range(5)]
        for k, part in enumerate(parts):
            vectors[l, k : k + 1, : owners * share] = joined(part)
        at = 5 * share
        query, values = (joined(first[:, at + k * half : at + (k + 1) * half]) for k in range(2))
        vectors[l, 5:6, : 3 * owners * half] = jnp.concatenate(
            [query, jnp.zeros_like(query), values], axis=1
        )
        up = sum(
            jnp.where(expert == e, third[:, 2 * e * share : 2 * (e + 1) * share], 0.0)
            for e in range(E)
        )
        vectors[l, 6:7, :] = joined(up)
        down = sum(
            jnp.where(expert == e, second[:, e * share : (e + 1) * share], 0.0) for e in range(E)
        )
        vectors[l, 7:8, : owners * share] = joined(down)


def live_rows(scalars, rows, images):
    return lax.broadcasted_iota(jnp.int32, (rows, 1), 0) < scalars[3] * (rows // images)


def attend_body(length, images, size, offsets, from_slots, split, ship, *refs):
    count = len(offsets)
    scalars, refs = refs[0], refs[1:]
    if from_slots:
        middle, *back = refs[: 1 + 2 * E]
        target, gate, vectors = refs[1 + 2 * E : 4 + 2 * E]
        refs = refs[4 + 2 * E :]
    else:
        stream_in, refs = refs[0], refs[1:]
        if split:
            small, refs = refs[0], refs[1:]
    pieces, refs = refs[:count], refs[count:]
    if from_slots:
        stream_out, partial, stream_kept, *refs = refs
    else:
        partial, all_vectors, *refs = refs
        vectors = all_vectors.at[0]
    kept, (normed, projected, probs, attended, project, merge, *rest) = refs[:4], refs[4:]
    place_attend(scalars[0], size, pieces, offsets, project, merge)
    if not from_slots:
        if not split:
            (small,) = rest
            for ref, offs in zip(pieces, offsets):
                for r, off in enumerate(offs):
                    small[scalars[0] ^ off] = ref[r, 4 * size :, :]
        join_vectors(scalars, small[...].astype(F32), all_vectors)
    if from_slots:
        stream = middle[...] + combined(scalars, target[...], gate[...], back)
        stream_out[...] = stream
        ship(stream_out, stream_kept)
    else:
        stream = stream_in[...]
    unit, inverse = unit_of(stream)
    width = stream.shape[1]
    normed[...] = (unit * vectors[0:1, :width] + vectors[2:3, :width]).astype(LOW)
    ship(normed, kept[0])
    bias = vectors[5:6, : project.shape[1]]
    projected[...] = (dot(normed[...], project[...]) + bias).astype(LOW)
    ship(projected, kept[1])
    rows = stream.shape[0] // images
    wide = merge.shape[0]
    heads = wide // HD
    keep = lax.broadcasted_iota(jnp.int32, (rows, rows), 1) < length
    for i in range(images):
        span = slice(i * rows, (i + 1) * rows)
        for h in range(heads):
            query = projected[span, h * HD : (h + 1) * HD]
            keys = projected[span, wide + h * HD : wide + (h + 1) * HD]
            values = projected[span, 2 * wide + h * HD : 2 * wide + (h + 1) * HD]
            scores = jnp.where(keep, dot_nt(query, keys) * SCALE, -1e30)
            raised = jnp.exp(scores - jnp.max(scores, axis=-1, keepdims=True))
            prob = raised / jnp.sum(raised, axis=-1, keepdims=True)
            prob_low = prob.astype(LOW)
            probs[i * heads + h] = prob_low
            attended[span, h * HD : (h + 1) * HD] = dot(prob_low, values).astype(LOW)
        ship(probs.at[pl.ds(i * heads, heads)], kept[2].at[pl.ds(i * heads, heads)])
    ship(attended, kept[3])
    partial[...] = dot(attended[...], merge[...].astype(LOW)).astype(LOW)


def middle_body(ship, scalars, stream, part, got, vectors, target, middle, *refs):
    sends, kept = refs[:E], refs[E]
    width = stream.shape[1]
    gain, shift, bias = (vectors[k : k + 1, :width] for k in (1, 3, 4))
    value = stream[...] + part[...].astype(F32) + got[...].astype(F32) + bias
    middle[...] = value
    ship(middle, kept)
    unit, inverse = unit_of(value)
    normed = (unit * gain + shift).astype(LOW)
    for r, send in enumerate(sends):
        send[...] = dot(slot_marks(scalars, r, target[...], None), normed).astype(LOW)


def expert_body(offsets, last, ship, scalars, *refs):
    count = len(offsets)
    chunks, vectors, refs = refs[: 2 * E], refs[2 * E], refs[2 * E + 1 :]
    pieces, refs = refs[:count], refs[count:]
    if last:
        others_kept, refs = refs[0], refs[1:]
        others, refs = refs[-1], refs[:-1]
    else:
        others, refs = refs[0], refs[1:]
    result_kept, active_kept, slope_kept, rows_kept, result, active, slope, rows, up, down = refs
    place_expert(scalars[0], pieces, offsets, up, down)
    bias = vectors[6:7, :]
    for k in reversed(range(0, 2 * E, 2)):
        at = k * HALF
        span = pl.ds(at, 2 * HALF)
        rows[span, :] = rows_of(chunks[k : k + 2])
        ship(rows.at[span], rows_kept.at[span])
        hidden = dot(rows[span, :], up[...]) + bias
        square = hidden * hidden
        bent = jnp.tanh(0.7978845608028654 * hidden * (1.0 + 0.044715 * square))
        low = 0.5 * (1.0 + bent)
        act = (hidden * low).astype(LOW)
        active[span, :] = act
        slope[span, :] = (
            low
            + hidden
            * (0.5 * 0.7978845608028654)
            * (1.0 - bent * bent)
            * (1.0 + 3 * 0.044715 * square)
        ).astype(LOW)
        ship(active.at[span], active_kept.at[span])
        ship(slope.at[span], slope_kept.at[span])
        out = dot(act, down[...])
        if k < E:
            result[span, :] = out
            ship(result.at[span], result_kept.at[span])
        else:
            span = pl.ds(at - E * HALF, 2 * HALF)
            others[span, :] = out.astype(LOW)
            if last:
                ship(others.at[span], others_kept.at[span])


def total_body(scalars, part, *refs):
    got, sends = refs[:-E], refs[-E:]
    vectors = None
    if got[-1].dtype == F32:
        got, vectors = got[:-1], got[-1]
    for r, send in enumerate(sends):
        span = slice(r * HALF, (r + 1) * HALF)
        value = part[span, :] + got[0][span, :].astype(F32)
        if vectors is not None:
            value = value + vectors[7:8, : value.shape[1]]
        send[...] = value.astype(LOW)


def output_body(scalars, middle, *refs):
    chunks, (target, gate, out) = refs[: 2 * E], refs[2 * E :]
    value = middle[...] + combined(scalars, target[...], gate[...], chunks)
    value = jnp.where(live_rows(scalars, value.shape[0], out.shape[0]), value, 0.0)
    rows = value.shape[0] // out.shape[0]
    for i in range(out.shape[0]):
        out[i] = value[i * rows : i * rows + out.shape[1]]


def first_grad_body(images, scalars, cotangent, target, gate, grad, *sends):
    value = jnp.where(live_rows(scalars, grad.shape[0], images), cotangent[...], 0.0)
    grad[...] = value
    low = value.astype(LOW)
    for r, send in enumerate(sends):
        send[...] = dot(slot_marks(scalars, r, target[...], gate[...]), low).astype(LOW)


def expert_pull_body(offsets, ship, scalars, *refs):
    count = len(offsets)
    chunks, slope, refs = refs[: 2 * E], refs[2 * E], refs[2 * E + 1 :]
    pieces, others, refs = refs[:count], refs[count], refs[count + 1 :]
    up_bias, down_bias, result_kept, hidden_kept, rows_kept, *refs = refs
    result, hidden_grad, rows, slope_here, up, down = refs
    spans = [pl.ds(k * HALF, 2 * HALF) for k in range(0, 2 * E, 2)]
    loads = [ship(slope.at[s], slope_here.at[s]) for s in reversed(spans)][::-1]
    place_expert(scalars[0], pieces, offsets, up, down)
    total = jnp.zeros(up_bias.shape, F32)
    total_down = jnp.zeros(down_bias.shape, F32)
    for k in reversed(range(0, 2 * E, 2)):
        span = pl.ds(k * HALF, 2 * HALF)
        value = rows_of(chunks[k : k + 2])
        rows[span, :] = value
        ship(rows.at[span], rows_kept.at[span])
        total_down = total_down + column_sum(value.astype(F32))
        ship.wait([loads[k // 2]])
        low = (dot_nt(value, down[...]) * slope_here[span, :].astype(F32)).astype(LOW)
        hidden_grad[span, :] = low
        ship(hidden_grad.at[span], hidden_kept.at[span])
        total = total + column_sum(low.astype(F32))
        out = dot_nt(low, up[...])
        if k < E:
            result[span, :] = out
            ship(result.at[span], result_kept.at[span])
        else:
            others[pl.ds((k - E) * HALF, 2 * HALF), :] = out.astype(LOW)
    up_bias[...] = total
    down_bias[...] = total_down


def expert_grad_body(offsets, ship, scalars, *refs):
    given, refs = refs[:4], refs[4:]
    pieces, (up, down, *held) = refs[: len(offsets)], refs[len(offsets) :]
    loads = []
    for a, b in zip(given, held):
        step = a.shape[0] // 4
        spans = [pl.ds(k * step, step) for k in range(4)]
        loads += [ship(a.at[span], b.at[span]) for span in spans]
    slot_rows, active, rows, pulled = held
    ship.wait(loads[:8])
    for at in range(0, up.shape[1], STEP):
        span = slice(at, at + STEP)
        down[span, :] = dot_tn(active[:, span], slot_rows[...]).astype(LOW)
    ship.wait(loads[8:])
    for at in range(0, up.shape[1], STEP):
        span = slice(at, at + STEP)
        up[:, span] = dot_tn(rows[...], pulled[:, span]).astype(LOW)
    for ref, offs in zip(pieces, offsets):
        size, wide = ref.shape[1] // 2, ref.shape[2] // 2
        for r, off in enumerate(offs):
            i = scalars[0] ^ off
            ref[r, :size, :] = up[pl.ds(pl.multiple_of(i * size, min(size, 16)), size), :]
            at = pl.multiple_of(i * 2 * size, min(size, 16))
            ref[r, size:, :wide] = down[pl.ds(at, size), :]
            ref[r, size:, wide:] = down[pl.ds(at + size, size), :]


def attend_pull_body(images, size, offsets, ship, scalars, *refs):
    count = len(offsets)
    chunks, refs = refs[: 2 * E], refs[2 * E :]
    target, middle, grad, vectors, probs, projected = refs[:6]
    pieces = refs[6 : 6 + count]
    first, small, middle_kept, merged_kept, pulled_kept, *refs = refs[6 + count :]
    middle_grad, merged, pulled, project, merge = refs
    place_attend(scalars[0], size, pieces, offsets, project, merge)
    normed_grad = combined(scalars, target[...], None, chunks)
    unit, inverse = unit_of(middle[...])
    value = grad[...] + norm_pull(normed_grad, unit, inverse, vectors[1:2, : grad.shape[1]])
    middle_grad[...] = value
    ship(middle_grad, middle_kept)
    low = value.astype(LOW)
    merged[...] = low
    ship(merged, merged_kept)
    small[0:1, :] = column_sum(normed_grad * unit)
    small[1:2, :] = column_sum(normed_grad)
    small[2:3, :] = column_sum(low.astype(F32))
    attended_grad = dot_nt(low, merge[...].astype(LOW)).astype(LOW)
    rows = value.shape[0] // images
    wide = merge.shape[0]
    heads = wide // HD
    for i in range(images):
        span = slice(i * rows, (i + 1) * rows)
        for h in range(heads):
            spans = [slice(s * wide + h * HD, s * wide + (h + 1) * HD) for s in range(3)]
            query, keys, values = (projected[span, s] for s in spans)
            head_grad = attended_grad[span, h * HD : (h + 1) * HD]
            prob_low = probs[i * heads + h]
            prob = prob_low.astype(F32)
            prob_grad = dot_nt(head_grad, values)
            score_grad = prob * (prob_grad - jnp.sum(prob_grad * prob, axis=-1, keepdims=True))
            score_grad = score_grad.astype(LOW)
            pulled[span, spans[0]] = (dot(score_grad, keys) * SCALE).astype(LOW)
            pulled[span, spans[1]] = (dot_tn(score_grad, query) * SCALE).astype(LOW)
            pulled[span, spans[2]] = dot_tn(prob_low, head_grad).astype(LOW)
    ship(pulled, pulled_kept)
    first[...] = dot_nt(pulled[...], project[...]).astype(LOW)


def attend_grad_body(size, offsets, scalars, normed, attended, merged, pulled, *refs):
    *refs, project, merge = refs
    small_rows = refs.pop() if len(refs) > len(offsets) + 1 else None
    *given, bias_out = refs
    given, pieces = given[: -len(offsets)], given[-len(offsets) :]
    wide = merge.shape[0]
    project[...] = dot_tn(normed[...], pulled[...]).astype(LOW)
    merge[...] = dot_tn(attended[...], merged[...])
    bias = [column_sum(pulled[:, k * wide : (k + 1) * wide].astype(F32)) for k in (0, 2)]
    bias_out[...] = jnp.concatenate(bias, axis=1)
    if small_rows is not None:
        owners = small_rows.shape[1]
        depth = (len(given) + 1) // 5
        for l in range(depth):
            one, two, up, down = given[4 * l : 4 * l + 4]
            pair = bias if l == 0 else [
                given[4 * depth + l - 1][:, k * wide : (k + 1) * wide] for k in range(2)
            ]
            norms = [one[0:1, :], two[0:1, :], one[1:2, :], two[1:2, :], two[2:3, :]]
            share = norms[0].shape[1] // owners
            first = sum(
                owned(v, owners, wide, k * share) for k, v in enumerate(norms)
            ) + sum(
                owned(v, owners, wide, 5 * share + k * share // 2) for k, v in enumerate(pair)
            )
            small_rows[3 * l] = first
            small_rows[3 * l + 1] = owned(down[...], owners, wide, scalars[1] * share)
            small_rows[3 * l + 2] = owned(up[...], owners, wide, scalars[1] * 2 * share)
    for ref, offs in zip(pieces, offsets):
        part = size // 2
        for r, off in enumerate(offs):
            i = scalars[0] ^ off
            at = pl.ds(pl.multiple_of(i * size, min(size, 16)), size)
            for s in range(3):
                ref[r, s * size : (s + 1) * size, :] = project[at, s * wide : (s + 1) * wide]
            rows = merge[pl.ds(pl.multiple_of(i * part, min(part, 8)), part), :]
            sides = jnp.concatenate([rows[:, :wide], rows[:, wide:]], axis=0)
            ref[r, 3 * size : 4 * size, :] = sides.astype(LOW)
            if small_rows is not None:
                lines = [small_rows[k, pl.ds(i, 1), :] for k in range(small_rows.shape[0])]
                lines.append(jnp.zeros((16 - len(lines), wide), F32))
                ref[r, 4 * size :, :] = jnp.concatenate(lines, axis=0).astype(LOW)


def stream_pull(part, got, stream, middle_grad, vectors, small):
    first = part[...].astype(F32) + got[...].astype(F32)
    unit, inverse = unit_of(stream[...])
    small[0:1, :] = column_sum(first * unit)
    small[1:2, :] = column_sum(first)
    return middle_grad[...] + norm_pull(first, unit, inverse, vectors[0:1, : first.shape[1]])


def stream_pull_body(
    scalars, part, got, stream, middle_grad, vectors, target, gate, grad, small, *sends
):
    value = stream_pull(part, got, stream, middle_grad, vectors, small)
    grad[...] = value
    low = value.astype(LOW)
    for r, send in enumerate(sends):
        send[...] = dot(slot_marks(scalars, r, target[...], gate[...]), low).astype(LOW)


def last_pull_body(scalars, part, got, stream, middle_grad, vectors, out, small):
    value = stream_pull(part, got, stream, middle_grad, vectors, small)
    rows = value.shape[0] // out.shape[0]
    for i in range(out.shape[0]):
        out[i] = value[i * rows : i * rows + out.shape[1]]


def pack_body(count, ship, scalars, *refs):
    given, packs, held = refs[:8], refs[8 : 8 + count], refs[8 + count :]
    ship.wait([ship(a, b) for a, b in zip(given, held)])
    attend, merge, *smalls = held
    depth, _, size, wide = attend.shape
    for l, pack in enumerate(packs):
        for k in range(3):
            pack[0, k * size : (k + 1) * size, :] = attend[l, k]
        rows = merge[l].astype(F32)
        sides = jnp.concatenate([rows[:, :wide], rows[:, wide:]], axis=0)
        pack[0, 3 * size : 4 * size, :] = sides.astype(LOW)

    def row(*parts):
        total, at = jnp.zeros((1, wide), F32), 0
        for part in parts:
            lane = lax.broadcasted_iota(jnp.int32, (part.shape[1], wide), 1)
            home = lax.broadcasted_iota(jnp.int32, lane.shape, 0) + at
            total = total + dot(part, jnp.where(lane == home, 1.0, 0.0).astype(LOW))
            at += part.shape[1]
        return total

    gain, shift, merge_bias, attend_bias, up_bias, down_bias = smalls
    rows = []
    for l in range(depth):
        norms = [v[l, k : k + 1, :] for v in (gain, shift) for k in range(2)]
        rows.append(
            row(*norms, merge_bias[l : l + 1, :], *(attend_bias[l, k : k + 1, :] for k in range(2)))
        )
        rows.append(row(*(down_bias[l, e : e + 1, :] for e in range(E))))
        rows.append(row(*(up_bias[l, e : e + 1, :] for e in range(E))))
    rows.append(jnp.zeros((16 - 3 * depth, wide), F32))
    packs[0][0, 4 * size :, :] = jnp.concatenate(rows, axis=0).astype(LOW)


def deal_body(layer, ship, scalars, up, down, *chunks):
    size, wide = up.shape[2], down.shape[3]
    for r, chunk in enumerate(chunks):
        e = scalars[1] ^ r
        ship(up.at[layer, e], chunk.at[pl.ds(0, size), :])
        for side in range(2):
            ship(
                down.at[layer, e, pl.ds(side * size, size), :],
                chunk.at[pl.ds(size, size), pl.ds(side * wide, wide)],
            )


def prepare_body(images, scalars, routes, gates, columns, rows_out, gate_rows):
    depth, total, _ = routes.shape
    live = live_rows(scalars, total, images)
    square = lax.broadcasted_iota(jnp.int32, (total, total), 0), lax.broadcasted_iota(
        jnp.int32, (total, total), 1
    )
    earlier = jnp.where(square[0] > square[1], 1.0, 0.0).astype(LOW)
    same = jnp.where(square[0] == square[1], 1.0, 0.0).astype(LOW)
    lane = lax.broadcasted_iota(jnp.int32, (total, 128), 1)
    for l in range(depth):
        picks = [routes[l, :, k : k + 1] for k in range(2)]
        chosen = ((lane == picks[0]) | (lane == picks[1])) & live
        taken = dot(earlier, jnp.where(chosen, 1.0, 0.0).astype(LOW))
        mixed = jnp.zeros((total, 128), F32)
        for k, pick in enumerate(picks):
            slot = jnp.sum(jnp.where(lane == pick, taken, 0.0), axis=1, keepdims=True)
            target = jnp.where(live & (pick >= 0), pick * SLOTS + slot.astype(jnp.int32), -1)
            columns[l, :, k : k + 1] = target
            high = (target + 1) >> 5
            mixed = jnp.where(lane == 3 * k, high.astype(F32), mixed)
            mixed = jnp.where(lane == 3 * k + 1, (target + 1 - (high << 5)).astype(F32), mixed)
            mixed = jnp.where(lane == 3 * k + 2, gates[l, :, k : k + 1], mixed)
        turned = dot_tn(mixed.astype(LOW), same)
        for k in range(2):
            high, low, gate = (turned[3 * k + j : 3 * k + j + 1] for j in range(3))
            rows_out[l, k : k + 1, :] = (high * 32.0 + low).astype(jnp.int32) - 1
            gate_rows[l, k : k + 1, :] = gate


def finish_body(depth, scalars, *refs):
    blocks, attends, outs = refs[: E * depth], refs[E * depth : -10], refs[-10:]
    gain, shift, attend, attend_bias, merge, merge_bias, up, up_bias, down, down_bias = outs
    size, wide = up.shape[2], down.shape[3]
    part, share = size // 2, gain.shape[2]
    small = attends[0][0, 4 * size :, :].astype(F32)
    for l in range(depth):
        for r in range(E):
            e = scalars[1] ^ r
            value = blocks[l * E + r][...].astype(F32)
            up[l, e] = value[:size]
            both = value[size:]
            down[l, e] = jnp.concatenate([both[:, :wide], both[:, wide:]], axis=0)
        for k in range(3):
            attend[l, k] = attends[l][0, k * size : (k + 1) * size, :].astype(F32)
        sides = attends[l][0, 3 * size : 4 * size, :].astype(F32)
        merge[l] = jnp.concatenate([sides[:part], sides[part:]], axis=1)
        first, second, third = (small[3 * l + k : 3 * l + k + 1, :] for k in range(3))
        for k in range(2):
            gain[l, k : k + 1, :] = first[:, k * share : (k + 1) * share]
            shift[l, k : k + 1, :] = first[:, (2 + k) * share : (3 + k) * share]
            at = 5 * share + k * share // 2
            attend_bias[l, k : k + 1, :] = first[:, at : at + share // 2]
        merge_bias[l : l + 1, :] = first[:, 4 * share : 5 * share]
        for e in range(E):
            down_bias[l, e : e + 1, :] = second[:, e * share : (e + 1) * share]
            up_bias[l, e : e + 1, :] = third[:, 2 * e * share : 2 * (e + 1) * share]


class Place:
    def __init__(self, count, rows, live):
        self.count = count
        self.me = lax.axis_index("dp").astype(jnp.int32)
        core = lax.axis_index("tensor").astype(jnp.int32)
        self.expert = (self.me >> 2) & 3
        self.near = self.expert ^ jnp.arange(E, dtype=jnp.int32)
        powers = [1 << k for k in range(count.bit_length() - 1)]
        self.powers, self.beyond = powers, [b for b in reversed(powers) if b > 8]
        self.aligned = rows % 16 == 0
        where = self.me if self.aligned else jnp.zeros((), jnp.int32)
        self.scalars = jnp.stack([where, self.expert, core, live, self.me])
        far = doubled([0], self.beyond)
        self.parts = [[f ^ l ^ p for f in far for l in LINE] for p in PLANE]
        self.all = [o for offs in self.parts for o in offs]
        blocks = [f ^ l for f in far for l in LINE]
        middle = len(blocks) // 2
        rounds = [(0, blocks), (1, blocks), (2, blocks), (3, blocks[:middle]), (3, blocks[middle:])]
        self.arrivals = [[b ^ p for b in some] for p, some in rounds]
        self.all_arrivals = [o for offs in self.arrivals for o in offs]
        self.fetched = self.arrivals if self.aligned else [[0]]
        self.offsets = self.parts if self.aligned else [[0]]

    def spread(self, value, offsets):
        return [value] + [swap(value, o, self.count) for o in offsets[1:]]

    def near_of(self, value):
        return [swap(value, p, self.count) for p in (1, 2)]

    def gather(self, value, near, anchor=()):
        half = value.shape[0] // 2
        one, two = after(near, anchor)
        return [value, *near, swap(two[:half], 1, self.count), swap(one[half:], 2, self.count)]

    def reduce_onward(self, pieces):
        own, one, two, far = pieces
        half = far.shape[0] // 2
        onward = swap(far[:half], 1, self.count), swap(far[half:], 2, self.count)
        two = jnp.concatenate([add_low(two[:half], onward[0]), two[half:]], axis=0)
        one = jnp.concatenate([one[:half], add_low(one[half:], onward[1])], axis=0)
        return own, one, two

    def reduce(self, own, one, two):
        return add_low(own, swap(one, 1, self.count), swap(two, 2, self.count))

    def deal(self, chunks):
        return [chunks[0]] + [swap(chunks[r], LINE[r], self.count) for r in range(1, E)]

    def exchange(self, chunks, hold=()):
        return self.crossed(self.deal(chunks), hold)

    def crossed(self, own, hold=()):
        return own + [cross(c) for c in (after(own, hold) if hold else own)]

    def doubled(self, value):
        for bit in self.beyond:
            value = jnp.concatenate([value, swap(value, bit, self.count)], axis=0)
        return value

    def halved(self, value):
        for bit in reversed(self.beyond):
            half = value.shape[0] // 2
            value = add_low(value[:half], swap(value[half:], bit, self.count))
        return value


def pack_small(gain, shift, merge, attend, up, down):
    depth, _, share = gain.shape
    spare = jnp.zeros((depth, 2 * share), LOW)
    first = [gain, shift, merge, attend, spare]
    first = jnp.concatenate([p.reshape(depth, -1) for p in first], axis=1)
    second = jnp.pad(down.reshape(depth, -1), ((0, 0), (0, 4 * share)))
    rows = jnp.stack([first, second, up.reshape(depth, -1)], axis=1).reshape(3 * depth, -1)
    return jnp.pad(rows, ((0, -(3 * depth) % 16), (0, 0)))[None]


def pack_attend(attend, merge):
    count, kinds, depth, wide = attend.shape
    rows = attend.reshape(count, 3 * depth, wide)
    return jnp.concatenate([rows, merge[:, :, :wide], merge[:, :, wide:]], axis=1)


def unpack_attend(pack):
    count, rows, wide = pack.shape
    depth = rows // 4
    attend = pack[:, : 3 * depth].reshape(count, 3, depth, wide)
    sides = pack[:, 3 * depth :]
    return attend, jnp.concatenate([sides[:, : depth // 2], sides[:, depth // 2 :]], axis=2)


def whole_attend(pack):
    attend, merge = unpack_attend(pack)
    attend = jnp.swapaxes(attend, 0, 1)
    attend = attend.reshape(3, -1, attend.shape[-1])
    return pack_attend(attend[None], merge.reshape(1, -1, merge.shape[-1]))


def split_attend(pack, count):
    attend, merge = unpack_attend(pack)
    attend = jnp.swapaxes(attend.reshape(3, count, -1, attend.shape[-1]), 0, 1)
    return pack_attend(attend, merge.reshape(count, -1, merge.shape[-1]))


def fetch_column(place, value):
    blocks = place.spread(place.doubled(value), LINE)
    value = jnp.stack(blocks, axis=1)
    return value.reshape((-1,) + value.shape[2:])


def attend_pieces_of(place, pieces):
    if place.aligned:
        return pieces
    return [whole_attend(ordered(jnp.concatenate(pieces), place.all_arrivals, place.me))]


def chunks_of(place, layer, up_weight, down_weight):
    depth, hidden = up_weight.shape[2:]
    if place.aligned:
        return call(
            functools.partial(deal_body, layer),
            [((2 * depth, hidden), LOW)] * E,
            place.scalars,
            up_weight,
            down_weight,
            stored=(0, 1),
        )
    sent = []
    for r in range(E):
        one = lax.dynamic_index_in_dim(up_weight[layer], place.near[r], 0, False)
        two = lax.dynamic_index_in_dim(down_weight[layer], place.near[r], 0, False)
        two = jnp.concatenate([two[:depth], two[depth:]], axis=1)
        sent.append(jnp.concatenate([one, two], axis=0))
    return sent


def fetch_base(place, chunks):
    return place.doubled(jnp.stack(place.deal(chunks)))


def expert_pieces_of(place, pieces):
    if place.aligned:
        return pieces
    pack = ordered(jnp.concatenate(pieces), place.all_arrivals, place.me)
    depth, wide = pack.shape[1] // 2, pack.shape[2] // 2
    up, down = pack[:, :depth], pack[:, depth:]
    down = jnp.concatenate([down[..., :wide], down[..., wide:]], axis=1).reshape(2, -1, wide)
    down = jnp.concatenate([down[0], down[1]], axis=1)
    return [jnp.concatenate([up.reshape(-1, up.shape[-1]), down])[None]]


def add_low(*terms):
    return sum(t.astype(F32) for t in terms).astype(LOW)


def spread_expert(place, pieces):
    if place.aligned:
        return pieces
    pack = pieces[0][0]
    depth, wide = pack.shape[0] // 2, pack.shape[1] // 2
    up = pack[:depth].reshape(place.count, -1, 2 * wide)
    down = jnp.concatenate([pack[depth:, :wide], pack[depth:, wide:]], axis=0)
    down = down.reshape(place.count, 2, -1, wide)
    down = jnp.concatenate([down[:, 0], down[:, 1]], axis=-1)
    value = relative(jnp.concatenate([up, down], axis=1), place.all, place.me)
    return list(value.reshape((len(PLANE), -1) + value.shape[1:]))


def finish_expert(place, blocks):
    pack = jnp.take(jnp.stack(blocks), place.near, axis=0, mode="clip").astype(F32)
    depth, wide = pack.shape[1] // 2, pack.shape[2] // 2
    low = pack[:, depth:]
    return pack[:, :depth], jnp.concatenate([low[..., :wide], low[..., wide:]], axis=1)


def spread_plane(place, full):
    value = relative(split_attend(full, place.count), place.all, place.me)
    return list(value.reshape((len(PLANE), -1) + value.shape[1:]))


def fold_column(place, value):
    value = place.halved(value)
    got = [swap(value[r : r + 1], LINE[r], place.count) for r in range(1, len(LINE))]
    return add_low(value[:1], *got)


def finish_attend(value):
    attend, merge = unpack_attend(value)
    return attend[0].astype(F32), merge[0].astype(F32)


def on_device(
    count,
    inputs,
    image_count,
    routes,
    gates,
    norm_gain,
    norm_shift,
    attend_weight,
    attend_bias,
    merge_weight,
    merge_bias,
    up_weight,
    up_bias,
    down_weight,
    down_bias,
    cotangent,
):
    images, length, width = inputs.shape
    depth = routes.shape[0]
    wide = attend_weight.shape[-1]
    hidden = up_weight.shape[-1]
    heads = wide // HD
    place = Place(count, up_weight.shape[2], image_count[0])
    scalars = place.scalars
    rows = -(-length // 16) * 16
    total = images * rows
    half = E * HALF
    size = width // count if place.aligned else width

    def padded(value, fill=0):
        spare = [(0, 0)] * value.ndim
        spare[-2] = (0, rows - length)
        value = jnp.pad(value, spare, constant_values=fill)
        return value.reshape(value.shape[:-3] + (total, value.shape[-1]))

    chunk = ((HALF, width), LOW)
    wide_rows = ((total, width), F32)
    low_rows = ((total, width), LOW)
    wide_half, low_slots = ((half, width), F32), ((2 * half, width), LOW)
    low_half = ((half, width), LOW)
    low_hidden = ((2 * half, hidden), LOW)
    low_project = ((total, 3 * wide), LOW)
    attend_scratch = [((width, 3 * wide), LOW), ((wide, width), F32)]
    expert_scratch = [((width, hidden), LOW), ((hidden, width), LOW)]

    smalls = (norm_gain, norm_shift, merge_bias, attend_bias, up_bias, down_bias)
    small = []
    if place.aligned:
        given = (attend_weight, merge_weight, *smalls)
        sizes = [4 * size + (16 if l == 0 else 0) for l in range(depth)]
        packs = call(
            functools.partial(pack_body, depth),
            [((1, n, wide), LOW) for n in sizes],
            scalars,
            *given,
            scratch=[(g.shape, LOW) for g in given],
            stored=range(len(given)),
        )
    else:
        packs = [pack_attend(attend_weight[l][None], merge_weight[l][None]) for l in range(depth)]
        small = place.spread(fetch_column(place, pack_small(*smalls)), PLANE)
        small = [ordered(jnp.concatenate(small), place.all, place.me)]
    column = fetch_column(place, packs[0])
    chunks = chunks_of(place, 0, up_weight, down_weight)
    base = fetch_base(place, after(chunks, column))
    near = place.near_of(column)
    attend_pieces = attend_pieces_of(place, place.gather(column, near))
    target, target_rows, gate_rows = call(
        functools.partial(prepare_body, images),
        [((depth, total, 2), jnp.int32)]
        + [((depth, 2, total), jnp.int32), ((depth, 2, total), F32)],
        scalars,
        *after((padded(routes, -1), padded(gates)), column),
    )
    gate = padded(gates)
    stream = padded(after(inputs, column))
    states = []
    back, first_sends = None, ()
    for l in range(depth):
        more = l + 1 < depth
        base = after(base, attend_pieces)
        near = place.near_of(base)
        kinds = [low_rows, low_project, ((images * heads, rows, rows), LOW), ((total, wide), LOW)]
        body = functools.partial(
            attend_body, length, images, size, place.fetched, l > 0, not place.aligned
        )
        if l == 0:
            table = [((count, 16, wide), LOW)] if place.aligned else []
            part, vectors, *keeps = call(
                body,
                [low_rows, ((depth, 8, hidden), F32)],
                scalars,
                stream,
                *small,
                *attend_pieces,
                saved=kinds,
                scratch=kinds + attend_scratch + table,
                before=(base,),
                us=LONG,
            )
            stream_kept = stream
        else:
            stream, part, stream_kept, *keeps = call(
                body,
                [wide_rows, low_rows],
                scalars,
                middle,
                *back,
                target[l - 1],
                gate[l - 1],
                vectors[l],
                *attend_pieces,
                saved=[wide_rows] + kinds,
                scratch=kinds + attend_scratch,
                before=first_sends,
                us=LONG,
            )
        normed, projected, probs, attended = keeps
        if more:
            chunks = chunks_of(place, l + 1, up_weight, down_weight)
            next_base = fetch_base(place, after(chunks, base))
        middle, *sends, middle_kept = call(
            middle_body,
            [wide_rows] + [chunk] * E,
            scalars,
            stream,
            part,
            cross(part),
            vectors[l],
            target_rows[l],
            saved=[wide_rows],
            before=(next_base,) if more else (),
        )
        own = place.deal(sends)
        expert_pieces = expert_pieces_of(place, place.gather(base, near, own[2]))
        taken = place.crossed(own)
        kept = attend_pieces
        if more:
            base = next_base
            column = fetch_column(place, after(packs[l + 1], own))
        others, result, active, slope, taken_rows = call(
            functools.partial(expert_body, place.fetched, not more),
            [low_half] if more else [],
            scalars,
            *taken,
            vectors[l],
            *expert_pieces,
            saved=([] if more else [low_half]) + [wide_half, low_hidden, low_hidden, low_slots],
            scratch=[wide_half, low_hidden, low_hidden, low_slots]
            + expert_scratch
            + ([] if more else [low_half]),
            us=LONG,
        )
        states.append(
            (stream_kept, middle_kept, normed, projected, probs, attended, taken_rows, active, slope)
            + (kept, expert_pieces)
        )
        if more:
            near = place.near_of(after(column, others))
            sends = call(
                total_body,
                [chunk] * E,
                scalars,
                result,
                cross(others),
                vectors[l],
                before=(column,),
            )
            attend_pieces = attend_pieces_of(place, place.gather(column, near, sends))
            back = place.exchange(sends)
            if l + 2 == depth:
                grad, *first_sends = call(
                    functools.partial(first_grad_body, images),
                    [wide_rows] + [chunk] * E,
                    scalars,
                    padded(after(cotangent, sends)),
                    target_rows[-1],
                    gate_rows[-1],
                )

    last, last_others = result, others
    slot_grad = place.crossed(place.deal(after(first_sends, own)), (result,))
    blocks = [None] * depth
    attend_sums, smalls, biases = [None] * depth, [None] * depth, [None] * depth
    waiting, before_expert, before_total, before_grad = [], (), (), ()
    for l in reversed(range(depth)):
        stream, middle, normed, projected, probs, attended, taken, active, slope = states[l][:9]
        attend_pieces, expert_pieces = states[l][9:]
        others, up_b, down_b, result, pulled, slot_rows = call(
            functools.partial(expert_pull_body, place.fetched),
            [low_half, ((1, hidden), F32), ((1, width), F32)],
            scalars,
            *slot_grad,
            slope,
            *expert_pieces,
            saved=[wide_half, low_hidden, low_slots],
            scratch=[wide_half, low_hidden, low_slots, low_hidden] + expert_scratch,
            stored=(2 * E,),
            us=LONG,
        )
        sends = call(
            total_body,
            [chunk] * E,
            scalars,
            result,
            cross(others),
        )
        own = place.deal(sends)
        before_attend = ()
        if waiting:
            attend_sum = place.reduce(*after(before_total, sends))
            before_attend = (attend_sum,)
            waiting.append(attend_sum)
        active, pulled_late = after((active, pulled), own[1])
        pieces = call(
            functools.partial(expert_grad_body, place.offsets),
            [((len(o), 2 * size, hidden), LOW) for o in place.offsets],
            scalars,
            slot_rows,
            active,
            taken,
            pulled_late,
            scratch=expert_scratch + [low_slots, low_hidden, low_slots, low_hidden],
            stored=range(4),
            us=7,
        )
        back = place.crossed(own, pieces)
        expert_onward = place.reduce_onward(spread_expert(place, pieces))
        if waiting:
            done, value, total_sum = waiting
            blocks[done] = place.deal(list(place.halved(after(value, back))))
            before_grad = blocks[done]
            waiting = [done, total_sum]
        pull_kinds = [wide_rows, low_rows, low_project]
        first, small_two, middle_grad, merged, pulled = call(
            functools.partial(attend_pull_body, images, size, place.fetched),
            [low_rows, ((3, width), F32)],
            scalars,
            *back,
            target[l],
            middle,
            grad,
            vectors[l],
            probs,
            projected,
            *attend_pieces,
            saved=pull_kinds,
            scratch=pull_kinds + attend_scratch,
            before=before_attend,
            us=LONG,
        )
        got = cross(first)
        if l > 0:
            grad, small_one, *sends = call(
                stream_pull_body,
                [wide_rows, ((2, width), F32)] + [chunk] * E,
                scalars,
                first,
                got,
                stream,
                middle_grad,
                vectors[l],
                target_rows[l - 1],
                gate_rows[l - 1],
                before=expert_onward,
            )
            own = place.deal(sends)
            slot_grad = place.crossed(own)
            pulled_late = after(pulled, own[3])
        else:
            input_grad, small_one = call(
                last_pull_body,
                [(inputs.shape, F32), ((2, width), F32)],
                scalars,
                first,
                got,
                stream,
                middle_grad,
                vectors[l],
                before=expert_onward,
            )
            pulled_late = pulled
        smalls[l] = (small_one, small_two, up_b, down_b)
        extra = []
        joint = place.aligned and l == 0
        if joint:
            extra = [v for some in smalls for v in some] + biases[1:]
        height = 4 * size + (16 if joint else 0)
        *pieces, biases[l] = call(
            functools.partial(attend_grad_body, size, place.offsets),
            [((len(o), height, wide), LOW) for o in place.offsets] + [((1, width), F32)],
            scalars,
            normed,
            attended,
            merged,
            pulled_late,
            *extra,
            scratch=([((3 * depth, count, wide), F32)] if joint else []) + attend_scratch,
            before=before_grad,
            us=4 if l else LONG,
        )
        if not place.aligned:
            pieces = spread_plane(place, pieces[0])
        if l == 0:
            ends = after((last, last_others), before_grad)
            ends = call(
                total_body, [chunk] * E, scalars, ends[0], cross(ends[1]), vectors[-1]
            )
            ends = place.deal(ends)
            pieces = after(pieces, ends)
            waiting[-1] = fold_column(place, after(waiting[-1], ends))
        before_total = place.reduce_onward(pieces)
        expert_sum = place.reduce(*expert_onward)
        before_expert = (expert_sum,)
        if waiting:
            done, total_sum = waiting
            attend_sums[done] = total_sum
        waiting = [l, expert_sum]
    expert_sum = after(expert_sum, attend_sums[1:])
    blocks[0] = place.deal(list(place.halved(expert_sum)))
    attend_sums[0] = fold_column(place, place.reduce(*after(before_total, expert_sum)))
    ends = after(ends, pieces)
    (output,) = call(
        output_body,
        [(inputs.shape, F32)],
        scalars,
        states[-1][1],
        *ends,
        *map(cross, ends),
        target[-1],
        gate[-1],
    )
    if place.aligned:
        grads = (norm_gain, norm_shift, attend_weight, attend_bias, merge_weight, merge_bias)
        grads += (up_weight, up_bias, down_weight, down_bias)
        return output, input_grad, *call(
            functools.partial(finish_body, depth),
            [(g.shape, F32) for g in grads],
            scalars,
            *[b for layer in blocks for b in layer],
            *attend_sums,
        )

    tables = []
    at_expert = jnp.arange(E, dtype=jnp.int32)[:, None, None] == place.expert
    for (small_one, small_two, up_b, down_b), bias in zip(smalls, biases):
        expert_rows = jnp.concatenate([up_b.reshape(-1, width), down_b], axis=0)
        expert_rows = jnp.where(at_expert, expert_rows[None], 0.0).reshape(-1, width)
        tables.append(jnp.concatenate([small_one, small_two, bias, expert_rows], axis=0))
    small = jnp.stack(tables)
    for bit in place.beyond:
        small = small + swap(small, bit, count)
    for offsets in (PLANE, LINE):
        terms = place.spread(small, offsets)
        small = (terms[0] + terms[1]) + (terms[2] + terms[3])

    def mine(value, size):
        return lax.dynamic_slice_in_dim(value, place.me * size, size, value.ndim - 1)

    share = norm_gain.shape[-1]
    gain_grad = jnp.stack([small[:, 0], small[:, 2]], axis=1)
    shift_grad = jnp.stack([small[:, 1], small[:, 3]], axis=1)
    attend_b = small[:, 5].reshape(depth, 2, wide)
    expert_rows = small[:, 6:].reshape(depth, E, -1, width)
    up_b = expert_rows[:, :, :-1].reshape(depth, E, hidden)
    finished = [finish_expert(place, b) + finish_attend(a) for b, a in zip(blocks, attend_sums)]
    up_grad, down_grad, attend_grad, merge_grad = (
        jnp.stack([f[k] for f in finished]) for k in range(4)
    )
    return (
        output,
        input_grad,
        mine(gain_grad, share),
        mine(shift_grad, share),
        attend_grad,
        mine(attend_b, attend_bias.shape[-1]),
        merge_grad,
        mine(small[:, 4], share),
        up_grad,
        mine(up_b, up_bias.shape[-1]),
        down_grad,
        mine(expert_rows[:, :, -1], share),
    )


def solution(mesh):
    placed = (
        P("dp", None, None),
        P("dp"),
        P(None, "dp", None, None),
        P(None, "dp", None, None),
        P(None, None, "dp"),
        P(None, None, "dp"),
        P(None, None, "dp", "tensor"),
        P(None, None, ("tensor", "dp")),
        P(None, ("tensor", "dp"), None),
        P(None, "dp"),
        P(None, None, "dp", "tensor"),
        P(None, None, ("tensor", "dp")),
        P(None, None, ("tensor", "dp"), None),
        P(None, None, "dp"),
        P("dp", None, None),
    )
    return jax.shard_map(
        functools.partial(on_device, mesh.shape["dp"]),
        mesh=mesh,
        in_specs=placed,
        out_specs=(
            P("dp", None, None),
            P("dp", None, None),
            P(None, None, "dp"),
            P(None, None, "dp"),
            P(None, None, "dp", "tensor"),
            P(None, None, ("tensor", "dp")),
            P(None, ("tensor", "dp"), None),
            P(None, "dp"),
            P(None, None, "dp", "tensor"),
            P(None, None, ("tensor", "dp")),
            P(None, None, ("tensor", "dp"), None),
            P(None, None, "dp"),
        ),
        check_vma=False,
    )
```
